256 devices in a mesh: tiles: 64 (over x, z, core), diag: 4 (over y).
Axes of the slice: x: 4, y: 4, z: 8, core: 2. Of those that a mesh axis runs over, the one named last changes fastest.
Arguments:
- inputs: bfloat16 [48, 8192, 512], P(None, 'tiles', 'diag'), may hold values from -6 to 6
- cotangent: bfloat16 [48, 8192, 512], P(None, 'tiles', 'diag'), may hold values from -6 to 6
- conv_weight: bfloat16 [9, 48, 48], replicated, may hold values from -0.3125 to 0.3125
- mix_weight: bfloat16 [48, 48], replicated, may hold values from -0.875 to 0.875
- counts: int32 [64], P('tiles'), may hold values from 1 to 4, 128 in all
- band_reach: int32 [256], P('tiles'), may hold values from 256 to 512
- dilation: int32 [2], replicated, may hold values from 1 to 8, as said below
Outputs:
- grad_inputs: bfloat16 [48, 8192, 512], P(None, 'tiles', 'diag')
- grad_conv: float32 [9, 48, 48], replicated
- grad_mix: float32 [48, 48], replicated
The draws below stay inside these ranges and needn't reach their ends.
Inputs may be any that keep to these rules, and one draw needn't show every extreme that they name: `counts`: the live tiles of the tiles indices, taken in order, are the consecutive tiles of the band; some index holds 4. `band_reach`: offsets at or beyond a slot's reach are empty cells; entries of empty slots are ignored. `dilation`: one of the two dilations equals 8, the other is smaller.
All inputs are finite; a program needn't handle non-finite values. No bound on the sum of `counts` on one device may be relied on, other than what follows from the above.
Results may differ from the reference program's by a relative error of at most 0.009.
Values may be sent and summed in bfloat16 or wider, within the bound.
A program may use at most 192 MiB of HBM per device.

```python
import math
import jax
import jax.numpy as jnp
import numpy as np
from jax import lax

C = 48
TR = 32
DMAX = 8
CAPT = 4
TOTAL = 128
SLOTS = 256
BAND = 512
N_TILES = 64


def draw_dilation(key, part):
    key = jax.random.fold_in(key, 7)
    first, second = jax.random.split(key)
    other = jax.random.randint(first, (), 1, DMAX)
    side = jax.random.randint(second, (), 0, 2)
    return jnp.where(jnp.arange(2) == side, DMAX, other).astype(jnp.int32)


def with_ends(entries, key, smallest, largest):
    longest = entries.shape.index(max(entries.shape))
    spots = []
    for shift in (0, 1):
        where = [jax.random.randint(jax.random.fold_in(key, axis), (), 0, length) for axis, length in enumerate(entries.shape)]
        where[longest] = (where[longest] + shift) % entries.shape[longest]
        spots.append(tuple(where))
    return entries.at[spots[0]].set(smallest).at[spots[1]].set(largest)


def block_levels(stream_key, shape, shards, smallest, top_value):
    level, own = 1.0, jax.random.fold_in(stream_key, 6)
    for dim, blocks in shards:
        heights = jnp.exp(jax.random.uniform(jax.random.fold_in(own, dim), (blocks,), jnp.float32, smallest / len(shards), top_value / len(shards)))
        level = level * jnp.repeat(heights, shape[dim] // blocks).reshape([-1 if axis == dim else 1 for axis in range(len(shape))])
    return level


def profile(amount, total, most, lean):
    weights = [(1 << 20) // math.isqrt(rank ** lean) + 1 for rank in range(2, amount + 1)]
    surplus, given = total - most - (amount - 1), [1] * (amount - 1)
    while surplus > 0:
        candidates = [i for i in range(amount - 1) if given[i] < most]
        whole, left = sum([weights[i] for i in candidates]), surplus
        for i in candidates:
            more = min(most - given[i], max(1, left * weights[i] // whole), surplus)
            given[i] = given[i] + more
            surplus = surplus - more
    return np.array([most] + given)


def uneven_parts(own_key, count, total, limit, lean):
    if count == 2:
        one = jax.random.randint(own_key, (), max(1, total - limit), min(limit, total - 1) + 1)
        return jnp.stack([one, total - one])
    sizes = jnp.asarray(profile(count, total, limit, lean), jnp.int32)
    twos = (count - 1) // 2
    source_of, sink = sizes[1:1 + 2 * twos:2], sizes[2:2 + 2 * twos:2]
    slack = jnp.minimum(source_of - 1, limit - sink)
    moved = jax.random.randint(jax.random.fold_in(own_key, 1), (twos,), 0, 1 << 20) % (slack + 1)
    sizes = sizes.at[1:1 + 2 * twos:2].set(source_of - moved).at[2:2 + 2 * twos:2].set(sink + moved)
    return sizes[jax.random.permutation(jax.random.fold_in(own_key, 2), count)]


def scatter_about(key, shape, scale, reach, shards=(), kind=jnp.bfloat16):
    array = jax.random.normal(key, shape, jnp.float32) * scale
    if len(shards) > 0:
        array = block_levels(key, shape, shards, -0.22, 0.18) * array
    return jnp.clip(array, min=-reach, max=reach).astype(kind)


def setup_inputs(seed: int = 0) -> dict:
    key_of = jax.random.split(jax.random.key(seed), 8)
    return {
        "inputs": scatter_about(key_of[0], (C, SLOTS * TR, BAND), 1.0, 6.0, ((1, 64), (2, 4))),
        "cotangent": scatter_about(key_of[1], (C, SLOTS * TR, BAND), 1.0, 6.0, ((1, 64), (2, 4))),
        "conv_weight": scatter_about(key_of[2], (9, C, C), (9 * C) ** -0.5, 0.3125),
        "mix_weight": scatter_about(key_of[3], (C, C), C ** -0.5, 0.875),
        "counts": uneven_parts(key_of[4], N_TILES, TOTAL, CAPT, 1).astype(jnp.int32),
        "band_reach": with_ends(jax.random.randint(key_of[5], (SLOTS,), BAND // 2, BAND + 1), jax.random.fold_in(key_of[5], 1), BAND // 2, BAND).astype(jnp.int32),
        "dilation": draw_dilation(jax.random.fold_in(key_of[7], 71), 0),
    }


def tile_slots(counts):
    ends = jnp.cumsum(counts.astype(jnp.int32)).astype(jnp.int32)
    order = jnp.arange(TOTAL, dtype=jnp.int32)
    owner = lax.optimization_barrier(jnp.sum((ends[None, :] <= order[:, None]).astype(jnp.int32), axis=1)).astype(jnp.int32)
    begin = (ends - counts.astype(jnp.int32)).astype(jnp.int32)
    local = order - begin[owner]
    return (owner * CAPT + local).astype(jnp.int32)

def stencil_offsets(dilation):
    result = []
    for row_step in range(3):
        for col_step in range(3):
            row_move = ((row_step - 1) * dilation[0]).astype(jnp.int32)
            col_move = ((col_step - 1) * dilation[1]).astype(jnp.int32)
            result.append((row_move, (col_move - row_move).astype(jnp.int32)))
    return result

def reference(inputs, cotangent, conv_weight, mix_weight, counts, band_reach, dilation):
    slots = tile_slots(counts)
    live_x = jnp.take(inputs.reshape(C, SLOTS, TR, BAND), slots, axis=1)
    live_g = jnp.take(cotangent.reshape(C, SLOTS, TR, BAND), slots, axis=1)
    reach_live = jnp.take(band_reach, slots).astype(jnp.int32)
    offsets_all = jnp.arange(BAND, dtype=jnp.int32)
    keep = offsets_all[None, :] < reach_live[:, None]
    rectified = jnp.where(keep[None, :, None, :], jnp.maximum(live_x, 0), 0).astype(jnp.bfloat16)
    rectified = rectified.reshape(C, TOTAL * TR, BAND)
    padded = jnp.pad(rectified, ((0, 0), (DMAX, DMAX), (2 * DMAX, 2 * DMAX)))
    shifts = stencil_offsets(dilation)
    conv32 = conv_weight.astype(jnp.float32)
    mix32 = mix_weight.astype(jnp.float32)
    zero = jnp.int32(0)

    def forward_tile(index):
        window = lax.dynamic_slice(padded, (zero, index * TR, zero), (C, TR + 2 * DMAX, BAND + 4 * DMAX))
        pieces = []
        pre_act = jnp.zeros((C, TR, BAND), jnp.float32)
        for stencil in range(9):
            row_move, band_move = shifts[stencil]
            piece = lax.dynamic_slice(window, (zero, DMAX + row_move, 2 * DMAX + band_move), (C, TR, BAND))
            piece = piece.astype(jnp.float32)
            pieces.append(piece)
            pre_act = pre_act + jnp.einsum('oi,irc->orc', conv32[stencil], piece)
        mask = keep[index][None, None, :]
        tile_g = lax.dynamic_index_in_dim(live_g, index, 1, keepdims=False)
        masked = jnp.where(mask, tile_g, 0).astype(jnp.float32)
        hidden = lax.optimization_barrier(jnp.maximum(pre_act, 0).astype(jnp.bfloat16)).astype(jnp.float32)
        mix_part = jnp.einsum('orc,irc->oi', masked, hidden)
        back = jnp.einsum('oi,orc->irc', mix32, masked)
        grad_pre = jnp.where(pre_act > 0, back, 0).astype(jnp.bfloat16)
        grad32 = lax.optimization_barrier(grad_pre).astype(jnp.float32)
        conv_part = jnp.stack([jnp.einsum('orc,irc->oi', grad32, piece) for piece in pieces])
        return (grad_pre, conv_part, mix_part)
    grad_tiles, conv_parts, mix_parts = lax.map(forward_tile, jnp.arange(TOTAL, dtype=jnp.int32))
    grad_field = jnp.moveaxis(grad_tiles, 0, 1).reshape(C, TOTAL * TR, BAND)
    grad_padded = jnp.pad(grad_field, ((0, 0), (DMAX, DMAX), (2 * DMAX, 2 * DMAX)))

    def backward_tile(index):
        window = lax.dynamic_slice(grad_padded, (zero, index * TR, zero), (C, TR + 2 * DMAX, BAND + 4 * DMAX))
        spread = jnp.zeros((C, TR, BAND), jnp.float32)
        for stencil in range(9):
            row_move, band_move = shifts[stencil]
            piece = lax.dynamic_slice(window, (zero, DMAX - row_move, 2 * DMAX - band_move), (C, TR, BAND))
            spread = spread + jnp.einsum('oi,orc->irc', conv32[stencil], piece.astype(jnp.float32))
        tile_x = lax.dynamic_index_in_dim(live_x, index, 1, keepdims=False)
        tile_g = lax.dynamic_index_in_dim(live_g, index, 1, keepdims=False)
        active = keep[index][None, None, :] & (tile_x > 0)
        return (tile_g.astype(jnp.float32) + jnp.where(active, spread, 0.0)).astype(jnp.bfloat16)
    grad_live = lax.map(backward_tile, jnp.arange(TOTAL, dtype=jnp.int32))
    placed = jnp.zeros((C, SLOTS, TR, BAND), jnp.bfloat16).at[:, slots].set(jnp.moveaxis(grad_live, 0, 1))
    scale = 1.0 / jnp.sqrt(jnp.float32(TOTAL * TR * BAND))
    grad_conv = lax.optimization_barrier(jnp.sum(conv_parts, axis=0)) * scale
    grad_mix = lax.optimization_barrier(jnp.sum(mix_parts, axis=0)) * scale
    return (placed.reshape(C, SLOTS * TR, BAND), grad_conv, grad_mix)
```

```python
import functools
import math

import jax
import jax.numpy as jnp
from jax import lax
from jax.experimental import pallas as pl
from jax.experimental.pallas import tpu as pltpu
from jax.sharding import PartitionSpec as P

MESH = pl.DeviceIdType.MESH
TPD = 2
DMAX = 8
CH = 48
ROWS = 128
COLS = 128
EDGE = 2 * DMAX
GROUPS = COLS // EDGE
STEP = 8
TAPS = 9
SHARES = 16
KPAD = 512
VMEM_LIMIT = 56 * 1024 * 1024
BF = jnp.bfloat16
F32 = jnp.float32
LIVE, REACH, DIL, TILE, DIAG, LAST_TILE, LAST_DIAG = 0, 1, 5, 7, 8, 9, 10


def iota(shape, dim):
    return lax.broadcasted_iota(jnp.int32, shape, dim)


def reach_of(par, ids):
    reach = jnp.where(ids < 64, jnp.where(ids < 32, par[REACH], par[REACH + 1]),
                      jnp.where(ids < 96, par[REACH + 2], par[REACH + 3]))
    return jnp.where(ids < par[LIVE], reach, 0)


def tap_moves(par):
    moves = []
    for a in range(3):
        for b in range(3):
            row = (a - 1) * par[DIL]
            moves.append((a, (b - 1) * par[DIL + 1] - row))
    return moves


def pack_edges(par, field, first, last, pick):
    lane = iota((1, 2 * ROWS), 1)
    near = lane % DMAX
    want = jnp.where(lane < ROWS, near, par[LIVE] - DMAX + near)
    place = (lane % ROWS) // DMAX
    rows = iota((ROWS, 2 * ROWS), 0)
    for kk in range(EDGE):
        hit = (rows == want) & (place == kk)
        pick[kk * ROWS:(kk + 1) * ROWS, :] = jnp.where(hit, 1.0, 0.0).astype(BF)

    def group(g, carry):
        lhs = jnp.concatenate([field[g * EDGE + kk] for kk in range(EDGE)], axis=1)
        out = jnp.dot(lhs, pick[...], preferred_element_type=F32).astype(BF)
        first[g] = out[:, :ROWS]
        last[g] = out[:, ROWS:]
        return carry

    lax.fori_loop(0, GROUPS, group, 0)


def shift_rows(par, field, left, right, top, bot, moved):
    lane = iota((1, 2 * ROWS), 1)
    move = jnp.where(lane < ROWS, -par[DIL], par[DIL])
    want = (lane % ROWS) + move
    rows = iota((ROWS, 2 * ROWS), 0)
    inner = jnp.where(rows == want, 1.0, 0.0).astype(BF)
    has_top = par[TILE] > 0
    has_bot = par[TILE] < par[LAST_TILE]
    top_want = jnp.where((want < 0) & has_top, want + DMAX, -1)
    low = want - par[LIVE]
    bot_want = jnp.where((low >= 0) & (low < DMAX) & has_bot, low, -1)
    has_left = par[DIAG] > 0
    has_right = par[DIAG] < par[LAST_DIAG]
    tops = top[...].reshape((GROUPS + 2) * CH, ROWS)
    bots = bot[...].reshape((GROUPS + 2) * CH, ROWS)

    def column(kk, carry):
        part = rows - kk * DMAX
        inside = (part >= 0) & (part < DMAX)
        part = jnp.where(inside, part, -2)
        upper = jnp.where(part == top_want, 1.0, 0.0).astype(BF)
        lower = jnp.where(part == bot_want, 1.0, 0.0).astype(BF)
        weight = jnp.concatenate([inner, upper, lower], axis=0)
        tiles = [left[kk]] + [field[g * EDGE + kk] for g in range(GROUPS)] + [right[kk]]
        lhs = jnp.concatenate([jnp.concatenate(tiles, axis=0), tops, bots], axis=1)
        out = jnp.dot(lhs, weight, preferred_element_type=F32)
        for g in range(GROUPS + 2):
            piece = out[g * CH:(g + 1) * CH]
            same = tiles[g]
            if g == 0:
                piece = jnp.where(has_left, piece, 0.0)
                same = jnp.where(has_left, same, jnp.zeros_like(same))
            if g == GROUPS + 1:
                piece = jnp.where(has_right, piece, 0.0)
                same = jnp.where(has_right, same, jnp.zeros_like(same))
            piece = piece.astype(BF)
            moved[0, g * EDGE + kk] = piece[:, :ROWS]
            moved[1, g * EDGE + kk] = same
            moved[2, g * EDGE + kk] = piece[:, ROWS:]
        return carry

    lax.fori_loop(0, EDGE, column, 0)


def prep_kernel(par, x_ref, g_ref, field, masked, first, last, x_t, g_t, pick):
    shape = (ROWS, COLS)
    keep = iota(shape, 1) + par[DIAG] * COLS < reach_of(par, iota(shape, 0))

    def channel(c, carry):
        x = jnp.where(keep, jnp.maximum(x_ref[c].astype(F32), 0.0), 0.0)
        g = jnp.where(keep, g_ref[c].astype(F32), 0.0)
        x_t[pl.ds(c, COLS, stride=CH), :] = x.T
        g_t[pl.ds(c, COLS, stride=CH), :] = g.T
        return carry

    lax.fori_loop(0, CH, channel, 0, unroll=2)

    def column(k, carry):
        at = pl.ds(pl.multiple_of(k * CH, CH), CH)
        field[k] = x_t[at, :].astype(BF)
        masked[k] = g_t[at, :].astype(BF)
        return carry

    lax.fori_loop(0, COLS, column, 0, unroll=4)
    pack_edges(par, field, first, last, pick)


def forward_kernel(par, field, left, right, top, bot, masked, weight,
                   grad_pre, first, last, total, moved, stack, acc, pick):
    shift_rows(par, field, left, right, top, bot, moved)
    moves = tap_moves(par)
    acc[...] = jnp.zeros_like(acc)
    used = (TAPS + 1) * CH
    stack[used:, :] = jnp.zeros((KPAD - used, STEP * ROWS), BF)

    def block(blk, carry):
        for j in range(STEP):
            k = blk * STEP + j
            lanes = slice(j * ROWS, (j + 1) * ROWS)
            for s, (a, shift) in enumerate(moves):
                stack[s * CH:(s + 1) * CH, lanes] = moved[a, EDGE + k + shift]
            stack[TAPS * CH:used, lanes] = masked[k]
        out = jnp.dot(weight[...], stack[...], preferred_element_type=F32)
        pre, back = out[:CH], out[CH:]
        grad = jnp.where(pre > 0, back, 0.0).astype(BF)
        lhs = jnp.concatenate([grad, stack[TAPS * CH:used, :]], axis=0)
        stack[TAPS * CH:used, :] = jnp.maximum(pre, 0.0).astype(BF)
        for j in range(STEP):
            grad_pre[blk * STEP + j] = grad[:, j * ROWS:(j + 1) * ROWS]
        acc[...] += lax.dot_general(lhs, stack[...], (((1,), (1,)), ((), ())),
                                    preferred_element_type=F32)
        return carry

    lax.fori_loop(0, COLS // STEP, block, 0)
    both = jnp.where(iota((CH, KPAD), 1) < TAPS * CH, acc[:CH], acc[CH:])
    for n in range(SHARES):
        if n < 2 * (CH // 8):
            at = (n // 2) * 8
            total[n] = both[at:at + 8, (n % 2) * 2 * ROWS:(n % 2 + 1) * 2 * ROWS]
        else:
            total[n] = jnp.zeros((8, 2 * ROWS), F32)
    pack_edges(par, grad_pre, first, last, pick)


def backward_kernel(par, field, left, right, top, bot, x_ref, g_ref, weight, out_ref,
                    moved, stack, spread):
    shift_rows(par, field, left, right, top, bot, moved)
    moves = tap_moves(par)
    used = TAPS * CH
    stack[used:, :] = jnp.zeros((KPAD - used, STEP * ROWS), BF)

    def block(blk, carry):
        for j in range(STEP):
            k = blk * STEP + j
            lanes = slice(j * ROWS, (j + 1) * ROWS)
            for s, (a, shift) in enumerate(moves):
                stack[s * CH:(s + 1) * CH, lanes] = moved[2 - a, EDGE + k - shift]
        out = jnp.dot(weight[...], stack[...], preferred_element_type=F32)
        for j in range(STEP):
            at = pl.ds(pl.multiple_of((blk * STEP + j) * CH, CH), CH)
            spread[at, :] = out[:, j * ROWS:(j + 1) * ROWS]
        return carry

    lax.fori_loop(0, COLS // STEP, block, 0)
    shape = (ROWS, COLS)
    ids = iota(shape, 0)
    keep = iota(shape, 1) + par[DIAG] * COLS < reach_of(par, ids)
    live = ids < par[LIVE]

    def channel(c, carry):
        part = spread[pl.ds(c, COLS, stride=CH), :].T
        x = x_ref[c].astype(F32)
        full = g_ref[c].astype(F32) + jnp.where(keep & (x > 0), part, 0.0)
        out_ref[c] = jnp.where(live, full, 0.0).astype(BF)
        return carry

    lax.fori_loop(0, CH, channel, 0, unroll=2)


def exchange_kernel(field, first, last, left, right, top, bot, send, recv):
    tile, diag = lax.axis_index("tiles"), lax.axis_index("diag")
    tiles, diags = lax.axis_size("tiles"), lax.axis_size("diag")
    up, down = lax.rem(tile + tiles - 1, tiles), lax.rem(tile + 1, tiles)
    lo, hi = lax.rem(diag + diags - 1, diags), lax.rem(diag + 1, diags)
    barrier = pltpu.get_barrier_semaphore()
    near = [(tile, lo), (tile, hi), (up, diag), (down, diag), (up, lo), (up, hi), (down, lo), (down, hi)]
    for device in near:
        pl.semaphore_signal(barrier, inc=1, device_id=device, device_id_type=MESH)
    pl.semaphore_wait(barrier, len(near))
    inner = pl.ds(1, GROUPS)
    plan = [
        (field.at[pl.ds(0, EDGE)], right, near[0]),
        (field.at[pl.ds(COLS - EDGE, EDGE)], left, near[1]),
        (first, bot.at[inner], near[2]),
        (last, top.at[inner], near[3]),
        (first.at[0], bot.at[GROUPS + 1], near[4]),
        (first.at[GROUPS - 1], bot.at[0], near[5]),
        (last.at[0], top.at[GROUPS + 1], near[6]),
        (last.at[GROUPS - 1], top.at[0], near[7]),
    ]
    copies = []
    for n, (src, dst, device) in enumerate(plan):
        copy = pltpu.make_async_remote_copy(src_ref=src, dst_ref=dst, send_sem=send.at[n], recv_sem=recv.at[n],
                                            device_id=device, device_id_type=MESH)
        copy.start()
        copies.append(copy)
    for copy in copies:
        copy.wait()


def sum_kernel(scale, part, conv_ref, mix_ref, near, far, done, send, recv, far_send, far_recv, out_send, out_recv):
    tile, diag = lax.axis_index("tiles"), lax.axis_index("diag")
    outer, other = lax.div(tile, SHARES), lax.rem(tile, SHARES)
    rank = outer * 4 + diag

    def friend(step):
        to = lax.rem(rank + step, SHARES)
        return to, (lax.div(to, 4) * SHARES + other, lax.rem(to, 4))

    def cousin(step):
        return (outer * SHARES + lax.rem(other + step, SHARES), diag)

    barrier = pltpu.get_barrier_semaphore()
    for step in range(1, SHARES):
        pl.semaphore_signal(barrier, inc=1, device_id=friend(step)[1], device_id_type=MESH)
        pl.semaphore_signal(barrier, inc=1, device_id=cousin(step), device_id_type=MESH)
    pl.semaphore_wait(barrier, 2 * (SHARES - 1))

    def first_copy(step):
        to, device = friend(step)
        return pltpu.make_async_remote_copy(
            src_ref=part.at[to], dst_ref=near.at[rank], send_sem=send.at[step], recv_sem=recv.at[step],
            device_id=device, device_id_type=MESH)

    def far_copy(step):
        return pltpu.make_async_remote_copy(
            src_ref=far.at[other], dst_ref=far.at[other], send_sem=far_send.at[step], recv_sem=far_recv.at[step],
            device_id=cousin(step), device_id_type=MESH)

    def out_copy(step):
        return pltpu.make_async_remote_copy(
            src_ref=done.at[rank], dst_ref=done.at[rank], send_sem=out_send.at[step], recv_sem=out_recv.at[step],
            device_id=friend(step)[1], device_id_type=MESH)

    steps = range(1, SHARES)
    for step in steps:
        first_copy(step).start()
    near[rank] = part[rank]
    for step in steps:
        first_copy(step).wait_recv()
    far[other] = jnp.sum(near[...], axis=0)
    for step in steps:
        far_copy(step).start()
    for step in steps:
        far_copy(step).wait_recv()
    done[rank] = jnp.sum(far[...], axis=0)
    for step in steps:
        out_copy(step).start()
    for step in steps:
        out_copy(step).wait_recv()
    for g in range(CH // 8):
        row = jnp.concatenate([done[2 * g], done[2 * g + 1]], axis=1) * scale
        for s in range(TAPS):
            conv_ref[s, 8 * g:8 * g + 8, :] = row[:, s * CH:(s + 1) * CH]
        mix_ref[8 * g:8 * g + 8, :] = row[:, TAPS * CH:(TAPS + 1) * CH]
    for step in steps:
        first_copy(step).wait_send()
        far_copy(step).wait_send()
        out_copy(step).wait_send()


def vmem_spec(count):
    return [pl.BlockSpec(memory_space=pltpu.VMEM)] * count


def local_call(kernel, outs, scratch, operands, flops):
    size = sum(math.prod(o.shape) * o.dtype.itemsize for o in operands + outs)
    return pl.pallas_call(
        kernel,
        out_shape=outs,
        in_specs=[pl.BlockSpec(memory_space=pltpu.SMEM)] + vmem_spec(len(operands) - 1),
        out_specs=vmem_spec(len(outs)),
        scratch_shapes=scratch,
        cost_estimate=pl.CostEstimate(flops=flops, bytes_accessed=size, transcendentals=0),
        compiler_params=pltpu.CompilerParams(vmem_limit_bytes=VMEM_LIMIT),
    )(*operands)


def exchange(field, first, last, number):
    shape = jax.ShapeDtypeStruct
    return pl.pallas_call(
        exchange_kernel,
        out_shape=[shape((EDGE, CH, ROWS), BF)] * 2 + [shape((GROUPS + 2, CH, ROWS), BF)] * 2,
        in_specs=[pl.BlockSpec(memory_space=pl.ANY)] * 3,
        out_specs=[pl.BlockSpec(memory_space=pl.ANY)] * 4,
        scratch_shapes=[pltpu.SemaphoreType.DMA((8,)), pltpu.SemaphoreType.DMA((8,))],
        compiler_params=pltpu.CompilerParams(collective_id=number, has_side_effects=True),
    )(field, first, last)


def sum_over_devices(part, scale):
    shape = jax.ShapeDtypeStruct
    slots = pltpu.VMEM((SHARES, 8, 2 * ROWS), F32)
    return pl.pallas_call(
        functools.partial(sum_kernel, scale),
        out_shape=[shape((TAPS, CH, CH), F32), shape((CH, CH), F32)],
        in_specs=vmem_spec(1),
        out_specs=vmem_spec(2),
        scratch_shapes=[slots] * 3 + [pltpu.SemaphoreType.DMA((SHARES,))] * 6,
        compiler_params=pltpu.CompilerParams(collective_id=2, has_side_effects=True),
    )(part)


def body(inputs, cotangent, conv_weight, mix_weight, counts, band_reach, dilation):
    shape = jax.ShapeDtypeStruct
    tiles, diags = lax.axis_size("tiles"), lax.axis_size("diag")
    place = [lax.axis_index("tiles"), lax.axis_index("diag"), tiles - 1, diags - 1]
    par = jnp.concatenate([counts * (ROWS // 4), band_reach, dilation, jnp.stack([jnp.int32(p) for p in place])])
    taps = conv_weight.transpose(1, 0, 2).reshape(CH, TAPS * CH)
    zeros = jnp.zeros((CH, CH), BF)
    forward_weight = jnp.concatenate([
        jnp.concatenate([taps, zeros], axis=1),
        jnp.concatenate([jnp.zeros_like(taps), mix_weight.T], axis=1)], axis=0)
    forward_weight = jnp.pad(forward_weight, ((0, 0), (0, KPAD - (TAPS + 1) * CH)))
    back_weight = jnp.pad(conv_weight.transpose(2, 0, 1).reshape(CH, TAPS * CH), ((0, 0), (0, KPAD - TAPS * CH)))

    field_shape = shape((COLS, CH, ROWS), BF)
    pack_shape = shape((GROUPS, CH, ROWS), BF)
    turned = pltpu.VMEM((COLS * CH, ROWS), F32)
    pick = pltpu.VMEM((EDGE * ROWS, 2 * ROWS), BF)
    moved = pltpu.VMEM((3, COLS + 2 * EDGE, CH, ROWS), BF)
    stack = pltpu.VMEM((KPAD, STEP * ROWS), BF)
    conv_flops = 2 * CH * CH * TAPS * ROWS * COLS

    field, masked, first, last = local_call(
        prep_kernel, [field_shape, field_shape, pack_shape, pack_shape], [turned, turned, pick],
        [par, inputs, cotangent], 0)
    left, right, top, bot = exchange(field, first, last, 0)
    grad_pre, first, last, part = local_call(
        forward_kernel, [field_shape, pack_shape, pack_shape, shape((SHARES, 8, 2 * ROWS), F32)],
        [moved, stack, pltpu.VMEM((2 * CH, KPAD), F32), pick],
        [par, field, left, right, top, bot, masked, forward_weight], 2 * conv_flops)
    left, right, top, bot = exchange(grad_pre, first, last, 1)
    cells = TPD * tiles * (ROWS // 4) * COLS * diags
    grad_conv, grad_mix = sum_over_devices(part, 1.0 / math.sqrt(cells))
    (grad_inputs,) = local_call(
        backward_kernel, [shape((CH, ROWS, COLS), BF)], [moved, stack, turned],
        [par, grad_pre, left, right, top, bot, inputs, cotangent, back_weight], conv_flops)
    return (grad_inputs, grad_conv, grad_mix)


def solution(mesh):
    in_specs = (
        P(None, "tiles", "diag"),
        P(None, "tiles", "diag"),
        P(),
        P(),
        P("tiles"),
        P("tiles"),
        P(),
    )
    out_specs = (P(None, "tiles", "diag"), P(), P())
    return jax.shard_map(body, mesh=mesh, in_specs=in_specs, out_specs=out_specs, check_vma=False)
```

```python
import functools
import math

import jax
import jax.numpy as jnp
from jax import lax
from jax.experimental import pallas as pl
from jax.experimental.pallas import tpu as pltpu
from jax.sharding import PartitionSpec as P

MESH = pl.DeviceIdType.MESH
TPD = 2
DMAX = 8
CH = 48
ROWS = 128
COLS = 128
EDGE = 2 * DMAX
GROUPS = COLS // EDGE
STEP = 8
TAPS = 9
SHARES = 16
KPAD = 512
VMEM_LIMIT = 56 * 1024 * 1024
BF = jnp.bfloat16
F32 = jnp.float32
LIVE, REACH, DIL, TILE, DIAG, LAST_TILE, LAST_DIAG = 0, 1, 5, 7, 8, 9, 10


def iota(shape, dim):
    return lax.broadcasted_iota(jnp.int32, shape, dim)


def reach_of(par, ids):
    reach = jnp.where(ids < 64, jnp.where(ids < 32, par[REACH], par[REACH + 1]),
                      jnp.where(ids < 96, par[REACH + 2], par[REACH + 3]))
    return jnp.where(ids < par[LIVE], reach, 0)


def tap_moves(par):
    moves = []
    for a in range(3):
        for b in range(3):
            row = (a - 1) * par[DIL]
            moves.append((a, (b - 1) * par[DIL + 1] - row))
    return moves


def pack_edges(par, field, first, last):
    lane = iota((1, 2 * ROWS), 1)
    near = lane % DMAX
    want = jnp.where(lane < ROWS, near, par[LIVE] - DMAX + near)
    place = jnp.where(lane < ROWS, (lane // DMAX + EDGE // 2) % EDGE, (lane - ROWS) // DMAX)
    hit = jnp.where(iota((ROWS, 2 * ROWS), 0) == want, 1.0, 0.0)
    out = jnp.zeros((GROUPS * CH, 2 * ROWS), F32)
    for kk in range(0, EDGE, 2):
        weight = jnp.concatenate([jnp.where(place == kk + n, hit, 0.0).astype(BF) for n in range(2)], axis=0)
        lhs = jnp.concatenate(
            [jnp.concatenate([field[g * EDGE + kk + n] for g in range(GROUPS)], axis=0) for n in range(2)], axis=1)
        out += jnp.dot(lhs, weight, preferred_element_type=F32)
    out = out.astype(BF)
    for g in range(GROUPS):
        first[g] = out[g * CH:(g + 1) * CH, :ROWS]
        last[g] = out[g * CH:(g + 1) * CH, ROWS:]


def shift_rows(par, field, left, right, top, bot, moved):
    half = ROWS // 2
    lane = iota((1, 2 * ROWS), 1)
    move = jnp.where(lane < ROWS, -par[DIL], par[DIL])
    want = (lane % ROWS) + move
    rows = iota((ROWS, 2 * ROWS), 0)
    inner = jnp.where(rows == want, 1.0, 0.0).astype(BF)
    has_top = par[TILE] > 0
    has_bot = par[TILE] < par[LAST_TILE]
    top_want = jnp.where((want < 0) & has_top, want + DMAX, -1)
    low = want - par[LIVE]
    bot_want = jnp.where((low >= 0) & (low < DMAX) & has_bot, low, -1)
    wants = [jnp.where(rows < half, top_want, bot_want), jnp.where(rows < half, bot_want, top_want)]
    outers = [jnp.where(rows % DMAX == w, 1.0, 0.0) for w in wants]
    place = (rows % half) // DMAX
    has_left = par[DIAG] > 0
    has_right = par[DIAG] < par[LAST_DIAG]
    tops = top[...].reshape((GROUPS + 2) * CH, ROWS)
    bots = bot[...].reshape((GROUPS + 2) * CH, ROWS)
    upper = iota(tops.shape, 1) < half
    halos = [jnp.where(upper, tops, bots), jnp.where(upper, bots, tops)]

    for part in range(2):
        def column(at, carry):
            kk = at + part * (EDGE // 2)
            weight = jnp.concatenate([inner, jnp.where(place == at, outers[part], 0.0).astype(BF)], axis=0)
            tiles = [left[kk]] + [field[g * EDGE + kk] for g in range(GROUPS)] + [right[kk]]
            tiles[0] = jnp.where(has_left, tiles[0], jnp.zeros_like(tiles[0]))
            tiles[-1] = jnp.where(has_right, tiles[-1], jnp.zeros_like(tiles[-1]))
            lhs = jnp.concatenate([jnp.concatenate(tiles, axis=0), halos[part]], axis=1)
            out = jnp.dot(lhs, weight, preferred_element_type=F32)
            for g in range(GROUPS + 2):
                piece = out[g * CH:(g + 1) * CH]
                if g == 0:
                    piece = jnp.where(has_left, piece, 0.0)
                if g == GROUPS + 1:
                    piece = jnp.where(has_right, piece, 0.0)
                piece = piece.astype(BF)
                moved[0, g * EDGE + kk] = piece[:, :ROWS]
                moved[1, g * EDGE + kk] = tiles[g]
                moved[2, g * EDGE + kk] = piece[:, ROWS:]
            return carry

        lax.fori_loop(0, EDGE // 2, column, 0)


def pair(refs):
    return jnp.concatenate(refs, axis=1)


def eye():
    return jnp.where(iota((ROWS, ROWS), 0) == iota((ROWS, ROWS), 1), 1.0, 0.0).astype(BF)


def turn(one, value):
    return lax.dot_general(one, value, (((1,), (1,)), ((), ())), preferred_element_type=F32)


def turn_field(value, held, field):
    one = eye()

    def channels(step, carry):
        c = step * 4
        out = turn(one, jnp.concatenate([value(c + n) for n in range(4)], axis=0))
        for n in range(4):
            held[pl.ds(c + n, COLS, stride=CH), :] = out[:, n * ROWS:(n + 1) * ROWS]
        return carry

    lax.fori_loop(0, CH // 4, channels, 0, unroll=2)

    def column(k, carry):
        field[k] = held[pl.ds(pl.multiple_of(k * CH, CH), CH), :].astype(BF)
        return carry

    lax.fori_loop(0, COLS, column, 0, unroll=8)


def kept_cells(par):
    shape = (ROWS, COLS)
    return iota(shape, 1) + par[DIAG] * COLS < reach_of(par, iota(shape, 0))


def prep_kernel(par, x_ref, g_ref, field, masked, first, last, held):
    keep = jnp.where(kept_cells(par), 1.0, 0.0).astype(BF)
    turn_field(lambda c: jnp.maximum(x_ref[c], jnp.zeros((), BF)) * keep, held, field)
    pack_edges(par, field, first, last)
    turn_field(lambda c: g_ref[c] * keep, held, masked)


def conv_forward(par, moved, masked, weight, grad_pre, hidden):
    moves = tap_moves(par)
    used = (TAPS + 1) * CH
    pad = jnp.zeros((KPAD - used, 2 * ROWS), BF)

    def block(blk, carry):
        for j in range(0, STEP, 2):
            k = blk * STEP + j
            tiles = [pair([moved[a, EDGE + k + n + shift] for n in range(2)]) for a, shift in moves]
            tiles += [pair([masked[k], masked[k + 1]]), pad]
            out = jnp.dot(weight[...], jnp.concatenate(tiles, axis=0), preferred_element_type=F32)
            pre, back = out[:CH], out[CH:]
            grad = jnp.where(pre > 0, back, 0.0).astype(BF)
            act = jnp.maximum(pre, 0.0).astype(BF)
            for n in range(2):
                grad_pre[k + n] = grad[:, n * ROWS:(n + 1) * ROWS]
                hidden[k + n] = act[:, n * ROWS:(n + 1) * ROWS]
        return carry

    lax.fori_loop(0, COLS // STEP, block, 0)


def kernel_grads(par, moved, masked, grad_pre, hidden, acc):
    moves = tap_moves(par)
    acc[...] = jnp.zeros_like(acc)

    def block(blk, carry):
        ks = [blk * STEP + j for j in range(STEP)]
        tiles = [pair([moved[a, EDGE + k + shift] for k in ks]) for a, shift in moves]
        lhs = jnp.concatenate(tiles + [pair([hidden[k] for k in ks])], axis=0)
        rhs = jnp.concatenate([pair([grad_pre[k] for k in ks]), pair([masked[k] for k in ks])], axis=0)
        acc[:, :2 * CH] += lax.dot_general(lhs, rhs, (((1,), (1,)), ((), ())), preferred_element_type=F32)
        return carry

    lax.fori_loop(0, COLS // STEP, block, 0)


def share_out(acc, total):
    flat = acc[...].T
    both = jnp.where(iota((CH, (TAPS + 1) * CH), 1) < TAPS * CH, flat[:CH], flat[CH:2 * CH])
    both = jnp.concatenate([both, jnp.zeros((CH, KPAD - (TAPS + 1) * CH), F32)], axis=1)
    for n in range(SHARES):
        if n < 2 * (CH // 8):
            at = (n // 2) * 8
            total[n] = both[at:at + 8, (n % 2) * 2 * ROWS:(n % 2 + 1) * 2 * ROWS]
        else:
            total[n] = jnp.zeros((8, 2 * ROWS), F32)


def forward_kernel(par, field, left, right, top, bot, masked, weight,
                   grad_pre, first, last, total, moved, hidden, acc):
    shift_rows(par, field, left, right, top, bot, moved)
    conv_forward(par, moved, masked, weight, grad_pre, hidden)
    pack_edges(par, grad_pre, first, last)
    kernel_grads(par, moved, masked, grad_pre, hidden, acc)
    share_out(acc, total)


def conv_back(par, moved, weight, spread):
    moves = tap_moves(par)
    pad = jnp.zeros((KPAD - TAPS * CH, 2 * ROWS), BF)

    def block(blk, carry):
        for j in range(0, STEP, 2):
            k = blk * STEP + j
            tiles = [pair([moved[2 - a, EDGE + k + n - shift] for n in range(2)]) for a, shift in moves]
            out = jnp.dot(weight[...], jnp.concatenate(tiles + [pad], axis=0), preferred_element_type=F32)
            for n in range(2):
                at = pl.ds(pl.multiple_of((k + n) * CH, CH), CH)
                spread[at, :] = out[:, n * ROWS:(n + 1) * ROWS]
        return carry

    lax.fori_loop(0, COLS // STEP, block, 0)


def finish(par, x_ref, g_ref, spread, out_ref):
    keep = kept_cells(par)
    live = iota((ROWS, COLS), 0) < par[LIVE]
    one = eye()

    def channels(step, carry):
        c = step * 4
        parts = [spread[pl.ds(c + n, COLS, stride=CH), :].astype(BF) for n in range(4)]
        out = turn(one, jnp.concatenate(parts, axis=0))
        for n in range(4):
            part = out[:, n * ROWS:(n + 1) * ROWS]
            x = x_ref[c + n].astype(F32)
            full = g_ref[c + n].astype(F32) + jnp.where(keep & (x > 0), part, 0.0)
            out_ref[c + n] = jnp.where(live, full, 0.0).astype(BF)
        return carry

    lax.fori_loop(0, CH // 4, channels, 0, unroll=2)


def backward_kernel(par, field, left, right, top, bot, x_ref, g_ref, weight, out_ref, moved, spread):
    shift_rows(par, field, left, right, top, bot, moved)
    conv_back(par, moved, weight, spread)
    finish(par, x_ref, g_ref, spread, out_ref)


def exchange_kernel(field, first, last, left, right, top, bot, send, recv):
    tile, diag = lax.axis_index("tiles"), lax.axis_index("diag")
    tiles, diags = lax.axis_size("tiles"), lax.axis_size("diag")
    up, down = lax.rem(tile + tiles - 1, tiles), lax.rem(tile + 1, tiles)
    lo, hi = lax.rem(diag + diags - 1, diags), lax.rem(diag + 1, diags)
    barrier = pltpu.get_barrier_semaphore()
    near = [(tile, lo), (tile, hi), (up, diag), (down, diag), (up, lo), (up, hi), (down, lo), (down, hi)]
    for device in near:
        pl.semaphore_signal(barrier, inc=1, device_id=device, device_id_type=MESH)
    pl.semaphore_wait(barrier, len(near))
    inner = pl.ds(1, GROUPS)
    plan = [
        (field.at[pl.ds(0, EDGE)], right, near[0]),
        (field.at[pl.ds(COLS - EDGE, EDGE)], left, near[1]),
        (first, bot.at[inner], near[2]),
        (last, top.at[inner], near[3]),
        (first.at[0], bot.at[GROUPS + 1], near[4]),
        (first.at[GROUPS - 1], bot.at[0], near[5]),
        (last.at[0], top.at[GROUPS + 1], near[6]),
        (last.at[GROUPS - 1], top.at[0], near[7]),
    ]
    copies = []
    for n, (src, dst, device) in enumerate(plan):
        copy = pltpu.make_async_remote_copy(src_ref=src, dst_ref=dst, send_sem=send.at[n], recv_sem=recv.at[n],
                                            device_id=device, device_id_type=MESH)
        copy.start()
        copies.append(copy)
    for copy in copies:
        copy.wait()


def sum_kernel(scale, part, conv_ref, mix_ref, near, far, done, send, recv, far_send, far_recv, out_send, out_recv):
    tile, diag = lax.axis_index("tiles"), lax.axis_index("diag")
    outer, other = lax.div(tile, SHARES), lax.rem(tile, SHARES)
    rank = outer * 4 + diag

    def friend(step):
        to = lax.rem(rank + step, SHARES)
        return to, (lax.div(to, 4) * SHARES + other, lax.rem(to, 4))

    def cousin(step):
        return (outer * SHARES + lax.rem(other + step, SHARES), diag)

    barrier = pltpu.get_barrier_semaphore()
    for step in range(1, SHARES):
        pl.semaphore_signal(barrier, inc=1, device_id=friend(step)[1], device_id_type=MESH)
        pl.semaphore_signal(barrier, inc=1, device_id=cousin(step), device_id_type=MESH)
    pl.semaphore_wait(barrier, 2 * (SHARES - 1))

    def first_copy(step):
        to, device = friend(step)
        return pltpu.make_async_remote_copy(
            src_ref=part.at[to], dst_ref=near.at[rank], send_sem=send.at[step], recv_sem=recv.at[step],
            device_id=device, device_id_type=MESH)

    def far_copy(step):
        return pltpu.make_async_remote_copy(
            src_ref=far.at[other], dst_ref=far.at[other], send_sem=far_send.at[step], recv_sem=far_recv.at[step],
            device_id=cousin(step), device_id_type=MESH)

    def out_copy(step):
        return pltpu.make_async_remote_copy(
            src_ref=done.at[rank], dst_ref=done.at[rank], send_sem=out_send.at[step], recv_sem=out_recv.at[step],
            device_id=friend(step)[1], device_id_type=MESH)

    steps = range(1, SHARES)
    for step in steps:
        first_copy(step).start()
    near[rank] = part[rank]
    for step in steps:
        first_copy(step).wait_recv()
    far[other] = jnp.sum(near[...], axis=0)
    for step in steps:
        far_copy(step).start()
    for step in steps:
        far_copy(step).wait_recv()
    done[rank] = jnp.sum(far[...], axis=0)
    for step in steps:
        out_copy(step).start()
    for step in steps:
        out_copy(step).wait_recv()
    for g in range(CH // 8):
        row = jnp.concatenate([done[2 * g], done[2 * g + 1]], axis=1) * scale
        for s in range(TAPS):
            conv_ref[s, 8 * g:8 * g + 8, :] = row[:, s * CH:(s + 1) * CH]
        mix_ref[8 * g:8 * g + 8, :] = row[:, TAPS * CH:(TAPS + 1) * CH]
    for step in steps:
        first_copy(step).wait_send()
        far_copy(step).wait_send()
        out_copy(step).wait_send()


def vmem_spec(count):
    return [pl.BlockSpec(memory_space=pltpu.VMEM)] * count


def local_call(kernel, outs, scratch, operands, flops):
    size = sum(math.prod(o.shape) * o.dtype.itemsize for o in operands + outs)
    return pl.pallas_call(
        kernel,
        out_shape=outs,
        in_specs=[pl.BlockSpec(memory_space=pltpu.SMEM)] + vmem_spec(len(operands) - 1),
        out_specs=vmem_spec(len(outs)),
        scratch_shapes=scratch,
        cost_estimate=pl.CostEstimate(flops=flops, bytes_accessed=size, transcendentals=0),
        compiler_params=pltpu.CompilerParams(vmem_limit_bytes=VMEM_LIMIT),
    )(*operands)


def exchange(field, first, last, number):
    shape = jax.ShapeDtypeStruct
    return pl.pallas_call(
        exchange_kernel,
        out_shape=[shape((EDGE, CH, ROWS), BF)] * 2 + [shape((GROUPS + 2, CH, ROWS), BF)] * 2,
        in_specs=[pl.BlockSpec(memory_space=pl.ANY)] * 3,
        out_specs=[pl.BlockSpec(memory_space=pl.ANY)] * 4,
        scratch_shapes=[pltpu.SemaphoreType.DMA((8,)), pltpu.SemaphoreType.DMA((8,))],
        compiler_params=pltpu.CompilerParams(collective_id=number, has_side_effects=True),
    )(field, first, last)


def sum_over_devices(part, scale):
    shape = jax.ShapeDtypeStruct
    slots = pltpu.VMEM((SHARES, 8, 2 * ROWS), F32)
    return pl.pallas_call(
        functools.partial(sum_kernel, scale),
        out_shape=[shape((TAPS, CH, CH), F32), shape((CH, CH), F32)],
        in_specs=vmem_spec(1),
        out_specs=vmem_spec(2),
        scratch_shapes=[slots] * 3 + [pltpu.SemaphoreType.DMA((SHARES,))] * 6,
        compiler_params=pltpu.CompilerParams(collective_id=2, has_side_effects=True),
    )(part)


def body(inputs, cotangent, conv_weight, mix_weight, counts, band_reach, dilation):
    shape = jax.ShapeDtypeStruct
    tiles, diags = lax.axis_size("tiles"), lax.axis_size("diag")
    place = [lax.axis_index("tiles"), lax.axis_index("diag"), tiles - 1, diags - 1]
    par = jnp.concatenate([counts * (ROWS // 4), band_reach, dilation, jnp.stack([jnp.int32(p) for p in place])])
    taps = conv_weight.transpose(1, 0, 2).reshape(CH, TAPS * CH)
    zeros = jnp.zeros((CH, CH), BF)
    forward_weight = jnp.concatenate([
        jnp.concatenate([taps, zeros], axis=1),
        jnp.concatenate([jnp.zeros_like(taps), mix_weight.T], axis=1)], axis=0)
    forward_weight = jnp.pad(forward_weight, ((0, 0), (0, KPAD - (TAPS + 1) * CH)))
    back_weight = jnp.pad(conv_weight.transpose(2, 0, 1).reshape(CH, TAPS * CH), ((0, 0), (0, KPAD - TAPS * CH)))

    field_shape = shape((COLS, CH, ROWS), BF)
    pack_shape = shape((GROUPS, CH, ROWS), BF)
    turned = pltpu.VMEM((COLS * CH, ROWS), F32)
    hidden = pltpu.VMEM((COLS, CH, ROWS), BF)
    moved = pltpu.VMEM((3, COLS + 2 * EDGE, CH, ROWS), BF)
    conv_flops = 2 * CH * CH * TAPS * ROWS * COLS

    field, masked, first, last = local_call(
        prep_kernel, [field_shape, field_shape, pack_shape, pack_shape], [turned],
        [par, inputs, cotangent], 0)
    left, right, top, bot = exchange(field, first, last, 0)
    grad_pre, first, last, part = local_call(
        forward_kernel, [field_shape, pack_shape, pack_shape, shape((SHARES, 8, 2 * ROWS), F32)],
        [moved, hidden, pltpu.VMEM(((TAPS + 1) * CH, ROWS), F32)],
        [par, field, left, right, top, bot, masked, forward_weight], 2 * conv_flops)
    left, right, top, bot = exchange(grad_pre, first, last, 1)
    cells = TPD * tiles * (ROWS // 4) * COLS * diags
    grad_conv, grad_mix = sum_over_devices(part, 1.0 / math.sqrt(cells))
    (grad_inputs,) = local_call(
        backward_kernel, [shape((CH, ROWS, COLS), BF)], [moved, turned],
        [par, grad_pre, left, right, top, bot, inputs, cotangent, back_weight], conv_flops)
    return (grad_inputs, grad_conv, grad_mix)


def solution(mesh):
    in_specs = (
        P(None, "tiles", "diag"),
        P(None, "tiles", "diag"),
        P(),
        P(),
        P("tiles"),
        P("tiles"),
        P(),
    )
    out_specs = (P(None, "tiles", "diag"), P(), P())
    return jax.shard_map(body, mesh=mesh, in_specs=in_specs, out_specs=out_specs, check_vma=False)
```

```python
import functools
import math

import jax
import jax.numpy as jnp
from jax import lax
from jax.experimental import pallas as pl
from jax.experimental.pallas import tpu as pltpu
from jax.sharding import PartitionSpec as P

MESH = pl.DeviceIdType.MESH
TPD = 2
DMAX = 8
CH = 48
ROWS = 128
COLS = 128
EDGE = 2 * DMAX
GROUPS = COLS // EDGE
STEP = 8
TAPS = 9
KPAD = 512
VMEM_LIMIT = 56 * 1024 * 1024
BF = jnp.bfloat16
F32 = jnp.float32
LIVE, REACH, DIL, TILE, DIAG, LAST_TILE, LAST_DIAG = 0, 1, 5, 7, 8, 9, 10
TURN = 56
BACK = 136
PIECES = 16
MOVES = 8


def iota(shape, dim):
    return lax.broadcasted_iota(jnp.int32, shape, dim)


def reach_of(par, ids):
    reach = jnp.where(ids < 64, jnp.where(ids < 32, par[REACH], par[REACH + 1]),
                      jnp.where(ids < 96, par[REACH + 2], par[REACH + 3]))
    return jnp.where(ids < par[LIVE], reach, 0)


def tap_moves(par):
    moves = []
    for a in range(3):
        for b in range(3):
            row = (a - 1) * par[DIL]
            moves.append((a, (b - 1) * par[DIL + 1] - row))
    return moves


def pack_edges(par, field, first, last):
    lane = iota((1, 2 * ROWS), 1)
    near = lane % DMAX
    want = jnp.where(lane < ROWS, near, par[LIVE] - DMAX + near)
    place = jnp.where(lane < ROWS, (lane // DMAX + EDGE // 2) % EDGE, (lane - ROWS) // DMAX)
    hit = jnp.where(iota((ROWS, 2 * ROWS), 0) == want, 1.0, 0.0)
    out = jnp.zeros((GROUPS * CH, 2 * ROWS), F32)
    for kk in range(0, EDGE, 2):
        weight = jnp.concatenate([jnp.where(place == kk + n, hit, 0.0).astype(BF) for n in range(2)], axis=0)
        lhs = jnp.concatenate(
            [jnp.concatenate([field[g * EDGE + kk + n] for g in range(GROUPS)], axis=0) for n in range(2)], axis=1)
        out += jnp.dot(lhs, weight, preferred_element_type=F32)
    out = out.astype(BF)
    for g in range(GROUPS):
        first[g] = out[g * CH:(g + 1) * CH, :ROWS]
        last[g] = out[g * CH:(g + 1) * CH, ROWS:]


def shift_rows(par, field, left, right, top, bot, moved):
    half = ROWS // 2
    lane = iota((1, 2 * ROWS), 1)
    move = jnp.where(lane < ROWS, -par[DIL], par[DIL])
    want = (lane % ROWS) + move
    rows = iota((ROWS, 2 * ROWS), 0)
    inner = jnp.where(rows == want, 1.0, 0.0).astype(BF)
    has_top = par[TILE] > 0
    has_bot = par[TILE] < par[LAST_TILE]
    top_want = jnp.where((want < 0) & has_top, want + DMAX, -1)
    low = want - par[LIVE]
    bot_want = jnp.where((low >= 0) & (low < DMAX) & has_bot, low, -1)
    wants = [jnp.where(rows < half, top_want, bot_want), jnp.where(rows < half, bot_want, top_want)]
    outers = [jnp.where(rows % DMAX == w, 1.0, 0.0) for w in wants]
    place = (rows % half) // DMAX
    has_left = par[DIAG] > 0
    has_right = par[DIAG] < par[LAST_DIAG]
    tops = top[...].reshape((GROUPS + 2) * CH, ROWS)
    bots = bot[...].reshape((GROUPS + 2) * CH, ROWS)
    upper = iota(tops.shape, 1) < half
    halos = [jnp.where(upper, tops, bots), jnp.where(upper, bots, tops)]

    for part in range(2):
        def column(at, carry):
            kk = at + part * (EDGE // 2)
            weight = jnp.concatenate([inner, jnp.where(place == at, outers[part], 0.0).astype(BF)], axis=0)
            tiles = [left[kk]] + [field[g * EDGE + kk] for g in range(GROUPS)] + [right[kk]]
            tiles[0] = jnp.where(has_left, tiles[0], jnp.zeros_like(tiles[0]))
            tiles[-1] = jnp.where(has_right, tiles[-1], jnp.zeros_like(tiles[-1]))
            lhs = jnp.concatenate([jnp.concatenate(tiles, axis=0), halos[part]], axis=1)
            out = jnp.dot(lhs, weight, preferred_element_type=F32)
            for g in range(GROUPS + 2):
                piece = out[g * CH:(g + 1) * CH]
                if g == 0:
                    piece = jnp.where(has_left, piece, 0.0)
                if g == GROUPS + 1:
                    piece = jnp.where(has_right, piece, 0.0)
                piece = piece.astype(BF)
                moved[0, g * EDGE + kk] = piece[:, :ROWS]
                moved[1, g * EDGE + kk] = tiles[g]
                moved[2, g * EDGE + kk] = piece[:, ROWS:]
            return carry

        lax.fori_loop(0, EDGE // 2, column, 0, unroll=2)


def pair(refs):
    return jnp.concatenate(refs, axis=1)


def eye():
    return jnp.where(iota((ROWS, ROWS), 0) == iota((ROWS, ROWS), 1), 1.0, 0.0).astype(BF)


def turn(one, value):
    return lax.dot_general(one, value, (((1,), (1,)), ((), ())), preferred_element_type=F32)


def turn_field(value, held, field):
    one = eye()

    def channels(step, carry):
        c = step * 4
        out = turn(one, jnp.concatenate([value(c + n) for n in range(4)], axis=0))
        for n in range(4):
            held[pl.ds(c + n, COLS, stride=TURN), :] = out[:, n * ROWS:(n + 1) * ROWS]
        return carry

    lax.fori_loop(0, CH // 4, channels, 0, unroll=2)

    def column(k, carry):
        field[k] = held[pl.ds(pl.multiple_of(k * TURN, 8), CH), :].astype(BF)
        return carry

    lax.fori_loop(0, COLS, column, 0, unroll=8)


def kept_cells(par):
    shape = (ROWS, COLS)
    return iota(shape, 1) + par[DIAG] * COLS < reach_of(par, iota(shape, 0))


def conv_forward(par, blocks, moved, masked, weight, grad_pre, hidden):
    moves = tap_moves(par)
    used = (TAPS + 1) * CH
    pad = jnp.zeros((KPAD - used, 2 * ROWS), BF)
    count, number = blocks

    def block(at, carry):
        for j in range(0, STEP, 2):
            k = number(at) * STEP + j
            tiles = [pair([moved[a, EDGE + k + n + shift] for n in range(2)]) for a, shift in moves]
            tiles += [pair([masked[k], masked[k + 1]]), pad]
            out = jnp.dot(weight[...], jnp.concatenate(tiles, axis=0), preferred_element_type=F32)
            pre, back = out[:CH], out[CH:]
            grad = jnp.where(pre > 0, back, 0.0).astype(BF)
            act = jnp.maximum(pre, 0.0).astype(BF)
            for n in range(2):
                grad_pre[k + n] = grad[:, n * ROWS:(n + 1) * ROWS]
                hidden[k + n] = act[:, n * ROWS:(n + 1) * ROWS]
        return carry

    lax.fori_loop(0, count, block, 0, unroll=4)


def kernel_grads(par, moved, masked, grad_pre, hidden, acc):
    moves = tap_moves(par)
    acc[...] = jnp.zeros_like(acc)

    def block(blk, carry):
        ks = [blk * STEP + j for j in range(STEP)]
        tiles = [pair([moved[a, EDGE + k + shift] for k in ks]) for a, shift in moves]
        lhs = jnp.concatenate(tiles + [pair([hidden[k] for k in ks])], axis=0)
        rhs = jnp.concatenate([pair([grad_pre[k] for k in ks]), pair([masked[k] for k in ks])], axis=0)
        acc[:, :2 * CH] += lax.dot_general(lhs, rhs, (((1,), (1,)), ((), ())), preferred_element_type=F32)
        return carry

    lax.fori_loop(0, COLS // STEP, block, 0, unroll=2)


def share_out(acc, part):
    flat = acc[...].T
    both = jnp.where(iota((CH, (TAPS + 1) * CH), 1) < TAPS * CH, flat[:CH], flat[CH:2 * CH])
    both = jnp.concatenate([both, jnp.zeros((CH, KPAD - (TAPS + 1) * CH), F32)], axis=1)
    per = part.shape[1]
    for n in range(PIECES):
        at, half = (n // 2) * 8, (n % 2) * 2 * ROWS
        piece = both[at:at + 8, half:half + 2 * ROWS] if at < CH else jnp.zeros((8, 2 * ROWS), F32)
        part[n // per, n % per] = piece


def place_weights(conv, mix, forward, backward):
    shape = (CH, KPAD)
    gap = iota(shape, 1) - iota(shape, 0)
    taps = jnp.zeros(shape, F32)
    back = jnp.zeros(shape, F32)
    for s in range(TAPS):
        put = jnp.where(gap == s * CH, 1.0, 0.0).astype(BF)
        taps += jnp.dot(conv[s], put, preferred_element_type=F32)
        back += lax.dot_general(conv[s], put, (((0,), (0,)), ((), ())), preferred_element_type=F32)
    put = jnp.where(gap == TAPS * CH, 1.0, 0.0).astype(BF)
    mixed = lax.dot_general(mix[...], put, (((0,), (0,)), ((), ())), preferred_element_type=F32)
    forward[...] = jnp.concatenate([taps, mixed], axis=0).astype(BF)
    backward[...] = back.astype(BF)


def conv_back(par, first, count, moved, weight, spread):
    moves = tap_moves(par)
    pad = jnp.zeros((KPAD - TAPS * CH, 2 * ROWS), BF)

    def block(blk, carry):
        for j in range(0, STEP, 2):
            k = blk * STEP + j
            tiles = [pair([moved[2 - a, EDGE + k + n - shift] for n in range(2)]) for a, shift in moves]
            out = jnp.dot(weight[...], jnp.concatenate(tiles + [pad], axis=0), preferred_element_type=F32)
            for n in range(2):
                spread[pl.ds(k + n, CH, stride=BACK), :] = out[:, n * ROWS:(n + 1) * ROWS]
        return carry

    lax.fori_loop(first, first + count, block, 0, unroll=4)


def finish(par, x_ref, g_ref, spread, out_hbm, sems):
    keep = kept_cells(par)
    live = iota((ROWS, COLS), 0) < par[LIVE]
    one = eye()

    def channels(step, carry):
        c = step * 4
        parts = [spread[pl.ds(pl.multiple_of((c + n) * BACK, 8), COLS), :].astype(BF) for n in range(4)]
        out = turn(one, jnp.concatenate(parts, axis=0))
        for n in range(4):
            part = out[:, n * ROWS:(n + 1) * ROWS]
            x = x_ref[c + n].astype(F32)
            full = g_ref[c + n].astype(F32) + jnp.where(keep & (x > 0), part, 0.0)
            x_ref[c + n] = jnp.where(live, full, 0.0).astype(BF)
        chunk(step).start()
        return carry

    def chunk(step):
        at = pl.ds(step * 4, 4)
        return pltpu.make_async_copy(x_ref.at[at], out_hbm.at[at], sems.at[step])

    def end(step, carry):
        chunk(step).wait()
        return carry

    lax.fori_loop(0, CH // 4, channels, 0, unroll=2)
    return lambda: lax.fori_loop(0, CH // 4, end, 0)


def remote(src, dst, send, recv, device):
    return pltpu.make_async_remote_copy(src_ref=src, dst_ref=dst, send_sem=send, recv_sem=recv,
                                        device_id=device, device_id_type=MESH)


def neighbours():
    tile, diag = lax.axis_index("tiles"), lax.axis_index("diag")
    tiles, diags = lax.axis_size("tiles"), lax.axis_size("diag")
    up, down = lax.rem(tile + tiles - 1, tiles), lax.rem(tile + 1, tiles)
    lo, hi = lax.rem(diag + diags - 1, diags), lax.rem(diag + 1, diags)
    return [(tile, lo), (tile, hi), (up, diag), (down, diag), (up, lo), (up, hi), (down, lo), (down, hi)]


def halo_copies(near, field, first, last, left, right, top, bot, send, recv):
    inner = pl.ds(1, GROUPS)
    plan = [
        (field.at[pl.ds(0, EDGE)], right),
        (field.at[pl.ds(COLS - EDGE, EDGE)], left),
        (first, bot.at[inner]),
        (last, top.at[inner]),
        (first.at[0], bot.at[GROUPS + 1]),
        (first.at[GROUPS - 1], bot.at[0]),
        (last.at[0], top.at[GROUPS + 1]),
        (last.at[GROUPS - 1], top.at[0]),
    ]
    return [remote(src, dst, send.at[n], recv.at[n], near[n]) for n, (src, dst) in enumerate(plan)]


def everything(inner, counts, reach, dilation, x_hbm, g_hbm, conv, mix, out_hbm, sum_ref,
               x_ref, g_ref, field, masked, grad_pre, hidden, moved, held, spread, acc, forward, backward,
               first1, last1, left1, right1, top1, bot1, first2, last2, left2, right2, top2, bot2,
               part, parts_in, far, done, load, leave, send1, recv1, send2, recv2, send3, recv3, send4, recv4, send5, recv5):
    tile, diag = lax.axis_index("tiles"), lax.axis_index("diag")
    tiles, diags = lax.axis_size("tiles"), lax.axis_size("diag")
    par = [counts[0] * (ROWS // 4)] + [reach[n] for n in range(4)] + [dilation[0], dilation[1]]
    par += [tile, diag, tiles - 1, diags - 1]
    x_load = pltpu.make_async_copy(x_hbm, x_ref, load.at[0])
    g_load = pltpu.make_async_copy(g_hbm, g_ref, load.at[1])
    x_load.start()
    g_load.start()

    shares = (tiles // inner) * diags
    outer, other = lax.div(tile, inner), lax.rem(tile, inner)
    rank = outer * diags + diag
    friends = [lax.rem(rank + step, shares) for step in range(1, shares)]
    friend_ids = [(lax.div(to, diags) * inner + other, lax.rem(to, diags)) for to in friends]
    cousin_ids = [(outer * inner + lax.rem(other + step, inner), diag) for step in range(1, inner)]
    near = neighbours()
    barrier = pltpu.get_barrier_semaphore()
    for device in near + friend_ids + cousin_ids:
        pl.semaphore_signal(barrier, inc=1, device_id=device, device_id_type=MESH)

    keep = jnp.where(kept_cells(par), 1.0, 0.0).astype(BF)
    x_load.wait()
    turn_field(lambda c: jnp.maximum(x_ref[c], jnp.zeros((), BF)) * keep, held, field)
    pl.semaphore_wait(barrier, len(near) + len(friend_ids) + len(cousin_ids))
    halo1 = halo_copies(near, field, first1, last1, left1, right1, top1, bot1, send1, recv1)
    halo1[0].start()
    halo1[1].start()
    pack_edges(par, field, first1, last1)
    for copy in halo1[2:]:
        copy.start()
    place_weights(conv, mix, forward, backward)
    g_load.wait()
    turn_field(lambda c: g_ref[c] * keep, held, masked)
    for copy in halo1:
        copy.wait_recv()

    shift_rows(par, field, left1, right1, top1, bot1, moved)
    halo2 = halo_copies(near, grad_pre, first2, last2, left2, right2, top2, bot2, send2, recv2)
    ends = EDGE // STEP
    middle = COLS // STEP - 2 * ends
    conv_forward(par, (2 * ends, lambda at: at + (at // ends) * middle), moved, masked, forward, grad_pre, hidden)
    halo2[0].start()
    halo2[1].start()
    conv_forward(par, (middle, lambda at: at + ends), moved, masked, forward, grad_pre, hidden)
    pack_edges(par, grad_pre, first2, last2)
    for copy in halo2[2:]:
        copy.start()
    kernel_grads(par, moved, masked, grad_pre, hidden, acc)
    share_out(acc, part)
    sum1 = [remote(part.at[to], parts_in.at[rank], send3.at[n], recv3.at[n], friend_ids[n]) for n, to in enumerate(friends)]
    sum2 = [remote(far.at[other], far.at[other], send4.at[n], recv4.at[n], to) for n, to in enumerate(cousin_ids)]
    sum3 = [remote(done.at[rank], done.at[rank], send5.at[n], recv5.at[n], to) for n, to in enumerate(friend_ids)]
    for copy in sum1:
        copy.start()
    parts_in[rank] = part[rank]

    for copy in halo2:
        copy.wait_recv()
    shift_rows(par, grad_pre, left2, right2, top2, bot2, moved)
    for copy in sum1:
        copy.wait_recv()
    far[other] = jnp.sum(parts_in[...], axis=0)
    for copy in sum2:
        copy.start()
    blocks = COLS // STEP
    conv_back(par, 0, blocks // 2, moved, backward, spread)
    for copy in sum2:
        copy.wait_recv()
    done[rank] = jnp.sum(far[...], axis=0)
    for copy in sum3:
        copy.start()
    conv_back(par, blocks // 2, blocks // 2, moved, backward, spread)
    drain = finish(par, x_ref, g_ref, spread, out_hbm, leave)
    for copy in sum3:
        copy.wait_recv()
    per = PIECES // shares
    for n in range(PIECES):
        sum_ref[n] = done[n // per, n % per]
    for copy in halo1 + halo2 + sum1 + sum2 + sum3:
        copy.wait_send()
    drain()


def unpack_kernel(scale, held, total, out, conv_ref, mix_ref, stage, enter, leave):
    size = CH // MOVES
    at = [pl.ds(n * size, size) for n in range(MOVES)]
    enters = [pltpu.make_async_copy(held.at[at[n]], stage.at[at[n]], enter.at[n]) for n in range(MOVES)]
    leaves = [pltpu.make_async_copy(stage.at[at[n]], out.at[at[n]], leave.at[n]) for n in range(MOVES)]
    for copy in enters:
        copy.start()
    for g in range(CH // 8):
        row = jnp.concatenate([total[2 * g], total[2 * g + 1]], axis=1) * scale
        for s in range(TAPS):
            conv_ref[s, 8 * g:8 * g + 8, :] = row[:, s * CH:(s + 1) * CH]
        mix_ref[8 * g:8 * g + 8, :] = row[:, TAPS * CH:(TAPS + 1) * CH]
        if g == 0:
            for n in range(MOVES):
                enters[n].wait()
                leaves[n].start()
    for copy in leaves:
        copy.wait()


def specs(space, count):
    return [pl.BlockSpec(memory_space=space)] * count


def body(inputs, cotangent, conv_weight, mix_weight, counts, band_reach, dilation):
    shape = jax.ShapeDtypeStruct
    tiles, diags = lax.axis_size("tiles"), lax.axis_size("diag")
    inner = 16 if tiles == 64 else 2
    shares = (tiles // inner) * diags
    dma = lambda n: pltpu.SemaphoreType.DMA((n,))
    whole = pltpu.VMEM((CH, ROWS, COLS), BF)
    field = pltpu.VMEM((COLS, CH, ROWS), BF)
    pack = pltpu.VMEM((GROUPS, CH, ROWS), BF)
    side = pltpu.VMEM((EDGE, CH, ROWS), BF)
    ends = pltpu.VMEM((GROUPS + 2, CH, ROWS), BF)
    slots = lambda n: pltpu.VMEM((n, PIECES // shares, 8, 2 * ROWS), F32)
    halo = [pack, pack, side, side, ends, ends]
    grad_inputs, total = pl.pallas_call(
        functools.partial(everything, inner),
        out_shape=[shape((CH, ROWS, COLS), BF), shape((PIECES, 8, 2 * ROWS), F32)],
        in_specs=specs(pltpu.SMEM, 3) + specs(pl.ANY, 2) + specs(pltpu.VMEM, 2),
        out_specs=specs(pl.ANY, 1) + specs(pltpu.VMEM, 1),
        scratch_shapes=[
            whole, whole, field, field, field, field,
            pltpu.VMEM((3, COLS + 2 * EDGE, CH, ROWS), BF),
            pltpu.VMEM((COLS * TURN, ROWS), F32),
            pltpu.VMEM((CH * BACK, ROWS), F32),
            pltpu.VMEM(((TAPS + 1) * CH, ROWS), F32),
            pltpu.VMEM((2 * CH, KPAD), BF),
            pltpu.VMEM((CH, KPAD), BF),
            *halo, *halo,
            slots(shares), slots(shares), slots(inner), slots(shares),
            dma(2), dma(CH // 4), dma(8), dma(8), dma(8), dma(8),
            dma(shares - 1), dma(shares - 1), dma(inner - 1), dma(inner - 1), dma(shares - 1), dma(shares - 1),
        ],
        cost_estimate=pl.CostEstimate(flops=6 * CH * CH * TAPS * ROWS * COLS, bytes_accessed=3 * 2 * CH * ROWS * COLS,
                                      transcendentals=0),
        compiler_params=pltpu.CompilerParams(collective_id=0, has_side_effects=True, vmem_limit_bytes=VMEM_LIMIT),
    )(counts, band_reach, dilation, inputs, cotangent, conv_weight, mix_weight)
    cells = TPD * tiles * (ROWS // 4) * COLS * diags
    return pl.pallas_call(
        functools.partial(unpack_kernel, 1.0 / math.sqrt(cells)),
        out_shape=[shape((CH, ROWS, COLS), BF), shape((TAPS, CH, CH), F32), shape((CH, CH), F32)],
        in_specs=specs(pltpu.HBM, 1) + specs(pltpu.VMEM, 1),
        out_specs=specs(pltpu.HBM, 1) + specs(pltpu.VMEM, 2),
        scratch_shapes=[whole, dma(MOVES), dma(MOVES)],
        compiler_params=pltpu.CompilerParams(vmem_limit_bytes=VMEM_LIMIT),
    )(grad_inputs, total)


def solution(mesh):
    in_specs = (
        P(None, "tiles", "diag"),
        P(None, "tiles", "diag"),
        P(),
        P(),
        P("tiles"),
        P("tiles"),
        P(),
    )
    out_specs = (P(None, "tiles", "diag"), P(), P())
    return jax.shard_map(body, mesh=mesh, in_specs=in_specs, out_specs=out_specs, check_vma=False)
```

```python
import functools
import math

import jax
import jax.numpy as jnp
from jax import lax
from jax.experimental import pallas as pl
from jax.experimental.pallas import tpu as pltpu
from jax.sharding import PartitionSpec as P

MESH = pl.DeviceIdType.MESH
TPD = 2
DMAX = 8
CH = 48
ROWS = 128
COLS = 128
EDGE = 2 * DMAX
GROUPS = COLS // EDGE
STEP = 8
TAPS = 9
KPAD = 512
VMEM_LIMIT = 56 * 1024 * 1024
BF = jnp.bfloat16
F32 = jnp.float32
LIVE, REACH, DIL, TILE, DIAG, LAST_TILE, LAST_DIAG = 0, 1, 5, 7, 8, 9, 10
TURN = 56
BACK = 136
PIECES = 16
LOADS = 3
MOVES = 4


def iota(shape, dim):
    return lax.broadcasted_iota(jnp.int32, shape, dim)


def reach_of(par, ids):
    reach = jnp.where(ids < 64, jnp.where(ids < 32, par[REACH], par[REACH + 1]),
                      jnp.where(ids < 96, par[REACH + 2], par[REACH + 3]))
    return jnp.where(ids < par[LIVE], reach, 0)


def tap_moves(par):
    moves = []
    for a in range(3):
        for b in range(3):
            row = (a - 1) * par[DIL]
            moves.append((a, (b - 1) * par[DIL + 1] - row))
    return moves


def pack_edges(par, field, first, last):
    lane = iota((1, 2 * ROWS), 1)
    near = lane % DMAX
    want = jnp.where(lane < ROWS, near, par[LIVE] - DMAX + near)
    place = jnp.where(lane < ROWS, (lane // DMAX + EDGE // 2) % EDGE, (lane - ROWS) // DMAX)
    hit = jnp.where(iota((ROWS, 2 * ROWS), 0) == want, 1.0, 0.0)
    out = jnp.zeros((GROUPS * CH, 2 * ROWS), F32)
    for kk in range(0, EDGE, 2):
        weight = jnp.concatenate([jnp.where(place == kk + n, hit, 0.0).astype(BF) for n in range(2)], axis=0)
        lhs = jnp.concatenate(
            [jnp.concatenate([field[(g + 1) * EDGE + kk + n] for g in range(GROUPS)], axis=0) for n in range(2)], axis=1)
        out += jnp.dot(lhs, weight, preferred_element_type=F32)
    out = out.astype(BF)
    for g in range(GROUPS):
        first[g] = out[g * CH:(g + 1) * CH, :ROWS]
        last[g] = out[g * CH:(g + 1) * CH, ROWS:]


def set_edges(par, left, right, field):
    for e in range(EDGE):
        low, high = left[e], right[e]
        field[e] = jnp.where(par[DIAG] > 0, low, jnp.zeros_like(low))
        field[EDGE + COLS + e] = jnp.where(par[DIAG] < par[LAST_DIAG], high, jnp.zeros_like(high))


def shift_rows(par, groups, field, top, bot, moved):
    half = ROWS // 2
    lane = iota((1, 2 * ROWS), 1)
    move = jnp.where(lane < ROWS, -par[DIL], par[DIL])
    want = (lane % ROWS) + move
    rows = iota((ROWS, 2 * ROWS), 0)
    inner = jnp.where(rows == want, 1.0, 0.0).astype(BF)
    has_top = par[TILE] > 0
    has_bot = par[TILE] < par[LAST_TILE]
    top_want = jnp.where((want < 0) & has_top, want + DMAX, -1)
    low = want - par[LIVE]
    bot_want = jnp.where((low >= 0) & (low < DMAX) & has_bot, low, -1)
    wants = [jnp.where(rows < half, top_want, bot_want), jnp.where(rows < half, bot_want, top_want)]
    outers = [jnp.where(rows % DMAX == w, 1.0, 0.0) for w in wants]
    place = (rows % half) // DMAX
    has_left = par[DIAG] > 0
    has_right = par[DIAG] < par[LAST_DIAG]
    tops = jnp.concatenate([top[g] for g in groups], axis=0)
    bots = jnp.concatenate([bot[g] for g in groups], axis=0)
    upper = iota(tops.shape, 1) < half
    halos = [jnp.where(upper, tops, bots), jnp.where(upper, bots, tops)]

    for part in range(2):
        def column(at, carry):
            kk = at + part * (EDGE // 2)
            weight = jnp.concatenate([inner, jnp.where(place == at, outers[part], 0.0).astype(BF)], axis=0)
            tiles = [field[g * EDGE + kk] for g in groups]
            lhs = jnp.concatenate([jnp.concatenate(tiles, axis=0), halos[part]], axis=1)
            out = jnp.dot(lhs, weight, preferred_element_type=F32)
            for n, g in enumerate(groups):
                piece = out[n * CH:(n + 1) * CH]
                if g == 0:
                    piece = jnp.where(has_left, piece, 0.0)
                if g == GROUPS + 1:
                    piece = jnp.where(has_right, piece, 0.0)
                piece = piece.astype(BF)
                moved[0, g * EDGE + kk] = piece[:, :ROWS]
                moved[1, g * EDGE + kk] = piece[:, ROWS:]
            return carry

        lax.fori_loop(0, EDGE // 2, column, 0, unroll=4)


def tapped(field, moved, a, k):
    return field[EDGE + k] if a == 1 else moved[a // 2, EDGE + k]


def pair(refs):
    return jnp.concatenate(refs, axis=1)


def eye():
    return jnp.where(iota((ROWS, ROWS), 0) == iota((ROWS, ROWS), 1), 1.0, 0.0).astype(BF)


def turn(one, value):
    return lax.dot_general(one, value, (((1,), (1,)), ((), ())), preferred_element_type=F32)


def turn_field(loads, value, held, put):
    one = eye()
    size = CH // len(loads)

    def channels(step, carry):
        c = step * 4
        out = turn(one, jnp.concatenate([value(c + n) for n in range(4)], axis=0))
        for n in range(4):
            held[pl.ds(c + n, COLS, stride=TURN), :] = out[:, n * ROWS:(n + 1) * ROWS]
        return carry

    for n, load in enumerate(loads):
        load.wait()
        lax.fori_loop(n * size // 4, (n + 1) * size // 4, channels, 0, unroll=size // 4)

    def column(k, carry):
        put(k, held[pl.ds(pl.multiple_of(k * TURN, 8), CH), :].astype(BF))
        return carry

    lax.fori_loop(0, COLS, column, 0, unroll=16)


def kept_cells(par):
    shape = (ROWS, COLS)
    return iota(shape, 1) + par[DIAG] * COLS < reach_of(par, iota(shape, 0))


def conv_forward(par, blocks, field, moved, masked, weight, grad_pre, hidden):
    moves = tap_moves(par)
    used = (TAPS + 1) * CH
    pad = jnp.zeros((KPAD - used, 2 * ROWS), BF)
    count, number = blocks

    def block(at, carry):
        for j in range(0, STEP, 2):
            k = number(at) * STEP + j
            tiles = [pair([tapped(field, moved, a, k + n + shift) for n in range(2)]) for a, shift in moves]
            tiles += [pair([masked[k], masked[k + 1]]), pad]
            out = jnp.dot(weight[...], jnp.concatenate(tiles, axis=0), preferred_element_type=F32)
            pre, back = out[:CH], out[CH:]
            grad = jnp.where(pre > 0, back, 0.0).astype(BF)
            act = jnp.maximum(pre, 0.0).astype(BF)
            for n in range(2):
                grad_pre[EDGE + k + n] = grad[:, n * ROWS:(n + 1) * ROWS]
                hidden[k + n] = act[:, n * ROWS:(n + 1) * ROWS]
        return carry

    lax.fori_loop(0, count, block, 0, unroll=4)


def kernel_grads(par, field, moved, masked, grad_pre, hidden, acc):
    moves = tap_moves(par)
    acc[...] = jnp.zeros_like(acc)

    def block(blk, carry):
        ks = [blk * STEP + j for j in range(STEP)]
        tiles = [pair([tapped(field, moved, a, k + shift) for k in ks]) for a, shift in moves]
        lhs = jnp.concatenate(tiles + [pair([hidden[k] for k in ks])], axis=0)
        rhs = jnp.concatenate([pair([grad_pre[EDGE + k] for k in ks]), pair([masked[k] for k in ks])], axis=0)
        acc[:, :2 * CH] += lax.dot_general(lhs, rhs, (((1,), (1,)), ((), ())), preferred_element_type=F32)
        return carry

    lax.fori_loop(0, COLS // STEP, block, 0, unroll=2)


def share_out(acc, part):
    flat = acc[...].T
    both = jnp.where(iota((CH, (TAPS + 1) * CH), 1) < TAPS * CH, flat[:CH], flat[CH:2 * CH])
    both = jnp.concatenate([both, jnp.zeros((CH, KPAD - (TAPS + 1) * CH), F32)], axis=1)
    per = part.shape[1]
    for n in range(PIECES):
        at, half = (n // 2) * 8, (n % 2) * 2 * ROWS
        piece = both[at:at + 8, half:half + 2 * ROWS] if at < CH else jnp.zeros((8, 2 * ROWS), F32)
        part[n // per, n % per] = piece


def place_weights(conv, mix, forward, backward):
    shape = (CH, KPAD)
    gap = iota(shape, 1) - iota(shape, 0)
    taps = jnp.zeros(shape, F32)
    back = jnp.zeros(shape, F32)
    for s in range(TAPS):
        put = jnp.where(gap == s * CH, 1.0, 0.0).astype(BF)
        taps += jnp.dot(conv[s], put, preferred_element_type=F32)
        back += lax.dot_general(conv[s], put, (((0,), (0,)), ((), ())), preferred_element_type=F32)
    put = jnp.where(gap == TAPS * CH, 1.0, 0.0).astype(BF)
    mixed = lax.dot_general(mix[...], put, (((0,), (0,)), ((), ())), preferred_element_type=F32)
    forward[...] = jnp.concatenate([taps, mixed], axis=0).astype(BF)
    backward[...] = back.astype(BF)


def conv_back(par, first, count, field, moved, weight, spread):
    moves = tap_moves(par)
    pad = jnp.zeros((KPAD - TAPS * CH, 2 * ROWS), BF)

    def block(blk, carry):
        for j in range(0, STEP, 2):
            k = blk * STEP + j
            tiles = [pair([tapped(field, moved, 2 - a, k + n - shift) for n in range(2)]) for a, shift in moves]
            out = jnp.dot(weight[...], jnp.concatenate(tiles + [pad], axis=0), preferred_element_type=F32)
            for n in range(2):
                spread[pl.ds(k + n, CH, stride=BACK), :] = out[:, n * ROWS:(n + 1) * ROWS]
        return carry

    lax.fori_loop(first, first + count, block, 0, unroll=4)


def finish(par, x_ref, g_ref, spread, out_ref):
    keep = jnp.where(kept_cells(par), 1.0, 0.0).astype(BF)
    live = jnp.where(iota((ROWS, COLS), 0) < par[LIVE], 1.0, 0.0).astype(BF)
    one = eye()
    zero = jnp.zeros((ROWS, COLS), BF)

    def channels(step, carry):
        c = step * 4
        parts = [spread[pl.ds(pl.multiple_of((c + n) * BACK, 8), COLS), :].astype(BF) for n in range(4)]
        out = turn(one, jnp.concatenate(parts, axis=0)).astype(BF)
        for n in range(4):
            part = jnp.where(x_ref[c + n] > zero, out[:, n * ROWS:(n + 1) * ROWS], zero)
            out_ref[c + n] = (g_ref[c + n] + part * keep) * live
        return carry

    lax.fori_loop(0, CH // 4, channels, 0, unroll=4)


def remote(src, dst, send, recv, device):
    return pltpu.make_async_remote_copy(src_ref=src, dst_ref=dst, send_sem=send, recv_sem=recv,
                                        device_id=device, device_id_type=MESH)


def neighbours():
    tile, diag = lax.axis_index("tiles"), lax.axis_index("diag")
    tiles, diags = lax.axis_size("tiles"), lax.axis_size("diag")
    up, down = lax.rem(tile + tiles - 1, tiles), lax.rem(tile + 1, tiles)
    lo, hi = lax.rem(diag + diags - 1, diags), lax.rem(diag + 1, diags)
    return [(tile, lo), (tile, hi), (up, diag), (down, diag), (up, lo), (up, hi), (down, lo), (down, hi)]


def halo_copies(near, field, first, last, left, right, top, bot, send, recv):
    inner = pl.ds(1, GROUPS)
    plan = [
        (field.at[pl.ds(EDGE, EDGE)], right),
        (field.at[pl.ds(COLS, EDGE)], left),
        (first, bot.at[inner]),
        (last, top.at[inner]),
        (first.at[0], bot.at[GROUPS + 1]),
        (first.at[GROUPS - 1], bot.at[0]),
        (last.at[0], top.at[GROUPS + 1]),
        (last.at[GROUPS - 1], top.at[0]),
    ]
    return [remote(src, dst, send.at[n], recv.at[n], near[n]) for n, (src, dst) in enumerate(plan)]


def unpack(scale, done, conv_ref, mix_ref):
    per = done.shape[1]
    for g in range(CH // 8):
        halves = [done[n // per, n % per] for n in (2 * g, 2 * g + 1)]
        row = jnp.concatenate(halves, axis=1) * scale
        for s in range(TAPS):
            conv_ref[s, 8 * g:8 * g + 8, :] = row[:, s * CH:(s + 1) * CH]
        mix_ref[8 * g:8 * g + 8, :] = row[:, TAPS * CH:(TAPS + 1) * CH]


def everything(inner, scale, counts, reach, dilation, x_hbm, g_hbm, conv, mix, out_ref, conv_ref, mix_ref,
               x_ref, g_ref, field, masked, grad_pre, hidden, moved, held, spread, acc, forward, backward,
               first1, last1, left1, right1, top1, bot1, first2, last2, left2, right2, top2, bot2,
               part, parts_in, far, done, load, send1, recv1, send2, recv2, send3, recv3, send4, recv4, send5, recv5):
    tile, diag = lax.axis_index("tiles"), lax.axis_index("diag")
    tiles, diags = lax.axis_size("tiles"), lax.axis_size("diag")
    par = [counts[0] * (ROWS // 4)] + [reach[n] for n in range(4)] + [dilation[0], dilation[1]]
    par += [tile, diag, tiles - 1, diags - 1]
    parts = [pl.ds(n * (CH // LOADS), CH // LOADS) for n in range(LOADS)]
    x_loads = [pltpu.make_async_copy(x_hbm.at[at], x_ref.at[at], load.at[n]) for n, at in enumerate(parts)]
    g_loads = [pltpu.make_async_copy(g_hbm.at[at], g_ref.at[at], load.at[LOADS + n]) for n, at in enumerate(parts)]
    for copy in x_loads + g_loads:
        copy.start()

    shares = (tiles // inner) * diags
    outer, other = lax.div(tile, inner), lax.rem(tile, inner)
    rank = outer * diags + diag
    friends = [lax.rem(rank + step, shares) for step in range(1, shares)]
    friend_ids = [(lax.div(to, diags) * inner + other, lax.rem(to, diags)) for to in friends]
    cousin_ids = [(outer * inner + lax.rem(other + step, inner), diag) for step in range(1, inner)]
    near = neighbours()
    barrier = pltpu.get_barrier_semaphore()
    for device in near + friend_ids + cousin_ids:
        pl.semaphore_signal(barrier, inc=1, device_id=device, device_id_type=MESH)

    keep = jnp.where(kept_cells(par), 1.0, 0.0).astype(BF)

    def put_field(k, value):
        field[EDGE + k] = value

    def put_masked(k, value):
        masked[k] = value

    turn_field(x_loads, lambda c: jnp.maximum(x_ref[c], jnp.zeros((), BF)) * keep, held, put_field)
    pl.semaphore_wait(barrier, len(near) + len(friend_ids) + len(cousin_ids))
    halo1 = halo_copies(near, field, first1, last1, left1, right1, top1, bot1, send1, recv1)
    halo1[0].start()
    halo1[1].start()
    pack_edges(par, field, first1, last1)
    for copy in halo1[2:]:
        copy.start()
    place_weights(conv, mix, forward, backward)
    turn_field(g_loads, lambda c: g_ref[c] * keep, held, put_masked)
    inside = range(1, GROUPS + 1)
    for copy in halo1[2:4]:
        copy.wait_recv()
    shift_rows(par, inside, field, top1, bot1, moved)
    halo2 = halo_copies(near, grad_pre, first2, last2, left2, right2, top2, bot2, send2, recv2)
    ends = EDGE // STEP
    middle = COLS // STEP - 2 * ends
    conv_forward(par, (middle, lambda at: at + ends), field, moved, masked, forward, grad_pre, hidden)
    for copy in halo1[:2] + halo1[4:]:
        copy.wait_recv()
    set_edges(par, left1, right1, field)
    shift_rows(par, [0, GROUPS + 1], field, top1, bot1, moved)
    conv_forward(par, (2 * ends, lambda at: at + (at // ends) * middle), field, moved, masked, forward, grad_pre, hidden)
    halo2[0].start()
    halo2[1].start()
    pack_edges(par, grad_pre, first2, last2)
    for copy in halo2[2:]:
        copy.start()
    kernel_grads(par, field, moved, masked, grad_pre, hidden, acc)
    share_out(acc, part)
    sum1 = [remote(part.at[to], parts_in.at[rank], send3, recv3, friend_ids[n]) for n, to in enumerate(friends)]
    sum2 = [remote(far.at[other], far.at[other], send4, recv4, to) for to in cousin_ids]
    sum3 = [remote(done.at[rank], done.at[rank], send5, recv5, to) for to in friend_ids]
    all1, all2, all3 = [
        remote(slots.at[pl.ds(0, slots.shape[0] - 1)], slots.at[pl.ds(0, slots.shape[0] - 1)], send, recv, near[0])
        for slots, send, recv in ((parts_in, send3, recv3), (far, send4, recv4), (done, send5, recv5))]
    for copy in sum1:
        copy.start()
    parts_in[rank] = part[rank]

    for copy in halo2:
        copy.wait_recv()
    set_edges(par, left2, right2, grad_pre)
    shift_rows(par, range(GROUPS + 2), grad_pre, top2, bot2, moved)
    all1.wait_recv()
    far[other] = jnp.sum(parts_in[...], axis=0)
    for copy in sum2:
        copy.start()
    blocks = COLS // STEP
    conv_back(par, 0, blocks // 2, grad_pre, moved, backward, spread)
    all2.wait_recv()
    done[rank] = jnp.sum(far[...], axis=0)
    for copy in sum3:
        copy.start()
    conv_back(par, blocks // 2, blocks // 2, grad_pre, moved, backward, spread)
    finish(par, x_ref, g_ref, spread, out_ref)
    all3.wait_recv()
    unpack(scale, done, conv_ref, mix_ref)
    for copy in halo1 + halo2 + [all1, all2, all3]:
        copy.wait_send()


def move_out(field, conv, mix, field_out, conv_out, mix_out, sems):
    size = CH // MOVES
    pieces = [(field.at[pl.ds(n * size, size)], field_out.at[pl.ds(n * size, size)]) for n in range(MOVES)]
    copies = [pltpu.make_async_copy(src, dst, sems.at[n])
              for n, (src, dst) in enumerate([(conv, conv_out), (mix, mix_out)] + pieces)]
    for copy in copies:
        copy.start()
    for copy in copies:
        copy.wait()


def specs(space, count):
    return [pl.BlockSpec(memory_space=space)] * count


def body(inputs, cotangent, conv_weight, mix_weight, counts, band_reach, dilation):
    shape = jax.ShapeDtypeStruct
    tiles, diags = lax.axis_size("tiles"), lax.axis_size("diag")
    inner = 16 if tiles == 64 else 2
    shares = (tiles // inner) * diags
    dma = lambda n: pltpu.SemaphoreType.DMA((n,))
    whole = pltpu.VMEM((CH, ROWS, COLS), BF)
    field = pltpu.VMEM((COLS, CH, ROWS), BF)
    pack = pltpu.VMEM((GROUPS, CH, ROWS), BF)
    wide = pltpu.VMEM((COLS + 2 * EDGE, CH, ROWS), BF)
    side = pltpu.VMEM((EDGE, CH, ROWS), BF)
    ends = pltpu.VMEM((GROUPS + 2, CH, ROWS), BF)
    slots = lambda n: pltpu.VMEM((n, PIECES // shares, 8, 2 * ROWS), F32)
    halo = [pack, pack, side, side, ends, ends]
    cells = TPD * tiles * (ROWS // 4) * COLS * diags
    results = pl.pallas_call(
        functools.partial(everything, inner, 1.0 / math.sqrt(cells)),
        out_shape=[pltpu.VMEM((CH, ROWS, COLS), BF), pltpu.VMEM((TAPS, CH, CH), F32), pltpu.VMEM((CH, CH), F32)],
        in_specs=specs(pltpu.SMEM, 3) + specs(pl.ANY, 2) + specs(pltpu.VMEM, 2),
        out_specs=specs(pltpu.VMEM, 3),
        scratch_shapes=[
            whole, whole, wide, field, wide, field,
            pltpu.VMEM((2, COLS + 2 * EDGE, CH, ROWS), BF),
            pltpu.VMEM(((COLS + 1) * TURN, ROWS), F32),
            pltpu.VMEM(((CH + 1) * BACK, ROWS), F32),
            pltpu.VMEM(((TAPS + 1) * CH, ROWS), F32),
            pltpu.VMEM((2 * CH, KPAD), BF),
            pltpu.VMEM((CH, KPAD), BF),
            *halo, *halo,
            slots(shares), slots(shares), slots(inner), slots(shares),
            dma(2 * LOADS), dma(8), dma(8), dma(8), dma(8),
            *[pltpu.SemaphoreType.DMA] * 6,
        ],
        cost_estimate=pl.CostEstimate(flops=6 * CH * CH * TAPS * ROWS * COLS, bytes_accessed=3 * 2 * CH * ROWS * COLS,
                                      transcendentals=0),
        compiler_params=pltpu.CompilerParams(collective_id=0, has_side_effects=True, vmem_limit_bytes=VMEM_LIMIT),
    )(counts, band_reach, dilation, inputs, cotangent, conv_weight, mix_weight)
    return pl.pallas_call(
        move_out,
        out_shape=[shape(r.shape, r.dtype) for r in results],
        in_specs=specs(pltpu.VMEM, 3),
        out_specs=specs(pltpu.HBM, 3),
        scratch_shapes=[dma(MOVES + 2)],
        compiler_params=pltpu.CompilerParams(vmem_limit_bytes=8 * 1024 * 1024),
    )(*results)


def solution(mesh):
    in_specs = (
        P(None, "tiles", "diag"),
        P(None, "tiles", "diag"),
        P(),
        P(),
        P("tiles"),
        P("tiles"),
        P(),
    )
    out_specs = (P(None, "tiles", "diag"), P(), P())
    return jax.shard_map(body, mesh=mesh, in_specs=in_specs, out_specs=out_specs, check_vma=False)
```

```python
import functools
import math

import jax
import jax.numpy as jnp
from jax import lax
from jax.experimental import pallas as pl
from jax.experimental.pallas import tpu as pltpu
from jax.sharding import PartitionSpec as P

MESH = pl.DeviceIdType.MESH
TPD = 2
DMAX = 8
CH = 48
ROWS = 128
COLS = 128
EDGE = 2 * DMAX
GROUPS = COLS // EDGE
STEP = 8
TAPS = 9
KPAD = 512
VMEM_LIMIT = 56 * 1024 * 1024
BF = jnp.bfloat16
F32 = jnp.float32
LIVE, REACH, DIL, TILE, DIAG, LAST_TILE, LAST_DIAG = 0, 1, 5, 7, 8, 9, 10
TURN = 56
BACK = 136
LOADS = 3
MOVES = 4


def iota(shape, dim):
    return lax.broadcasted_iota(jnp.int32, shape, dim)


def reach_of(par, ids):
    reach = jnp.where(ids < 64, jnp.where(ids < 32, par[REACH], par[REACH + 1]),
                      jnp.where(ids < 96, par[REACH + 2], par[REACH + 3]))
    return jnp.where(ids < par[LIVE], reach, 0)


def tap_moves(par):
    moves = []
    for a in range(3):
        for b in range(3):
            row = (a - 1) * par[DIL]
            moves.append((a, (b - 1) * par[DIL + 1] - row))
    return moves


def pack_edges(par, field, first, last):
    lane = iota((1, 2 * ROWS), 1)
    near = lane % DMAX
    want = jnp.where(lane < ROWS, near, par[LIVE] - DMAX + near)
    place = jnp.where(lane < ROWS, (lane // DMAX + EDGE // 2) % EDGE, (lane - ROWS) // DMAX)
    hit = jnp.where(iota((ROWS, 2 * ROWS), 0) == want, 1.0, 0.0)
    out = jnp.zeros((GROUPS * CH, 2 * ROWS), F32)
    for kk in range(0, EDGE, 2):
        weight = jnp.concatenate([jnp.where(place == kk + n, hit, 0.0).astype(BF) for n in range(2)], axis=0)
        lhs = jnp.concatenate(
            [jnp.concatenate([field[(g + 1) * EDGE + kk + n] for g in range(GROUPS)], axis=0) for n in range(2)], axis=1)
        out += jnp.dot(lhs, weight, preferred_element_type=F32)
    out = out.astype(BF)
    for g in range(GROUPS):
        first[g] = out[g * CH:(g + 1) * CH, :ROWS]
        last[g] = out[g * CH:(g + 1) * CH, ROWS:]


def set_edges(par, left, right, field):
    for e in range(EDGE):
        low, high = left[e], right[e]
        field[e] = jnp.where(par[DIAG] > 0, low, jnp.zeros_like(low))
        field[EDGE + COLS + e] = jnp.where(par[DIAG] < par[LAST_DIAG], high, jnp.zeros_like(high))


def shift_rows(par, groups, field, top, bot, moved):
    half = ROWS // 2
    lane = iota((1, 2 * ROWS), 1)
    move = jnp.where(lane < ROWS, -par[DIL], par[DIL])
    want = (lane % ROWS) + move
    rows = iota((ROWS, 2 * ROWS), 0)
    inner = jnp.where(rows == want, 1.0, 0.0).astype(BF)
    has_top = par[TILE] > 0
    has_bot = par[TILE] < par[LAST_TILE]
    top_want = jnp.where((want < 0) & has_top, want + DMAX, -1)
    low = want - par[LIVE]
    bot_want = jnp.where((low >= 0) & (low < DMAX) & has_bot, low, -1)
    wants = [jnp.where(rows < half, top_want, bot_want), jnp.where(rows < half, bot_want, top_want)]
    outers = [jnp.where(rows % DMAX == w, 1.0, 0.0) for w in wants]
    place = (rows % half) // DMAX
    has_left = par[DIAG] > 0
    has_right = par[DIAG] < par[LAST_DIAG]
    tops = jnp.concatenate([top[g] for g in groups], axis=0)
    bots = jnp.concatenate([bot[g] for g in groups], axis=0)
    upper = iota(tops.shape, 1) < half
    halos = [jnp.where(upper, tops, bots), jnp.where(upper, bots, tops)]

    for part in range(2):
        def column(at, carry):
            kk = at + part * (EDGE // 2)
            weight = jnp.concatenate([inner, jnp.where(place == at, outers[part], 0.0).astype(BF)], axis=0)
            tiles = [field[g * EDGE + kk] for g in groups]
            lhs = jnp.concatenate([jnp.concatenate(tiles, axis=0), halos[part]], axis=1)
            out = jnp.dot(lhs, weight, preferred_element_type=F32)
            for n, g in enumerate(groups):
                piece = out[n * CH:(n + 1) * CH]
                if g == 0:
                    piece = jnp.where(has_left, piece, 0.0)
                if g == GROUPS + 1:
                    piece = jnp.where(has_right, piece, 0.0)
                piece = piece.astype(BF)
                moved[0, g * EDGE + kk] = piece[:, :ROWS]
                moved[1, g * EDGE + kk] = piece[:, ROWS:]
            return carry

        lax.fori_loop(0, EDGE // 2, column, 0, unroll=4)


def tapped(field, moved, a, k):
    return field[EDGE + k] if a == 1 else moved[a // 2, EDGE + k]


def pair(refs):
    return jnp.concatenate(refs, axis=1)


def eye():
    return jnp.where(iota((ROWS, ROWS), 0) == iota((ROWS, ROWS), 1), 1.0, 0.0).astype(BF)


def turn(one, value):
    return lax.dot_general(one, value, (((1,), (1,)), ((), ())), preferred_element_type=F32)


def turn_field(loads, value, held, put):
    one = eye()
    size = CH // len(loads)

    def channels(step, carry):
        c = step * 4
        out = turn(one, jnp.concatenate([value(c + n) for n in range(4)], axis=0))
        for n in range(4):
            held[pl.ds(c + n, COLS, stride=TURN), :] = out[:, n * ROWS:(n + 1) * ROWS]
        return carry

    for n, load in enumerate(loads):
        load.wait()
        lax.fori_loop(n * size // 4, (n + 1) * size // 4, channels, 0, unroll=size // 4)

    def column(k, carry):
        put(k, held[pl.ds(pl.multiple_of(k * TURN, 8), CH), :].astype(BF))
        return carry

    lax.fori_loop(0, COLS, column, 0, unroll=16)


def kept_cells(par):
    shape = (ROWS, COLS)
    return iota(shape, 1) + par[DIAG] * COLS < reach_of(par, iota(shape, 0))


def conv_forward(par, blocks, field, moved, masked, weight, grad_pre, hidden):
    moves = tap_moves(par)
    used = (TAPS + 1) * CH
    pad = jnp.zeros((KPAD - used, 2 * ROWS), BF)
    count, number = blocks

    def block(at, carry):
        for j in range(0, STEP, 2):
            k = number(at) * STEP + j
            tiles = [pair([tapped(field, moved, a, k + n + shift) for n in range(2)]) for a, shift in moves]
            tiles += [pair([masked[k], masked[k + 1]]), pad]
            out = jnp.dot(weight[...], jnp.concatenate(tiles, axis=0), preferred_element_type=F32)
            pre, back = out[:CH], out[CH:]
            grad = jnp.where(pre > 0, back, 0.0).astype(BF)
            act = jnp.maximum(pre, 0.0).astype(BF)
            for n in range(2):
                grad_pre[EDGE + k + n] = grad[:, n * ROWS:(n + 1) * ROWS]
                hidden[k + n] = act[:, n * ROWS:(n + 1) * ROWS]
        return carry

    lax.fori_loop(0, count, block, 0, unroll=4)


def kernel_grads(par, field, moved, masked, grad_pre, hidden, acc):
    moves = tap_moves(par)
    acc[...] = jnp.zeros_like(acc)

    def block(blk, carry):
        ks = [blk * STEP + j for j in range(STEP)]
        tiles = [pair([tapped(field, moved, a, k + shift) for k in ks]) for a, shift in moves]
        lhs = jnp.concatenate(tiles + [pair([hidden[k] for k in ks])], axis=0)
        rhs = jnp.concatenate([pair([grad_pre[EDGE + k] for k in ks]), pair([masked[k] for k in ks])], axis=0)
        acc[:, :2 * CH] += lax.dot_general(lhs, rhs, (((1,), (1,)), ((), ())), preferred_element_type=F32)
        return carry

    lax.fori_loop(0, COLS // STEP, block, 0, unroll=2)


def share_out(acc, part):
    flat = acc[...].T
    both = jnp.where(iota((CH, (TAPS + 1) * CH), 1) < TAPS * CH, flat[:CH], flat[CH:2 * CH])
    both = jnp.concatenate([both, jnp.zeros((CH, KPAD - (TAPS + 1) * CH), F32)], axis=1)
    rows = jnp.concatenate([both[:, n * ROWS:(n + 1) * ROWS] for n in range(KPAD // ROWS)], axis=0)
    size = part.shape[1]
    for n in range(part.shape[0]):
        part[n] = rows[n * size:(n + 1) * size]


def place_weights(conv, mix, forward, backward):
    shape = (CH, KPAD)
    gap = iota(shape, 1) - iota(shape, 0)
    taps = jnp.zeros(shape, F32)
    back = jnp.zeros(shape, F32)
    for s in range(TAPS):
        put = jnp.where(gap == s * CH, 1.0, 0.0).astype(BF)
        taps += jnp.dot(conv[s], put, preferred_element_type=F32)
        back += lax.dot_general(conv[s], put, (((0,), (0,)), ((), ())), preferred_element_type=F32)
    put = jnp.where(gap == TAPS * CH, 1.0, 0.0).astype(BF)
    mixed = lax.dot_general(mix[...], put, (((0,), (0,)), ((), ())), preferred_element_type=F32)
    forward[...] = jnp.concatenate([taps, mixed], axis=0).astype(BF)
    backward[...] = back.astype(BF)


def conv_back(par, first, count, field, moved, weight, spread):
    moves = tap_moves(par)
    pad = jnp.zeros((KPAD - TAPS * CH, 2 * ROWS), BF)

    def block(blk, carry):
        for j in range(0, STEP, 2):
            k = blk * STEP + j
            tiles = [pair([tapped(field, moved, 2 - a, k + n - shift) for n in range(2)]) for a, shift in moves]
            out = jnp.dot(weight[...], jnp.concatenate(tiles + [pad], axis=0), preferred_element_type=F32)
            for n in range(2):
                spread[pl.ds(k + n, CH, stride=BACK), :] = out[:, n * ROWS:(n + 1) * ROWS]
        return carry

    lax.fori_loop(first, first + count, block, 0, unroll=4)


def finish(par, x_ref, g_ref, spread, out_ref):
    keep = jnp.where(kept_cells(par), 1.0, 0.0).astype(BF)
    live = jnp.where(iota((ROWS, COLS), 0) < par[LIVE], 1.0, 0.0).astype(BF)
    one = eye()
    zero = jnp.zeros((ROWS, COLS), BF)

    def channels(step, carry):
        c = step * 4
        parts = [spread[pl.ds(pl.multiple_of((c + n) * BACK, 8), COLS), :].astype(BF) for n in range(4)]
        out = turn(one, jnp.concatenate(parts, axis=0)).astype(BF)
        for n in range(4):
            part = jnp.where(x_ref[c + n] > zero, out[:, n * ROWS:(n + 1) * ROWS], zero)
            out_ref[c + n] = (g_ref[c + n] + part * keep) * live
        return carry

    lax.fori_loop(0, CH // 4, channels, 0, unroll=4)


def remote(src, dst, send, recv, device):
    return pltpu.make_async_remote_copy(src_ref=src, dst_ref=dst, send_sem=send, recv_sem=recv,
                                        device_id=device, device_id_type=MESH)


def neighbours():
    tile, diag = lax.axis_index("tiles"), lax.axis_index("diag")
    tiles, diags = lax.axis_size("tiles"), lax.axis_size("diag")
    up, down = lax.rem(tile + tiles - 1, tiles), lax.rem(tile + 1, tiles)
    lo, hi = lax.rem(diag + diags - 1, diags), lax.rem(diag + 1, diags)
    return [(tile, lo), (tile, hi), (up, diag), (down, diag), (up, lo), (up, hi), (down, lo), (down, hi)]


def halo_copies(near, field, first, last, left, right, top, bot, send, recv):
    inner = pl.ds(1, GROUPS)
    plan = [
        (field.at[pl.ds(EDGE, EDGE)], right),
        (field.at[pl.ds(COLS, EDGE)], left),
        (first, bot.at[inner]),
        (last, top.at[inner]),
        (first.at[0], bot.at[GROUPS + 1]),
        (first.at[GROUPS - 1], bot.at[0]),
        (last.at[0], top.at[GROUPS + 1]),
        (last.at[GROUPS - 1], top.at[0]),
    ]
    return [remote(src, dst, send.at[n], recv.at[n], near[n]) for n, (src, dst) in enumerate(plan)]


def unpack(scale, done, conv_ref, mix_ref):
    rows = jnp.concatenate([done[n] for n in range(done.shape[0])], axis=0) * scale
    both = jnp.concatenate([rows[n * CH:(n + 1) * CH] for n in range(KPAD // ROWS)], axis=1)
    for s in range(TAPS):
        conv_ref[s] = both[:, s * CH:(s + 1) * CH]
    mix_ref[...] = both[:, TAPS * CH:(TAPS + 1) * CH]


def everything(inner, scale, counts_in, reach_in, dilation_in, x_hbm, g_hbm, conv_in, mix_in, out_ref, conv_ref, mix_ref,
               counts, reach, dilation, conv, mix,
               x_ref, g_ref, field, masked, grad_pre, hidden, moved, held, spread, acc, forward, backward,
               first1, last1, left1, right1, top1, bot1, first2, last2, left2, right2, top2, bot2,
               part, parts_in, far, done, load, send1, recv1, send2, recv2, send3, recv3, send4, recv4, send5, recv5):
    tile, diag = lax.axis_index("tiles"), lax.axis_index("diag")
    tiles, diags = lax.axis_size("tiles"), lax.axis_size("diag")
    pairs = [(counts_in, counts), (reach_in, reach), (dilation_in, dilation), (conv_in, conv), (mix_in, mix)]
    small = [pltpu.make_async_copy(src, dst, load.at[2 * LOADS + n]) for n, (src, dst) in enumerate(pairs)]
    parts = [pl.ds(n * (CH // LOADS), CH // LOADS) for n in range(LOADS)]
    x_loads = [pltpu.make_async_copy(x_hbm.at[at], x_ref.at[at], load.at[n]) for n, at in enumerate(parts)]
    g_loads = [pltpu.make_async_copy(g_hbm.at[at], g_ref.at[at], load.at[LOADS + n]) for n, at in enumerate(parts)]
    for copy in small + x_loads:
        copy.start()

    shares = (tiles // inner) * diags
    outer, other = lax.div(tile, inner), lax.rem(tile, inner)
    rank = outer * diags + diag
    friends = [lax.rem(rank + step, shares) for step in range(1, shares)]
    friend_ids = [(lax.div(to, diags) * inner + other, lax.rem(to, diags)) for to in friends]
    cousin_ids = [(outer * inner + lax.rem(other + step, inner), diag) for step in range(1, inner)]
    near = neighbours()
    barrier = pltpu.get_barrier_semaphore()
    for device in near + friend_ids + cousin_ids:
        pl.semaphore_signal(barrier, inc=1, device_id=device, device_id_type=MESH)

    for copy in g_loads:
        copy.start()
    for copy in small:
        copy.wait()
    par = [counts[0] * (ROWS // 4)] + [reach[n] for n in range(4)] + [dilation[0], dilation[1]]
    par += [tile, diag, tiles - 1, diags - 1]
    place_weights(conv, mix, forward, backward)
    keep = jnp.where(kept_cells(par), 1.0, 0.0).astype(BF)

    def put_field(k, value):
        field[EDGE + k] = value

    def put_masked(k, value):
        masked[k] = value

    turn_field(x_loads, lambda c: jnp.maximum(x_ref[c], jnp.zeros((), BF)) * keep, held, put_field)
    pl.semaphore_wait(barrier, len(near) + len(friend_ids) + len(cousin_ids))
    halo1 = halo_copies(near, field, first1, last1, left1, right1, top1, bot1, send1, recv1)
    pack_edges(par, field, first1, last1)
    for copy in halo1[2:] + halo1[:2]:
        copy.start()
    turn_field(g_loads, lambda c: g_ref[c] * keep, held, put_masked)
    inside = range(1, GROUPS + 1)
    for copy in halo1[2:4]:
        copy.wait_recv()
    shift_rows(par, inside, field, top1, bot1, moved)
    halo2 = halo_copies(near, grad_pre, first2, last2, left2, right2, top2, bot2, send2, recv2)
    ends = EDGE // STEP
    middle = COLS // STEP - 2 * ends
    conv_forward(par, (middle, lambda at: at + ends), field, moved, masked, forward, grad_pre, hidden)
    for copy in halo1[:2] + halo1[4:]:
        copy.wait_recv()
    set_edges(par, left1, right1, field)
    shift_rows(par, [0, GROUPS + 1], field, top1, bot1, moved)
    conv_forward(par, (2 * ends, lambda at: at + (at // ends) * middle), field, moved, masked, forward, grad_pre, hidden)
    halo2[0].start()
    halo2[1].start()
    pack_edges(par, grad_pre, first2, last2)
    for copy in halo2[2:]:
        copy.start()
    kernel_grads(par, field, moved, masked, grad_pre, hidden, acc)
    share_out(acc, part)
    sum1 = [remote(part.at[to], parts_in.at[rank], send3, recv3, friend_ids[n]) for n, to in enumerate(friends)]
    sum2 = [remote(far.at[other], far.at[other], send4, recv4, to) for to in cousin_ids]
    sum3 = [remote(done.at[rank], done.at[rank], send5, recv5, to) for to in friend_ids]
    all1, all2, all3 = [
        remote(slots.at[pl.ds(0, slots.shape[0] - 1)], slots.at[pl.ds(0, slots.shape[0] - 1)], send, recv, near[0])
        for slots, send, recv in ((parts_in, send3, recv3), (far, send4, recv4), (done, send5, recv5))]
    for copy in sum1:
        copy.start()
    parts_in[rank] = part[rank]

    for copy in halo2:
        copy.wait_recv()
    set_edges(par, left2, right2, grad_pre)
    shift_rows(par, range(GROUPS + 2), grad_pre, top2, bot2, moved)
    all1.wait_recv()
    far[other] = jnp.sum(parts_in[...], axis=0)
    for copy in sum2:
        copy.start()
    blocks = COLS // STEP
    early = blocks * 3 // 4
    conv_back(par, 0, early, grad_pre, moved, backward, spread)
    all2.wait_recv()
    done[rank] = jnp.sum(far[...], axis=0)
    for copy in sum3:
        copy.start()
    conv_back(par, early, blocks - early, grad_pre, moved, backward, spread)
    finish(par, x_ref, g_ref, spread, out_ref)
    all3.wait_recv()
    unpack(scale, done, conv_ref, mix_ref)
    for copy in halo1 + halo2 + [all1, all2, all3]:
        copy.wait_send()


def move_out(field, conv, mix, field_out, conv_out, mix_out, sems):
    size = CH // MOVES
    pieces = [(field.at[pl.ds(n * size, size)], field_out.at[pl.ds(n * size, size)]) for n in range(MOVES)]
    copies = [pltpu.make_async_copy(src, dst, sems.at[n])
              for n, (src, dst) in enumerate([(conv, conv_out), (mix, mix_out)] + pieces)]
    for copy in copies:
        copy.start()
    for copy in copies:
        copy.wait()


def specs(space, count):
    return [pl.BlockSpec(memory_space=space)] * count


def body(inputs, cotangent, conv_weight, mix_weight, counts, band_reach, dilation):
    shape = jax.ShapeDtypeStruct
    tiles, diags = lax.axis_size("tiles"), lax.axis_size("diag")
    inner = 16 if tiles == 64 else 2
    shares = (tiles // inner) * diags
    dma = lambda n: pltpu.SemaphoreType.DMA((n,))
    whole = pltpu.VMEM((CH, ROWS, COLS), BF)
    field = pltpu.VMEM((COLS, CH, ROWS), BF)
    pack = pltpu.VMEM((GROUPS, CH, ROWS), BF)
    wide = pltpu.VMEM((COLS + 2 * EDGE, CH, ROWS), BF)
    side = pltpu.VMEM((EDGE, CH, ROWS), BF)
    ends = pltpu.VMEM((GROUPS + 2, CH, ROWS), BF)
    slots = lambda n: pltpu.VMEM((n, CH * KPAD // ROWS // shares, ROWS), F32)
    halo = [pack, pack, side, side, ends, ends]
    cells = TPD * tiles * (ROWS // 4) * COLS * diags
    results = pl.pallas_call(
        functools.partial(everything, inner, 1.0 / math.sqrt(cells)),
        out_shape=[pltpu.VMEM((CH, ROWS, COLS), BF), pltpu.VMEM((TAPS, CH, CH), F32), pltpu.VMEM((CH, CH), F32)],
        in_specs=specs(pltpu.HBM, 7),
        out_specs=specs(pltpu.VMEM, 3),
        scratch_shapes=[
            pltpu.SMEM(counts.shape, jnp.int32), pltpu.SMEM(band_reach.shape, jnp.int32), pltpu.SMEM(dilation.shape, jnp.int32),
            pltpu.VMEM(conv_weight.shape, BF), pltpu.VMEM(mix_weight.shape, BF),
            whole, whole, wide, field, wide, field,
            pltpu.VMEM((2, COLS + 2 * EDGE, CH, ROWS), BF),
            pltpu.VMEM(((COLS + 1) * TURN, ROWS), F32),
            pltpu.VMEM(((CH + 1) * BACK, ROWS), F32),
            pltpu.VMEM(((TAPS + 1) * CH, ROWS), F32),
            pltpu.VMEM((2 * CH, KPAD), BF),
            pltpu.VMEM((CH, KPAD), BF),
            *halo, *halo,
            slots(shares), slots(shares), slots(inner), slots(shares),
            dma(2 * LOADS + 5), dma(8), dma(8), dma(8), dma(8),
            *[pltpu.SemaphoreType.DMA] * 6,
        ],
        cost_estimate=pl.CostEstimate(flops=6 * CH * CH * TAPS * ROWS * COLS, bytes_accessed=3 * 2 * CH * ROWS * COLS,
                                      transcendentals=0),
        compiler_params=pltpu.CompilerParams(collective_id=0, has_side_effects=True, vmem_limit_bytes=VMEM_LIMIT),
    )(counts, band_reach, dilation, inputs, cotangent, conv_weight, mix_weight)
    return pl.pallas_call(
        move_out,
        out_shape=[shape(r.shape, r.dtype) for r in results],
        in_specs=specs(pltpu.VMEM, 3),
        out_specs=specs(pltpu.HBM, 3),
        scratch_shapes=[dma(MOVES + 2)],
        compiler_params=pltpu.CompilerParams(vmem_limit_bytes=8 * 1024 * 1024),
    )(*results)


def solution(mesh):
    in_specs = (
        P(None, "tiles", "diag"),
        P(None, "tiles", "diag"),
        P(),
        P(),
        P("tiles"),
        P("tiles"),
        P(),
    )
    out_specs = (P(None, "tiles", "diag"), P(), P())
    return jax.shard_map(body, mesh=mesh, in_specs=in_specs, out_specs=out_specs, check_vma=False)
```

```python
import functools
import math

import jax
import jax.numpy as jnp
from jax import lax
from jax.experimental import pallas as pl
from jax.experimental.pallas import tpu as pltpu
from jax.sharding import PartitionSpec as P

MESH = pl.DeviceIdType.MESH
TPD = 2
DMAX = 8
CH = 48
ROWS = 128
COLS = 128
EDGE = 2 * DMAX
GROUPS = COLS // EDGE
STEP = 8
TAPS = 9
KPAD = 512
VMEM_LIMIT = 56 * 1024 * 1024
BF = jnp.bfloat16
F32 = jnp.float32
LIVE, REACH, DIL, TILE, DIAG, LAST_TILE, LAST_DIAG = 0, 1, 5, 7, 8, 9, 10
TURN = 56
BACK = 136
LOADS = 3
MOVES = 4


def iota(shape, dim):
    return lax.broadcasted_iota(jnp.int32, shape, dim)


def reach_of(par, ids):
    reach = jnp.where(ids < 64, jnp.where(ids < 32, par[REACH], par[REACH + 1]),
                      jnp.where(ids < 96, par[REACH + 2], par[REACH + 3]))
    return jnp.where(ids < par[LIVE], reach, 0)


def tap_moves(par):
    moves = []
    for a in range(3):
        for b in range(3):
            row = (a - 1) * par[DIL]
            moves.append((a, (b - 1) * par[DIL + 1] - row))
    return moves


def pack_edges(par, field, first, last):
    lane = iota((1, 2 * ROWS), 1)
    near = lane % DMAX
    want = jnp.where(lane < ROWS, near, par[LIVE] - DMAX + near)
    place = jnp.where(lane < ROWS, (lane // DMAX + EDGE // 2) % EDGE, (lane - ROWS) // DMAX)
    hit = jnp.where(iota((ROWS, 2 * ROWS), 0) == want, 1.0, 0.0)
    weight = jnp.concatenate([jnp.where(place == kk, hit, 0.0).astype(BF) for kk in range(EDGE)], axis=0)
    lhs = jnp.concatenate(
        [jnp.concatenate([field[(g + 1) * EDGE + kk] for g in range(GROUPS)], axis=0) for kk in range(EDGE)], axis=1)
    out = jnp.dot(lhs, weight, preferred_element_type=F32).astype(BF)
    for g in range(GROUPS):
        first[g] = out[g * CH:(g + 1) * CH, :ROWS]
        last[g] = out[g * CH:(g + 1) * CH, ROWS:]


def set_edges(par, left, right, field):
    for e in range(EDGE):
        low, high = left[e], right[e]
        field[e] = jnp.where(par[DIAG] > 0, low, jnp.zeros_like(low))
        field[EDGE + COLS + e] = jnp.where(par[DIAG] < par[LAST_DIAG], high, jnp.zeros_like(high))


def shift_rows(par, groups, field, top, bot, moved):
    half = ROWS // 2
    lane = iota((1, 2 * ROWS), 1)
    move = jnp.where(lane < ROWS, -par[DIL], par[DIL])
    want = (lane % ROWS) + move
    rows = iota((ROWS, 2 * ROWS), 0)
    inner = jnp.where(rows == want, 1.0, 0.0).astype(BF)
    has_top = par[TILE] > 0
    has_bot = par[TILE] < par[LAST_TILE]
    top_want = jnp.where((want < 0) & has_top, want + DMAX, -1)
    low = want - par[LIVE]
    bot_want = jnp.where((low >= 0) & (low < DMAX) & has_bot, low, -1)
    wants = [jnp.where(rows < half, top_want, bot_want), jnp.where(rows < half, bot_want, top_want)]
    outers = [jnp.where(rows % DMAX == w, 1.0, 0.0) for w in wants]
    place = (rows % half) // DMAX
    has_left = par[DIAG] > 0
    has_right = par[DIAG] < par[LAST_DIAG]
    tops = jnp.concatenate([top[g] for g in groups], axis=0)
    bots = jnp.concatenate([bot[g] for g in groups], axis=0)
    upper = iota(tops.shape, 1) < half
    halos = [jnp.where(upper, tops, bots), jnp.where(upper, bots, tops)]

    for part in range(2):
        def column(at, carry):
            kk = at + part * (EDGE // 2)
            weight = jnp.concatenate([inner, jnp.where(place == at, outers[part], 0.0).astype(BF)], axis=0)
            tiles = [field[g * EDGE + kk] for g in groups]
            lhs = jnp.concatenate([jnp.concatenate(tiles, axis=0), halos[part]], axis=1)
            out = jnp.dot(lhs, weight, preferred_element_type=F32)
            for n, g in enumerate(groups):
                piece = out[n * CH:(n + 1) * CH]
                if g == 0:
                    piece = jnp.where(has_left, piece, 0.0)
                if g == GROUPS + 1:
                    piece = jnp.where(has_right, piece, 0.0)
                piece = piece.astype(BF)
                moved[0, g * EDGE + kk] = piece[:, :ROWS]
                moved[1, g * EDGE + kk] = piece[:, ROWS:]
            return carry

        lax.fori_loop(0, EDGE // 2, column, 0, unroll=4)


def tapped(field, moved, a, k):
    return field[EDGE + k] if a == 1 else moved[a // 2, EDGE + k]


def pair(refs):
    return jnp.concatenate(refs, axis=1)


def eye():
    return jnp.where(iota((ROWS, ROWS), 0) == iota((ROWS, ROWS), 1), 1.0, 0.0).astype(BF)


def turn(one, value):
    return lax.dot_general(one, value, (((1,), (1,)), ((), ())), preferred_element_type=F32)


def turn_field(loads, value, held, put):
    one = eye()
    size = CH // len(loads)

    def channels(step, carry):
        c = step * 4
        out = turn(one, jnp.concatenate([value(c + n) for n in range(4)], axis=0))
        for n in range(4):
            held[pl.ds(c + n, COLS, stride=TURN), :] = out[:, n * ROWS:(n + 1) * ROWS]
        return carry

    for n, load in enumerate(loads):
        load.wait()
        lax.fori_loop(n * size // 4, (n + 1) * size // 4, channels, 0, unroll=size // 4)

    def column(k, carry):
        put(k, held[pl.ds(pl.multiple_of(k * TURN, 8), CH), :].astype(BF))
        return carry

    lax.fori_loop(0, COLS, column, 0, unroll=16)


def kept_cells(par):
    shape = (ROWS, COLS)
    return iota(shape, 1) + par[DIAG] * COLS < reach_of(par, iota(shape, 0))


def conv_forward(par, blocks, field, moved, masked, weight, grad_pre, hidden):
    moves = tap_moves(par)
    used = (TAPS + 1) * CH
    pad = jnp.zeros((KPAD - used, 2 * ROWS), BF)
    count, number = blocks

    def block(at, carry):
        for j in range(0, STEP, 2):
            k = number(at) * STEP + j
            tiles = [pair([tapped(field, moved, a, k + n + shift) for n in range(2)]) for a, shift in moves]
            tiles += [pair([masked[k], masked[k + 1]]), pad]
            out = jnp.dot(weight[...], jnp.concatenate(tiles, axis=0), preferred_element_type=F32)
            pre, back = out[:CH], out[CH:]
            grad = jnp.where(pre > 0, back, 0.0).astype(BF)
            act = jnp.maximum(pre, 0.0).astype(BF)
            for n in range(2):
                grad_pre[EDGE + k + n] = grad[:, n * ROWS:(n + 1) * ROWS]
                hidden[k + n] = act[:, n * ROWS:(n + 1) * ROWS]
        return carry

    lax.fori_loop(0, count, block, 0, unroll=4)


def kernel_grads(par, field, moved, masked, grad_pre, hidden, acc):
    moves = tap_moves(par)
    acc[...] = jnp.zeros_like(acc)
    pad = jnp.zeros((KPAD - (TAPS + 1) * CH, STEP * ROWS), BF)

    def block(blk, carry):
        ks = [blk * STEP + j for j in range(STEP)]
        tiles = [pair([tapped(field, moved, a, k + shift) for k in ks]) for a, shift in moves]
        rhs = jnp.concatenate(tiles + [pair([hidden[k] for k in ks]), pad], axis=0)
        lhs = jnp.concatenate([pair([grad_pre[EDGE + k] for k in ks]), pair([masked[k] for k in ks])], axis=0)
        acc[...] += lax.dot_general(lhs, rhs, (((1,), (1,)), ((), ())), preferred_element_type=F32)
        return carry

    lax.fori_loop(0, COLS // STEP, block, 0, unroll=2)


def share_out(acc, part):
    both = jnp.where(iota((CH, KPAD), 1) < TAPS * CH, acc[:CH], acc[CH:])
    rows = jnp.concatenate([both[:, n * ROWS:(n + 1) * ROWS] for n in range(KPAD // ROWS)], axis=0)
    size = part.shape[1]
    for n in range(part.shape[0]):
        part[n] = rows[n * size:(n + 1) * size]


def place_weights(conv, mix, forward, backward):
    shape = (CH, KPAD)
    gap = iota(shape, 1) - iota(shape, 0)
    taps = jnp.zeros(shape, F32)
    back = jnp.zeros(shape, F32)
    for s in range(TAPS):
        put = jnp.where(gap == s * CH, 1.0, 0.0).astype(BF)
        taps += jnp.dot(conv[s], put, preferred_element_type=F32)
        back += lax.dot_general(conv[s], put, (((0,), (0,)), ((), ())), preferred_element_type=F32)
    put = jnp.where(gap == TAPS * CH, 1.0, 0.0).astype(BF)
    mixed = lax.dot_general(mix[...], put, (((0,), (0,)), ((), ())), preferred_element_type=F32)
    forward[...] = jnp.concatenate([taps, mixed], axis=0).astype(BF)
    backward[...] = back.astype(BF)


def conv_back(par, first, count, field, moved, weight, spread):
    moves = tap_moves(par)
    pad = jnp.zeros((KPAD - TAPS * CH, 2 * ROWS), BF)

    def block(blk, carry):
        for j in range(0, STEP, 2):
            k = blk * STEP + j
            tiles = [pair([tapped(field, moved, 2 - a, k + n - shift) for n in range(2)]) for a, shift in moves]
            out = jnp.dot(weight[...], jnp.concatenate(tiles + [pad], axis=0), preferred_element_type=F32)
            for n in range(2):
                spread[pl.ds(k + n, CH, stride=BACK), :] = out[:, n * ROWS:(n + 1) * ROWS]
        return carry

    lax.fori_loop(first, first + count, block, 0, unroll=4)


def finish(par, x_ref, g_ref, spread, out_ref):
    keep = jnp.where(kept_cells(par), 1.0, 0.0).astype(BF)
    live = jnp.where(iota((ROWS, COLS), 0) < par[LIVE], 1.0, 0.0).astype(BF)
    one = eye()
    zero = jnp.zeros((ROWS, COLS), BF)

    def channels(step, carry):
        c = step * 4
        parts = [spread[pl.ds(pl.multiple_of((c + n) * BACK, 8), COLS), :].astype(BF) for n in range(4)]
        out = turn(one, jnp.concatenate(parts, axis=0)).astype(BF)
        for n in range(4):
            part = jnp.where(x_ref[c + n] > zero, out[:, n * ROWS:(n + 1) * ROWS], zero)
            out_ref[c + n] = (g_ref[c + n] + part * keep) * live
        return carry

    lax.fori_loop(0, CH // 4, channels, 0, unroll=4)


def remote(src, dst, send, recv, device):
    return pltpu.make_async_remote_copy(src_ref=src, dst_ref=dst, send_sem=send, recv_sem=recv,
                                        device_id=device, device_id_type=MESH)


def neighbours():
    tile, diag = lax.axis_index("tiles"), lax.axis_index("diag")
    tiles, diags = lax.axis_size("tiles"), lax.axis_size("diag")
    up, down = lax.rem(tile + tiles - 1, tiles), lax.rem(tile + 1, tiles)
    lo, hi = lax.rem(diag + diags - 1, diags), lax.rem(diag + 1, diags)
    return [(tile, lo), (tile, hi), (up, diag), (down, diag), (up, lo), (up, hi), (down, lo), (down, hi)]


def halo_copies(near, field, first, last, left, right, top, bot, send, recv):
    inner = pl.ds(1, GROUPS)
    plan = [
        (field.at[pl.ds(EDGE, EDGE)], right),
        (field.at[pl.ds(COLS, EDGE)], left),
        (first, bot.at[inner]),
        (last, top.at[inner]),
        (first.at[0], bot.at[GROUPS + 1]),
        (first.at[GROUPS - 1], bot.at[0]),
        (last.at[0], top.at[GROUPS + 1]),
        (last.at[GROUPS - 1], top.at[0]),
    ]
    return [remote(src, dst, send.at[n], recv.at[n], near[n]) for n, (src, dst) in enumerate(plan)]


def unpack(scale, done, conv_ref, mix_ref):
    rows = jnp.concatenate([done[n] for n in range(done.shape[0])], axis=0) * scale
    both = jnp.concatenate([rows[n * CH:(n + 1) * CH] for n in range(KPAD // ROWS)], axis=1)
    for s in range(TAPS):
        conv_ref[s] = both[:, s * CH:(s + 1) * CH]
    mix_ref[...] = both[:, TAPS * CH:(TAPS + 1) * CH]


def everything(inner, scale, counts_in, reach_in, dilation_in, x_hbm, g_hbm, conv_in, mix_in, out_ref, conv_ref, mix_ref,
               counts, reach, dilation, conv, mix,
               x_ref, g_ref, field, masked, grad_pre, hidden, moved, held, spread, acc, forward, backward,
               first1, last1, left1, right1, top1, bot1, first2, last2, left2, right2, top2, bot2,
               part, parts_in, far, done, load, send1, recv1, send2, recv2, send3, recv3, send4, recv4, send5, recv5):
    tile, diag = lax.axis_index("tiles"), lax.axis_index("diag")
    tiles, diags = lax.axis_size("tiles"), lax.axis_size("diag")
    pairs = [(counts_in, counts), (reach_in, reach), (dilation_in, dilation), (conv_in, conv), (mix_in, mix)]
    small = [pltpu.make_async_copy(src, dst, load.at[2 * LOADS + n]) for n, (src, dst) in enumerate(pairs)]
    parts = [pl.ds(n * (CH // LOADS), CH // LOADS) for n in range(LOADS)]
    x_loads = [pltpu.make_async_copy(x_hbm.at[at], x_ref.at[at], load.at[n]) for n, at in enumerate(parts)]
    g_loads = [pltpu.make_async_copy(g_hbm.at[at], g_ref.at[at], load.at[LOADS + n]) for n, at in enumerate(parts)]
    for copy in small + x_loads:
        copy.start()

    shares = (tiles // inner) * diags
    outer, other = lax.div(tile, inner), lax.rem(tile, inner)
    rank = outer * diags + diag
    friends = [lax.rem(rank + step, shares) for step in range(1, shares)]
    friend_ids = [(lax.div(to, diags) * inner + other, lax.rem(to, diags)) for to in friends]
    cousin_ids = [(outer * inner + lax.rem(other + step, inner), diag) for step in range(1, inner)]
    near = neighbours()
    barrier = pltpu.get_barrier_semaphore()
    for device in near + friend_ids + cousin_ids:
        pl.semaphore_signal(barrier, inc=1, device_id=device, device_id_type=MESH)

    for copy in g_loads:
        copy.start()
    for copy in small:
        copy.wait()
    par = [counts[0] * (ROWS // 4)] + [reach[n] for n in range(4)] + [dilation[0], dilation[1]]
    par += [tile, diag, tiles - 1, diags - 1]
    place_weights(conv, mix, forward, backward)
    keep = jnp.where(kept_cells(par), 1.0, 0.0).astype(BF)

    def put_field(k, value):
        field[EDGE + k] = value

    def put_masked(k, value):
        masked[k] = value

    turn_field(x_loads, lambda c: jnp.maximum(x_ref[c], jnp.zeros((), BF)) * keep, held, put_field)
    pl.semaphore_wait(barrier, len(near) + len(friend_ids) + len(cousin_ids))
    halo1 = halo_copies(near, field, first1, last1, left1, right1, top1, bot1, send1, recv1)
    pack_edges(par, field, first1, last1)
    for copy in halo1[2:] + halo1[:2]:
        copy.start()
    turn_field(g_loads, lambda c: g_ref[c] * keep, held, put_masked)
    inside = range(1, GROUPS + 1)
    for copy in halo1[2:4]:
        copy.wait_recv()
    shift_rows(par, inside, field, top1, bot1, moved)
    halo2 = halo_copies(near, grad_pre, first2, last2, left2, right2, top2, bot2, send2, recv2)
    ends = EDGE // STEP
    middle = COLS // STEP - 2 * ends
    conv_forward(par, (middle, lambda at: at + ends), field, moved, masked, forward, grad_pre, hidden)
    for copy in halo1[:2] + halo1[4:]:
        copy.wait_recv()
    set_edges(par, left1, right1, field)
    shift_rows(par, [0, GROUPS + 1], field, top1, bot1, moved)
    conv_forward(par, (2 * ends, lambda at: at + (at // ends) * middle), field, moved, masked, forward, grad_pre, hidden)
    halo2[0].start()
    halo2[1].start()
    pack_edges(par, grad_pre, first2, last2)
    for copy in halo2[2:]:
        copy.start()
    kernel_grads(par, field, moved, masked, grad_pre, hidden, acc)
    share_out(acc, part)
    sum1 = [remote(part.at[to], parts_in.at[rank], send3, recv3, friend_ids[n]) for n, to in enumerate(friends)]
    sum2 = [remote(far.at[other], far.at[other], send4, recv4, to) for to in cousin_ids]
    sum3 = [remote(done.at[rank], done.at[rank], send5, recv5, to) for to in friend_ids]
    all1, all2, all3 = [
        remote(slots.at[pl.ds(0, slots.shape[0] - 1)], slots.at[pl.ds(0, slots.shape[0] - 1)], send, recv, near[0])
        for slots, send, recv in ((parts_in, send3, recv3), (far, send4, recv4), (done, send5, recv5))]
    for copy in sum1:
        copy.start()
    parts_in[rank] = part[rank]

    for copy in halo2:
        copy.wait_recv()
    set_edges(par, left2, right2, grad_pre)
    shift_rows(par, range(GROUPS + 2), grad_pre, top2, bot2, moved)
    all1.wait_recv()
    far[other] = jnp.sum(parts_in[...], axis=0)
    for copy in sum2:
        copy.start()
    blocks = COLS // STEP
    early = blocks * 3 // 4
    conv_back(par, 0, early, grad_pre, moved, backward, spread)
    all2.wait_recv()
    done[rank] = jnp.sum(far[...], axis=0)
    for copy in sum3:
        copy.start()
    conv_back(par, early, blocks - early, grad_pre, moved, backward, spread)
    finish(par, x_ref, g_ref, spread, out_ref)
    all3.wait_recv()
    unpack(scale, done, conv_ref, mix_ref)
    for copy in halo1 + halo2 + [all1, all2, all3]:
        copy.wait_send()


def move_out(field, conv, mix, field_out, conv_out, mix_out, sems):
    size = CH // MOVES
    pieces = [(field.at[pl.ds(n * size, size)], field_out.at[pl.ds(n * size, size)]) for n in range(MOVES)]
    copies = [pltpu.make_async_copy(src, dst, sems.at[n])
              for n, (src, dst) in enumerate([(conv, conv_out), (mix, mix_out)] + pieces)]
    for copy in copies:
        copy.start()
    for copy in copies:
        copy.wait()


def specs(space, count):
    return [pl.BlockSpec(memory_space=space)] * count


def body(inputs, cotangent, conv_weight, mix_weight, counts, band_reach, dilation):
    shape = jax.ShapeDtypeStruct
    tiles, diags = lax.axis_size("tiles"), lax.axis_size("diag")
    inner = 16 if tiles == 64 else 2
    shares = (tiles // inner) * diags
    dma = lambda n: pltpu.SemaphoreType.DMA((n,))
    whole = pltpu.VMEM((CH, ROWS, COLS), BF)
    field = pltpu.VMEM((COLS, CH, ROWS), BF)
    pack = pltpu.VMEM((GROUPS, CH, ROWS), BF)
    wide = pltpu.VMEM((COLS + 2 * EDGE, CH, ROWS), BF)
    side = pltpu.VMEM((EDGE, CH, ROWS), BF)
    ends = pltpu.VMEM((GROUPS + 2, CH, ROWS), BF)
    slots = lambda n: pltpu.VMEM((n, CH * KPAD // ROWS // shares, ROWS), F32)
    halo = [pack, pack, side, side, ends, ends]
    cells = TPD * tiles * (ROWS // 4) * COLS * diags
    results = pl.pallas_call(
        functools.partial(everything, inner, 1.0 / math.sqrt(cells)),
        out_shape=[pltpu.VMEM((CH, ROWS, COLS), BF), pltpu.VMEM((TAPS, CH, CH), F32), pltpu.VMEM((CH, CH), F32)],
        in_specs=specs(pltpu.HBM, 7),
        out_specs=specs(pltpu.VMEM, 3),
        scratch_shapes=[
            pltpu.SMEM(counts.shape, jnp.int32), pltpu.SMEM(band_reach.shape, jnp.int32), pltpu.SMEM(dilation.shape, jnp.int32),
            pltpu.VMEM(conv_weight.shape, BF), pltpu.VMEM(mix_weight.shape, BF),
            whole, whole, wide, field, wide, field,
            pltpu.VMEM((2, COLS + 2 * EDGE, CH, ROWS), BF),
            pltpu.VMEM(((COLS + 1) * TURN, ROWS), F32),
            pltpu.VMEM(((CH + 1) * BACK, ROWS), F32),
            pltpu.VMEM((2 * CH, KPAD), F32),
            pltpu.VMEM((2 * CH, KPAD), BF),
            pltpu.VMEM((CH, KPAD), BF),
            *halo, *halo,
            slots(shares), slots(shares), slots(inner), slots(shares),
            dma(2 * LOADS + 5), dma(8), dma(8), dma(8), dma(8),
            *[pltpu.SemaphoreType.DMA] * 6,
        ],
        cost_estimate=pl.CostEstimate(flops=6 * CH * CH * TAPS * ROWS * COLS, bytes_accessed=3 * 2 * CH * ROWS * COLS,
                                      transcendentals=0),
        compiler_params=pltpu.CompilerParams(collective_id=0, has_side_effects=True, vmem_limit_bytes=VMEM_LIMIT),
    )(counts, band_reach, dilation, inputs, cotangent, conv_weight, mix_weight)
    return pl.pallas_call(
        move_out,
        out_shape=[shape(r.shape, r.dtype) for r in results],
        in_specs=specs(pltpu.VMEM, 3),
        out_specs=specs(pltpu.HBM, 3),
        scratch_shapes=[dma(MOVES + 2)],
        compiler_params=pltpu.CompilerParams(vmem_limit_bytes=8 * 1024 * 1024),
    )(*results)


def solution(mesh):
    in_specs = (
        P(None, "tiles", "diag"),
        P(None, "tiles", "diag"),
        P(),
        P(),
        P("tiles"),
        P("tiles"),
        P(),
    )
    out_specs = (P(None, "tiles", "diag"), P(), P())
    return jax.shard_map(body, mesh=mesh, in_specs=in_specs, out_specs=out_specs, check_vma=False)
```

```python
import functools
import math

import jax
import jax.numpy as jnp
from jax import lax
from jax.experimental import pallas as pl
from jax.experimental.pallas import tpu as pltpu
from jax.sharding import PartitionSpec as P

MESH = pl.DeviceIdType.MESH
TPD = 2
DMAX = 8
CH = 48
ROWS = 128
COLS = 128
EDGE = 2 * DMAX
GROUPS = COLS // EDGE
STEP = 8
TAPS = 9
SUM_ROWS = 192
VMEM_LIMIT = 56 * 1024 * 1024
BF = jnp.bfloat16
F32 = jnp.float32
LIVE, REACH, DIL, TILE, DIAG, LAST_TILE, LAST_DIAG = 0, 1, 5, 7, 8, 9, 10
TURN = 56
BACK = 136
LOADS = 3
MOVES = 4


def iota(shape, dim):
    return lax.broadcasted_iota(jnp.int32, shape, dim)


def reach_of(par, ids):
    reach = jnp.where(ids < 64, jnp.where(ids < 32, par[REACH], par[REACH + 1]),
                      jnp.where(ids < 96, par[REACH + 2], par[REACH + 3]))
    return jnp.where(ids < par[LIVE], reach, 0)


def pack_edges(par, field, first, last):
    lane = iota((1, 2 * ROWS), 1)
    near = lane % DMAX
    want = jnp.where(lane < ROWS, near, par[LIVE] - DMAX + near)
    place = jnp.where(lane < ROWS, (lane // DMAX + EDGE // 2) % EDGE, (lane - ROWS) // DMAX)
    hit = jnp.where(iota((ROWS, 2 * ROWS), 0) == want, 1.0, 0.0)
    weight = jnp.concatenate([jnp.where(place == kk, hit, 0.0).astype(BF) for kk in range(EDGE)], axis=0)
    lhs = jnp.concatenate(
        [jnp.concatenate([field[(g + 1) * EDGE + kk] for g in range(GROUPS)], axis=0) for kk in range(EDGE)], axis=1)
    out = jnp.dot(lhs, weight, preferred_element_type=F32).astype(BF)
    for g in range(GROUPS):
        first[g] = out[g * CH:(g + 1) * CH, :ROWS]
        last[g] = out[g * CH:(g + 1) * CH, ROWS:]


def set_edges(par, left, right, field):
    for e in range(EDGE):
        low, high = left[e], right[e]
        field[e] = jnp.where(par[DIAG] > 0, low, jnp.zeros_like(low))
        field[EDGE + COLS + e] = jnp.where(par[DIAG] < par[LAST_DIAG], high, jnp.zeros_like(high))


def shift_rows(par, groups, field, top, bot, moved):
    half = ROWS // 2
    lane = iota((1, 2 * ROWS), 1)
    move = jnp.where(lane < ROWS, -par[DIL], par[DIL])
    want = (lane % ROWS) + move
    rows = iota((ROWS, 2 * ROWS), 0)
    inner = jnp.where(rows == want, 1.0, 0.0).astype(BF)
    has_top = par[TILE] > 0
    has_bot = par[TILE] < par[LAST_TILE]
    top_want = jnp.where((want < 0) & has_top, want + DMAX, -1)
    low = want - par[LIVE]
    bot_want = jnp.where((low >= 0) & (low < DMAX) & has_bot, low, -1)
    wants = [jnp.where(rows < half, top_want, bot_want), jnp.where(rows < half, bot_want, top_want)]
    outers = [jnp.where(rows % DMAX == w, 1.0, 0.0) for w in wants]
    place = (rows % half) // DMAX
    has_left = par[DIAG] > 0
    has_right = par[DIAG] < par[LAST_DIAG]
    tops = jnp.concatenate([top[g] for g in groups], axis=0)
    bots = jnp.concatenate([bot[g] for g in groups], axis=0)
    upper = iota(tops.shape, 1) < half
    halos = [jnp.where(upper, tops, bots), jnp.where(upper, bots, tops)]

    for part in range(2):
        def column(at, carry):
            kk = at + part * (EDGE // 2)
            weight = jnp.concatenate([inner, jnp.where(place == at, outers[part], 0.0).astype(BF)], axis=0)
            tiles = [field[g * EDGE + kk] for g in groups]
            lhs = jnp.concatenate([jnp.concatenate(tiles, axis=0), halos[part]], axis=1)
            out = jnp.dot(lhs, weight, preferred_element_type=F32)
            for n, g in enumerate(groups):
                piece = out[n * CH:(n + 1) * CH]
                if g == 0:
                    piece = jnp.where(has_left, piece, 0.0)
                if g == GROUPS + 1:
                    piece = jnp.where(has_right, piece, 0.0)
                piece = piece.astype(BF)
                moved[0, g * EDGE + kk] = piece[:, :ROWS]
                moved[1, g * EDGE + kk] = piece[:, ROWS:]
            return carry

        lax.fori_loop(0, EDGE // 2, column, 0, unroll=4)


def stacked(par, field, moved, k):
    step = par[DIL]
    return jnp.concatenate([moved[0, EDGE + k + step], field[EDGE + k], moved[1, EDGE + k - step]], axis=0)


def pair(refs):
    return jnp.concatenate(refs, axis=1)


def eye():
    return jnp.where(iota((ROWS, ROWS), 0) == iota((ROWS, ROWS), 1), 1.0, 0.0).astype(BF)


def turn(one, value):
    return lax.dot_general(one, value, (((1,), (1,)), ((), ())), preferred_element_type=F32)


def turn_field(loads, value, held, put):
    one = eye()
    size = CH // len(loads)

    def channels(step, carry):
        c = step * 4
        out = turn(one, jnp.concatenate([value(c + n) for n in range(4)], axis=0))
        for n in range(4):
            held[pl.ds(c + n, COLS, stride=TURN), :] = out[:, n * ROWS:(n + 1) * ROWS]
        return carry

    for n, load in enumerate(loads):
        load.wait()
        lax.fori_loop(n * size // 4, (n + 1) * size // 4, channels, 0, unroll=size // 4)

    def column(k, carry):
        put(k, held[pl.ds(pl.multiple_of(k * TURN, 8), CH), :].astype(BF))
        return carry

    lax.fori_loop(0, COLS, column, 0, unroll=16)


def kept_cells(par):
    shape = (ROWS, COLS)
    return iota(shape, 1) + par[DIAG] * COLS < reach_of(par, iota(shape, 0))


def products(par, blocks, field, moved, weight, prod):
    count, unroll, number = blocks

    def block(at, carry):
        for j in range(0, STEP, 2):
            k = number(at) + j
            rhs = pair([stacked(par, field, moved, k), stacked(par, field, moved, k + 1)])
            out = jnp.dot(weight[...], rhs, preferred_element_type=F32)
            for n in range(2):
                prod[DMAX + k + n] = out[:, n * ROWS:(n + 1) * ROWS]
        return carry

    lax.fori_loop(0, count, block, 0, unroll=unroll)


def gathered(par, prod, k):
    step = par[DIL + 1]
    return prod[DMAX + k - step, :CH] + prod[DMAX + k, CH:2 * CH] + prod[DMAX + k + step, 2 * CH:]


def activate(par, blocks, prod, masked, mix_t, grad_pre, acc_mix):
    count, number = blocks

    def block(at, carry):
        ks = [number(at) * STEP + j for j in range(STEP)]
        upstream = pair([masked[k] for k in ks])
        back = jnp.dot(mix_t[...], upstream, preferred_element_type=F32)
        pre = pair([gathered(par, prod, k) for k in ks])
        grad = jnp.where(pre > 0, back, 0.0).astype(BF)
        for j, k in enumerate(ks):
            grad_pre[EDGE + k] = grad[:, j * ROWS:(j + 1) * ROWS]
        acc_mix[...] += lax.dot_general(upstream, jnp.maximum(pre, 0.0).astype(BF), (((1,), (1,)), ((), ())),
                                        preferred_element_type=F32)
        return carry

    lax.fori_loop(0, count, block, 0, unroll=2)


def kernel_grads(par, field, moved, grad_pre, acc):
    acc[...] = jnp.zeros_like(acc)
    step = par[DIL + 1]

    def block(blk, carry):
        ks = [blk * STEP - DMAX + j for j in range(STEP)]
        rhs = pair([stacked(par, field, moved, k) for k in ks])
        lhs = jnp.concatenate([pair([grad_pre[EDGE + k - move] for k in ks]) for move in (-step, 0, step)], axis=0)
        acc[...] += lax.dot_general(lhs, rhs, (((1,), (1,)), ((), ())), preferred_element_type=F32)
        return carry

    lax.fori_loop(0, (COLS + 2 * DMAX) // STEP, block, 0, unroll=2)


def share_out(acc, acc_mix, part):
    main, side = acc[:, :ROWS], acc[:, ROWS:3 * CH]
    tail = [side[n * CH:(n + 1) * CH] for n in range(3)] + [acc_mix[...], jnp.zeros((CH, 2 * EDGE), F32)]
    rows = jnp.concatenate([main, jnp.concatenate(tail, axis=1)], axis=0)
    size = part.shape[1]
    for n in range(part.shape[0]):
        part[n] = rows[n * size:(n + 1) * size]


def place_weights(conv, mix, forward, backward, mix_t):
    shape = (CH, 3 * CH)
    gap = iota(shape, 1) - iota(shape, 0)
    puts = [jnp.where(gap == a * CH, 1.0, 0.0).astype(BF) for a in range(3)]
    turned = (((0,), (0,)), ((), ()))
    for b in range(3):
        taps = jnp.zeros(shape, F32)
        back = jnp.zeros(shape, F32)
        for a in range(3):
            taps += jnp.dot(conv[3 * a + b], puts[a], preferred_element_type=F32)
            back += lax.dot_general(conv[3 * (2 - a) + 2 - b], puts[a], turned, preferred_element_type=F32)
        forward[b * CH:(b + 1) * CH, :] = taps.astype(BF)
        backward[b * CH:(b + 1) * CH, :] = back.astype(BF)
    mix_t[...] = lax.dot_general(mix[...], puts[0], turned, preferred_element_type=F32)[:, :CH].astype(BF)


def lay_out(par, prod, spread):
    def block(blk, carry):
        for j in range(STEP):
            k = blk * STEP + j
            spread[pl.ds(k, CH, stride=BACK), :] = gathered(par, prod, k)
        return carry

    lax.fori_loop(0, COLS // STEP, block, 0, unroll=2)


def finish(par, x_ref, g_ref, spread, out_ref):
    keep = jnp.where(kept_cells(par), 1.0, 0.0).astype(BF)
    live = jnp.where(iota((ROWS, COLS), 0) < par[LIVE], 1.0, 0.0).astype(BF)
    one = eye()
    zero = jnp.zeros((ROWS, COLS), BF)

    def channels(step, carry):
        c = step * 4
        parts = [spread[pl.ds(pl.multiple_of((c + n) * BACK, 8), COLS), :].astype(BF) for n in range(4)]
        out = turn(one, jnp.concatenate(parts, axis=0)).astype(BF)
        for n in range(4):
            part = jnp.where(x_ref[c + n] > zero, out[:, n * ROWS:(n + 1) * ROWS], zero)
            out_ref[c + n] = (g_ref[c + n] + part * keep) * live
        return carry

    lax.fori_loop(0, CH // 4, channels, 0, unroll=4)


def remote(src, dst, send, recv, device):
    return pltpu.make_async_remote_copy(src_ref=src, dst_ref=dst, send_sem=send, recv_sem=recv,
                                        device_id=device, device_id_type=MESH)


def neighbours():
    tile, diag = lax.axis_index("tiles"), lax.axis_index("diag")
    tiles, diags = lax.axis_size("tiles"), lax.axis_size("diag")
    up, down = lax.rem(tile + tiles - 1, tiles), lax.rem(tile + 1, tiles)
    lo, hi = lax.rem(diag + diags - 1, diags), lax.rem(diag + 1, diags)
    return [(tile, lo), (tile, hi), (up, diag), (down, diag), (up, lo), (up, hi), (down, lo), (down, hi)]


def halo_copies(near, field, first, last, left, right, top, bot, send, recv):
    inner = pl.ds(1, GROUPS)
    plan = [
        (field.at[pl.ds(EDGE, EDGE)], right),
        (field.at[pl.ds(COLS, EDGE)], left),
        (first, bot.at[inner]),
        (last, top.at[inner]),
        (first.at[0], bot.at[GROUPS + 1]),
        (first.at[GROUPS - 1], bot.at[0]),
        (last.at[0], top.at[GROUPS + 1]),
        (last.at[GROUPS - 1], top.at[0]),
    ]
    return [remote(src, dst, send.at[n], recv.at[n], near[n]) for n, (src, dst) in enumerate(plan)]


def unpack(scale, done, conv_ref, mix_ref):
    rows = jnp.concatenate([done[n] for n in range(done.shape[0])], axis=0) * scale
    tail = rows[3 * CH:]
    for b in range(3):
        full = jnp.concatenate([rows[b * CH:(b + 1) * CH], tail[:, b * EDGE:(b + 1) * EDGE]], axis=1)
        for a in range(3):
            conv_ref[3 * a + b] = full[:, a * CH:(a + 1) * CH]
    mix_ref[...] = tail[:, 3 * EDGE:3 * EDGE + CH]


def everything(inner, scale, counts_in, reach_in, dilation_in, x_hbm, g_hbm, conv_in, mix_in, out_ref, conv_ref, mix_ref,
               counts, reach, dilation, conv, mix,
               x_ref, g_ref, field, masked, grad_pre, prod, moved, held, spread, acc, acc_mix, forward, backward, mix_t,
               first1, last1, left1, right1, top1, bot1, first2, last2, left2, right2, top2, bot2,
               part, parts_in, far, done, load, send1, recv1, send2, recv2, send3, recv3, send4, recv4, send5, recv5):
    tile, diag = lax.axis_index("tiles"), lax.axis_index("diag")
    tiles, diags = lax.axis_size("tiles"), lax.axis_size("diag")
    pairs = [(counts_in, counts), (reach_in, reach), (dilation_in, dilation), (conv_in, conv), (mix_in, mix)]
    small = [pltpu.make_async_copy(src, dst, load.at[2 * LOADS + n]) for n, (src, dst) in enumerate(pairs)]
    parts = [pl.ds(n * (CH // LOADS), CH // LOADS) for n in range(LOADS)]
    x_loads = [pltpu.make_async_copy(x_hbm.at[at], x_ref.at[at], load.at[n]) for n, at in enumerate(parts)]
    g_loads = [pltpu.make_async_copy(g_hbm.at[at], g_ref.at[at], load.at[LOADS + n]) for n, at in enumerate(parts)]
    for copy in small + x_loads:
        copy.start()

    shares = (tiles // inner) * diags
    outer, other = lax.div(tile, inner), lax.rem(tile, inner)
    rank = outer * diags + diag
    friends = [lax.rem(rank + step, shares) for step in range(1, shares)]
    friend_ids = [(lax.div(to, diags) * inner + other, lax.rem(to, diags)) for to in friends]
    cousin_ids = [(outer * inner + lax.rem(other + step, inner), diag) for step in range(1, inner)]
    near = neighbours()
    barrier = pltpu.get_barrier_semaphore()
    for device in near + friend_ids + cousin_ids:
        pl.semaphore_signal(barrier, inc=1, device_id=device, device_id_type=MESH)

    for copy in g_loads:
        copy.start()
    for copy in small:
        copy.wait()
    par = [counts[0] * (ROWS // 4)] + [reach[n] for n in range(4)] + [dilation[0], dilation[1]]
    par += [tile, diag, tiles - 1, diags - 1]
    place_weights(conv, mix, forward, backward, mix_t)
    keep = jnp.where(kept_cells(par), 1.0, 0.0).astype(BF)

    def put_field(k, value):
        field[EDGE + k] = value

    def put_masked(k, value):
        masked[k] = value

    turn_field(x_loads, lambda c: jnp.maximum(x_ref[c], jnp.zeros((), BF)) * keep, held, put_field)
    pl.semaphore_wait(barrier, len(near) + len(friend_ids) + len(cousin_ids))
    halo1 = halo_copies(near, field, first1, last1, left1, right1, top1, bot1, send1, recv1)
    pack_edges(par, field, first1, last1)
    for copy in halo1[2:] + halo1[:2]:
        copy.start()
    turn_field(g_loads, lambda c: g_ref[c] * keep, held, put_masked)
    inside = range(1, GROUPS + 1)
    for copy in halo1[2:4]:
        copy.wait_recv()
    shift_rows(par, inside, field, top1, bot1, moved)
    halo2 = halo_copies(near, grad_pre, first2, last2, left2, right2, top2, bot2, send2, recv2)
    ends = EDGE // STEP
    middle = COLS // STEP - 2 * ends
    acc_mix[...] = jnp.zeros_like(acc_mix)
    products(par, (middle + 2, 7, lambda at: at * STEP + DMAX), field, moved, forward, prod)
    activate(par, (middle, lambda at: at + ends), prod, masked, mix_t, grad_pre, acc_mix)
    for copy in halo1[:2] + halo1[4:]:
        copy.wait_recv()
    set_edges(par, left1, right1, field)
    shift_rows(par, [0, GROUPS + 1], field, top1, bot1, moved)
    products(par, (4, 4, lambda at: at * STEP - DMAX + (at // 2) * (middle + 2) * STEP), field, moved, forward, prod)
    activate(par, (2 * ends, lambda at: at + (at // ends) * middle), prod, masked, mix_t, grad_pre, acc_mix)
    halo2[0].start()
    halo2[1].start()
    pack_edges(par, grad_pre, first2, last2)
    for copy in halo2[2:]:
        copy.start()
    for e in range(EDGE):
        grad_pre[e] = jnp.zeros((CH, ROWS), BF)
        grad_pre[EDGE + COLS + e] = jnp.zeros((CH, ROWS), BF)
    kernel_grads(par, field, moved, grad_pre, acc)
    share_out(acc, acc_mix, part)
    sum1 = [remote(part.at[to], parts_in.at[rank], send3, recv3, friend_ids[n]) for n, to in enumerate(friends)]
    sum2 = [remote(far.at[other], far.at[other], send4, recv4, to) for to in cousin_ids]
    sum3 = [remote(done.at[rank], done.at[rank], send5, recv5, to) for to in friend_ids]
    all1, all2, all3 = [
        remote(slots.at[pl.ds(0, slots.shape[0] - 1)], slots.at[pl.ds(0, slots.shape[0] - 1)], send, recv, near[0])
        for slots, send, recv in ((parts_in, send3, recv3), (far, send4, recv4), (done, send5, recv5))]
    for copy in sum1:
        copy.start()
    parts_in[rank] = part[rank]

    for copy in halo2:
        copy.wait_recv()
    set_edges(par, left2, right2, grad_pre)
    shift_rows(par, range(GROUPS + 2), grad_pre, top2, bot2, moved)
    all1.wait_recv()
    far[other] = jnp.sum(parts_in[...], axis=0)
    for copy in sum2:
        copy.start()
    products(par, (COLS // STEP + 2, 6, lambda at: at * STEP - DMAX), grad_pre, moved, backward, prod)
    all2.wait_recv()
    done[rank] = jnp.sum(far[...], axis=0)
    for copy in sum3:
        copy.start()
    lay_out(par, prod, spread)
    finish(par, x_ref, g_ref, spread, out_ref)
    all3.wait_recv()
    unpack(scale, done, conv_ref, mix_ref)
    for copy in halo1 + halo2 + [all1, all2, all3]:
        copy.wait_send()


def move_out(field, conv, mix, field_out, conv_out, mix_out, sems):
    size = CH // MOVES
    pieces = [(field.at[pl.ds(n * size, size)], field_out.at[pl.ds(n * size, size)]) for n in range(MOVES)]
    copies = [pltpu.make_async_copy(src, dst, sems.at[n])
              for n, (src, dst) in enumerate([(conv, conv_out), (mix, mix_out)] + pieces)]
    for copy in copies:
        copy.start()
    for copy in copies:
        copy.wait()


def specs(space, count):
    return [pl.BlockSpec(memory_space=space)] * count


def body(inputs, cotangent, conv_weight, mix_weight, counts, band_reach, dilation):
    shape = jax.ShapeDtypeStruct
    tiles, diags = lax.axis_size("tiles"), lax.axis_size("diag")
    inner = 16 if tiles == 64 else 2
    shares = (tiles // inner) * diags
    dma = lambda n: pltpu.SemaphoreType.DMA((n,))
    whole = pltpu.VMEM((CH, ROWS, COLS), BF)
    field = pltpu.VMEM((COLS, CH, ROWS), BF)
    pack = pltpu.VMEM((GROUPS, CH, ROWS), BF)
    wide = pltpu.VMEM((COLS + 2 * EDGE, CH, ROWS), BF)
    side = pltpu.VMEM((EDGE, CH, ROWS), BF)
    ends = pltpu.VMEM((GROUPS + 2, CH, ROWS), BF)
    slots = lambda n: pltpu.VMEM((n, SUM_ROWS // shares, ROWS), F32)
    halo = [pack, pack, side, side, ends, ends]
    cells = TPD * tiles * (ROWS // 4) * COLS * diags
    results = pl.pallas_call(
        functools.partial(everything, inner, 1.0 / math.sqrt(cells)),
        out_shape=[pltpu.VMEM((CH, ROWS, COLS), BF), pltpu.VMEM((TAPS, CH, CH), F32), pltpu.VMEM((CH, CH), F32)],
        in_specs=specs(pltpu.HBM, 7),
        out_specs=specs(pltpu.VMEM, 3),
        scratch_shapes=[
            pltpu.SMEM(counts.shape, jnp.int32), pltpu.SMEM(band_reach.shape, jnp.int32), pltpu.SMEM(dilation.shape, jnp.int32),
            pltpu.VMEM(conv_weight.shape, BF), pltpu.VMEM(mix_weight.shape, BF),
            whole, whole, wide, field, wide,
            pltpu.VMEM((COLS + 2 * DMAX, 3 * CH, ROWS), F32),
            pltpu.VMEM((2, COLS + 2 * EDGE, CH, ROWS), BF),
            pltpu.VMEM(((COLS + 1) * TURN, ROWS), F32),
            pltpu.VMEM(((CH + 1) * BACK, ROWS), F32),
            pltpu.VMEM((3 * CH, 3 * CH), F32),
            pltpu.VMEM((CH, CH), F32),
            pltpu.VMEM((3 * CH, 3 * CH), BF),
            pltpu.VMEM((3 * CH, 3 * CH), BF),
            pltpu.VMEM((CH, CH), BF),
            *halo, *halo,
            slots(shares), slots(shares), slots(inner), slots(shares),
            dma(2 * LOADS + 5), dma(8), dma(8), dma(8), dma(8),
            *[pltpu.SemaphoreType.DMA] * 6,
        ],
        cost_estimate=pl.CostEstimate(flops=6 * CH * CH * TAPS * ROWS * COLS, bytes_accessed=3 * 2 * CH * ROWS * COLS,
                                      transcendentals=0),
        compiler_params=pltpu.CompilerParams(collective_id=0, has_side_effects=True, vmem_limit_bytes=VMEM_LIMIT),
    )(counts, band_reach, dilation, inputs, cotangent, conv_weight, mix_weight)
    return pl.pallas_call(
        move_out,
        out_shape=[shape(r.shape, r.dtype) for r in results],
        in_specs=specs(pltpu.VMEM, 3),
        out_specs=specs(pltpu.HBM, 3),
        scratch_shapes=[dma(MOVES + 2)],
        compiler_params=pltpu.CompilerParams(vmem_limit_bytes=8 * 1024 * 1024),
    )(*results)


def solution(mesh):
    in_specs = (
        P(None, "tiles", "diag"),
        P(None, "tiles", "diag"),
        P(),
        P(),
        P("tiles"),
        P("tiles"),
        P(),
    )
    out_specs = (P(None, "tiles", "diag"), P(), P())
    return jax.shard_map(body, mesh=mesh, in_specs=in_specs, out_specs=out_specs, check_vma=False)
```

```python
import functools
import math

import jax
import jax.numpy as jnp
from jax import lax
from jax.experimental import pallas as pl
from jax.experimental.pallas import tpu as pltpu
from jax.sharding import PartitionSpec as P

MESH = pl.DeviceIdType.MESH
TPD = 2
DMAX = 8
CH = 48
ROWS = 128
COLS = 128
EDGE = 2 * DMAX
GROUPS = COLS // EDGE
STEP = 8
TAPS = 9
SUM_ROWS = 192
VMEM_LIMIT = 56 * 1024 * 1024
BF = jnp.bfloat16
F32 = jnp.float32
LIVE, REACH, DIL, TILE, DIAG, LAST_TILE, LAST_DIAG = 0, 1, 5, 7, 8, 9, 10
TURN = 56
BACK = 136
LOADS = 3
MOVES = 4


def iota(shape, dim):
    return lax.broadcasted_iota(jnp.int32, shape, dim)


def reach_of(par, ids):
    reach = jnp.where(ids < 64, jnp.where(ids < 32, par[REACH], par[REACH + 1]),
                      jnp.where(ids < 96, par[REACH + 2], par[REACH + 3]))
    return jnp.where(ids < par[LIVE], reach, 0)


def pack_edges(par, field, first, last):
    lane = iota((1, 2 * ROWS), 1)
    near = lane % DMAX
    want = jnp.where(lane < ROWS, near, par[LIVE] - DMAX + near)
    place = jnp.where(lane < ROWS, (lane // DMAX + EDGE // 2) % EDGE, (lane - ROWS) // DMAX)
    hit = jnp.where(iota((ROWS, 2 * ROWS), 0) == want, 1.0, 0.0)
    weight = jnp.concatenate([jnp.where(place == kk, hit, 0.0).astype(BF) for kk in range(EDGE)], axis=0)
    lhs = jnp.concatenate(
        [jnp.concatenate([field[(g + 1) * EDGE + kk] for g in range(GROUPS)], axis=0) for kk in range(EDGE)], axis=1)
    out = jnp.dot(lhs, weight, preferred_element_type=F32).astype(BF)
    for g in range(GROUPS):
        first[g] = out[g * CH:(g + 1) * CH, :ROWS]
        last[g] = out[g * CH:(g + 1) * CH, ROWS:]


def set_edges(par, left, right, field):
    for e in range(EDGE):
        low, high = left[e], right[e]
        field[e] = jnp.where(par[DIAG] > 0, low, jnp.zeros_like(low))
        field[EDGE + COLS + e] = jnp.where(par[DIAG] < par[LAST_DIAG], high, jnp.zeros_like(high))


def shift_rows(par, groups, field, top, bot, moved):
    half = ROWS // 2
    lane = iota((1, 2 * ROWS), 1)
    move = jnp.where(lane < ROWS, -par[DIL], par[DIL])
    want = (lane % ROWS) + move
    rows = iota((ROWS, 2 * ROWS), 0)
    inner = jnp.where(rows == want, 1.0, 0.0).astype(BF)
    has_top = par[TILE] > 0
    has_bot = par[TILE] < par[LAST_TILE]
    top_want = jnp.where((want < 0) & has_top, want + DMAX, -1)
    low = want - par[LIVE]
    bot_want = jnp.where((low >= 0) & (low < DMAX) & has_bot, low, -1)
    wants = [jnp.where(rows < half, top_want, bot_want), jnp.where(rows < half, bot_want, top_want)]
    outers = [jnp.where(rows % DMAX == w, 1.0, 0.0) for w in wants]
    place = (rows % half) // DMAX
    has_left = par[DIAG] > 0
    has_right = par[DIAG] < par[LAST_DIAG]
    tops = jnp.concatenate([top[g] for g in groups], axis=0)
    bots = jnp.concatenate([bot[g] for g in groups], axis=0)
    upper = iota(tops.shape, 1) < half
    halos = [jnp.where(upper, tops, bots), jnp.where(upper, bots, tops)]

    for part in range(2):
        def column(at, carry):
            kk = at + part * (EDGE // 2)
            weight = jnp.concatenate([inner, jnp.where(place == at, outers[part], 0.0).astype(BF)], axis=0)
            tiles = [field[g * EDGE + kk] for g in groups]
            lhs = jnp.concatenate([jnp.concatenate(tiles, axis=0), halos[part]], axis=1)
            out = jnp.dot(lhs, weight, preferred_element_type=F32)
            for n, g in enumerate(groups):
                piece = out[n * CH:(n + 1) * CH]
                if g == 0:
                    piece = jnp.where(has_left, piece, 0.0)
                if g == GROUPS + 1:
                    piece = jnp.where(has_right, piece, 0.0)
                piece = piece.astype(BF)
                moved[0, g * EDGE + kk] = piece[:, :ROWS]
                moved[1, g * EDGE + kk] = piece[:, ROWS:]
            return carry

        lax.fori_loop(0, EDGE // 2, column, 0, unroll=4)


def stacked(par, field, moved, k):
    step = par[DIL]
    return jnp.concatenate([moved[0, EDGE + k + step], field[EDGE + k], moved[1, EDGE + k - step]], axis=0)


def pair(refs):
    return jnp.concatenate(refs, axis=1)


def eye():
    return jnp.where(iota((ROWS, ROWS), 0) == iota((ROWS, ROWS), 1), 1.0, 0.0).astype(BF)


def turn(one, value):
    return lax.dot_general(one, value, (((1,), (1,)), ((), ())), preferred_element_type=F32)


def turn_field(loads, value, held, put):
    one = eye()
    size = CH // len(loads)

    def channels(step, carry):
        c = step * 4
        out = turn(one, jnp.concatenate([value(c + n) for n in range(4)], axis=0))
        for n in range(4):
            held[pl.ds(c + n, COLS, stride=TURN), :] = out[:, n * ROWS:(n + 1) * ROWS]
        return carry

    for n, load in enumerate(loads):
        load.wait()
        lax.fori_loop(n * size // 4, (n + 1) * size // 4, channels, 0, unroll=size // 4)

    def column(k, carry):
        put(k, held[pl.ds(pl.multiple_of(k * TURN, 8), CH), :].astype(BF))
        return carry

    lax.fori_loop(0, COLS, column, 0, unroll=16)


def kept_cells(par):
    shape = (ROWS, COLS)
    return iota(shape, 1) + par[DIAG] * COLS < reach_of(par, iota(shape, 0))


def products(par, blocks, field, moved, weight, prod):
    count, unroll, number = blocks

    def block(at, carry):
        for j in range(0, STEP, 2):
            k = number(at) + j
            rhs = pair([stacked(par, field, moved, k), stacked(par, field, moved, k + 1)])
            out = jnp.dot(weight[...], rhs, preferred_element_type=F32)
            for n in range(2):
                prod[DMAX + k + n] = out[:, n * ROWS:(n + 1) * ROWS]
        return carry

    lax.fori_loop(0, count, block, 0, unroll=unroll)


def gathered(par, prod, k):
    step = par[DIL + 1]
    return prod[DMAX + k - step, :CH] + prod[DMAX + k, CH:2 * CH] + prod[DMAX + k + step, 2 * CH:]


def activate(par, blocks, prod, masked, mix_t, grad_pre, acc_mix):
    count, number = blocks

    def block(at, carry):
        ks = [number(at) * STEP + j for j in range(STEP)]
        upstream = pair([masked[k] for k in ks])
        back = jnp.dot(mix_t[...], upstream, preferred_element_type=F32)
        pre = pair([gathered(par, prod, k) for k in ks])
        grad = jnp.where(pre > 0, back, 0.0).astype(BF)
        for j, k in enumerate(ks):
            grad_pre[EDGE + k] = grad[:, j * ROWS:(j + 1) * ROWS]
        acc_mix[...] += lax.dot_general(upstream, jnp.maximum(pre, 0.0).astype(BF), (((1,), (1,)), ((), ())),
                                        preferred_element_type=F32)
        return carry

    lax.fori_loop(0, count, block, 0, unroll=2)


def kernel_grads(par, field, moved, grad_pre, acc):
    acc[...] = jnp.zeros_like(acc)
    step = par[DIL + 1]

    def block(blk, carry):
        ks = [blk * STEP - DMAX + j for j in range(STEP)]
        rhs = pair([stacked(par, field, moved, k) for k in ks])
        lhs = jnp.concatenate([pair([grad_pre[EDGE + k - move] for k in ks]) for move in (-step, 0, step)], axis=0)
        acc[...] += lax.dot_general(lhs, rhs, (((1,), (1,)), ((), ())), preferred_element_type=F32)
        return carry

    lax.fori_loop(0, (COLS + 2 * DMAX) // STEP, block, 0, unroll=2)


def share_out(acc, acc_mix, part):
    main, side = acc[:, :ROWS], acc[:, ROWS:3 * CH]
    tail = [side[n * CH:(n + 1) * CH] for n in range(3)] + [acc_mix[...], jnp.zeros((CH, 2 * EDGE), F32)]
    rows = jnp.concatenate([main, jnp.concatenate(tail, axis=1)], axis=0)
    size = part.shape[1]
    for n in range(part.shape[0]):
        part[n] = rows[n * size:(n + 1) * size]


def place_weights(conv, mix, forward, backward, mix_t):
    shape = (CH, 3 * CH)
    gap = iota(shape, 1) - iota(shape, 0)
    puts = [jnp.where(gap == a * CH, 1.0, 0.0).astype(BF) for a in range(3)]
    turned = (((0,), (0,)), ((), ()))
    for b in range(3):
        taps = jnp.zeros(shape, F32)
        back = jnp.zeros(shape, F32)
        for a in range(3):
            taps += jnp.dot(conv[3 * a + b], puts[a], preferred_element_type=F32)
            back += lax.dot_general(conv[3 * (2 - a) + 2 - b], puts[a], turned, preferred_element_type=F32)
        forward[b * CH:(b + 1) * CH, :] = taps.astype(BF)
        backward[b * CH:(b + 1) * CH, :] = back.astype(BF)
    mix_t[...] = lax.dot_general(mix[...], puts[0], turned, preferred_element_type=F32)[:, :CH].astype(BF)


def lay_out(par, prod, spread):
    def block(blk, carry):
        for j in range(STEP):
            k = blk * STEP + j
            spread[pl.ds(k, CH, stride=BACK), :] = gathered(par, prod, k)
        return carry

    lax.fori_loop(0, COLS // STEP, block, 0, unroll=2)


def finish(par, x_ref, g_ref, spread, out_ref):
    keep = jnp.where(kept_cells(par), 1.0, 0.0).astype(BF)
    live = jnp.where(iota((ROWS, COLS), 0) < par[LIVE], 1.0, 0.0).astype(BF)
    one = eye()
    zero = jnp.zeros((ROWS, COLS), BF)

    def channels(step, carry):
        c = step * 4
        parts = [spread[pl.ds(pl.multiple_of((c + n) * BACK, 8), COLS), :].astype(BF) for n in range(4)]
        out = turn(one, jnp.concatenate(parts, axis=0)).astype(BF)
        for n in range(4):
            part = jnp.where(x_ref[c + n] > zero, out[:, n * ROWS:(n + 1) * ROWS], zero)
            out_ref[c + n] = (g_ref[c + n] + part * keep) * live
        return carry

    lax.fori_loop(0, CH // 4, channels, 0, unroll=4)


def remote(src, dst, send, recv, device):
    return pltpu.make_async_remote_copy(src_ref=src, dst_ref=dst, send_sem=send, recv_sem=recv,
                                        device_id=device, device_id_type=MESH)


def neighbours():
    tile, diag = lax.axis_index("tiles"), lax.axis_index("diag")
    tiles, diags = lax.axis_size("tiles"), lax.axis_size("diag")
    up, down = lax.rem(tile + tiles - 1, tiles), lax.rem(tile + 1, tiles)
    lo, hi = lax.rem(diag + diags - 1, diags), lax.rem(diag + 1, diags)
    return [(tile, lo), (tile, hi), (up, diag), (down, diag), (up, lo), (up, hi), (down, lo), (down, hi)]


def halo_copies(near, field, first, last, left, right, top, bot, send, recv):
    inner = pl.ds(1, GROUPS)
    plan = [
        (field.at[pl.ds(EDGE, EDGE)], right),
        (field.at[pl.ds(COLS, EDGE)], left),
        (first, bot.at[inner]),
        (last, top.at[inner]),
        (first.at[0], bot.at[GROUPS + 1]),
        (first.at[GROUPS - 1], bot.at[0]),
        (last.at[0], top.at[GROUPS + 1]),
        (last.at[GROUPS - 1], top.at[0]),
    ]
    return [remote(src, dst, send.at[n], recv.at[n], near[n]) for n, (src, dst) in enumerate(plan)]


def unpack(scale, done, conv_ref, mix_ref):
    rows = jnp.concatenate([done[n] for n in range(done.shape[0])], axis=0) * scale
    tail = rows[3 * CH:]
    for b in range(3):
        full = jnp.concatenate([rows[b * CH:(b + 1) * CH], tail[:, b * EDGE:(b + 1) * EDGE]], axis=1)
        for a in range(3):
            conv_ref[3 * a + b] = full[:, a * CH:(a + 1) * CH]
    mix_ref[...] = tail[:, 3 * EDGE:3 * EDGE + CH]


def everything(depth, scale, counts_in, reach_in, dilation_in, x_hbm, g_hbm, conv_in, mix_in, out_ref, conv_ref, mix_ref,
               counts, reach, dilation, conv, mix,
               x_ref, g_ref, field, masked, grad_pre, prod, moved, held, spread, acc, acc_mix, forward, backward, mix_t,
               first1, last1, left1, right1, top1, bot1, first2, last2, left2, right2, top2, bot2,
               part, parts_in, over_diag, over_z, done, load, send1, recv1, send2, recv2,
               send3, recv3, send4, recv4, send5, recv5, send6, recv6):
    tile, diag = lax.axis_index("tiles"), lax.axis_index("diag")
    tiles, diags = lax.axis_size("tiles"), lax.axis_size("diag")
    pairs = [(counts_in, counts), (reach_in, reach), (dilation_in, dilation), (conv_in, conv), (mix_in, mix)]
    small = [pltpu.make_async_copy(src, dst, load.at[2 * LOADS + n]) for n, (src, dst) in enumerate(pairs)]
    parts = [pl.ds(n * (CH // LOADS), CH // LOADS) for n in range(LOADS)]
    x_loads = [pltpu.make_async_copy(x_hbm.at[at], x_ref.at[at], load.at[n]) for n, at in enumerate(parts)]
    g_loads = [pltpu.make_async_copy(g_hbm.at[at], g_ref.at[at], load.at[LOADS + n]) for n, at in enumerate(parts)]
    for copy in small + x_loads:
        copy.start()

    shares = (tiles // (2 * depth)) * 2
    across, z, core = lax.div(tile, 2 * depth), lax.rem(lax.div(tile, 2), depth), lax.rem(tile, 2)
    rank = across * 2 + core
    friends = [lax.rem(rank + step, shares) for step in range(1, shares)]
    friend_ids = [(lax.div(to, 2) * 2 * depth + z * 2 + lax.rem(to, 2), diag) for to in friends]
    diag_ids = [(tile, lax.rem(diag + step, diags)) for step in range(1, diags)]
    z_ids = [((across * depth + lax.rem(z + step, depth)) * 2 + core, diag) for step in range(1, depth)]
    near = neighbours()
    barrier = pltpu.get_barrier_semaphore()
    for device in near + friend_ids + diag_ids + z_ids:
        pl.semaphore_signal(barrier, inc=1, device_id=device, device_id_type=MESH)

    for copy in g_loads:
        copy.start()
    for copy in small:
        copy.wait()
    par = [counts[0] * (ROWS // 4)] + [reach[n] for n in range(4)] + [dilation[0], dilation[1]]
    par += [tile, diag, tiles - 1, diags - 1]
    place_weights(conv, mix, forward, backward, mix_t)
    keep = jnp.where(kept_cells(par), 1.0, 0.0).astype(BF)

    def put_field(k, value):
        field[EDGE + k] = value

    def put_masked(k, value):
        masked[k] = value

    turn_field(x_loads, lambda c: jnp.maximum(x_ref[c], jnp.zeros((), BF)) * keep, held, put_field)
    pl.semaphore_wait(barrier, len(near) + len(friend_ids) + len(diag_ids) + len(z_ids))
    halo1 = halo_copies(near, field, first1, last1, left1, right1, top1, bot1, send1, recv1)
    pack_edges(par, field, first1, last1)
    for copy in halo1[2:] + halo1[:2]:
        copy.start()
    turn_field(g_loads, lambda c: g_ref[c] * keep, held, put_masked)
    inside = range(1, GROUPS + 1)
    for copy in halo1[2:4]:
        copy.wait_recv()
    shift_rows(par, inside, field, top1, bot1, moved)
    halo2 = halo_copies(near, grad_pre, first2, last2, left2, right2, top2, bot2, send2, recv2)
    ends = EDGE // STEP
    middle = COLS // STEP - 2 * ends
    acc_mix[...] = jnp.zeros_like(acc_mix)
    products(par, (middle + 2, 7, lambda at: at * STEP + DMAX), field, moved, forward, prod)
    activate(par, (middle, lambda at: at + ends), prod, masked, mix_t, grad_pre, acc_mix)
    for copy in halo1[:2] + halo1[4:]:
        copy.wait_recv()
    set_edges(par, left1, right1, field)
    shift_rows(par, [0, GROUPS + 1], field, top1, bot1, moved)
    products(par, (4, 4, lambda at: at * STEP - DMAX + (at // 2) * (middle + 2) * STEP), field, moved, forward, prod)
    activate(par, (2 * ends, lambda at: at + (at // ends) * middle), prod, masked, mix_t, grad_pre, acc_mix)
    halo2[0].start()
    halo2[1].start()
    pack_edges(par, grad_pre, first2, last2)
    for copy in halo2[2:]:
        copy.start()
    for e in range(EDGE):
        grad_pre[e] = jnp.zeros((CH, ROWS), BF)
        grad_pre[EDGE + COLS + e] = jnp.zeros((CH, ROWS), BF)
    kernel_grads(par, field, moved, grad_pre, acc)
    share_out(acc, acc_mix, part)
    sum1 = [remote(part.at[to], parts_in.at[rank], send3, recv3, friend_ids[n]) for n, to in enumerate(friends)]
    sum2 = [remote(over_diag.at[diag], over_diag.at[diag], send4, recv4, to) for to in diag_ids]
    sum3 = [remote(over_z.at[z], over_z.at[z], send5, recv5, to) for to in z_ids]
    sum4 = [remote(done.at[rank], done.at[rank], send6, recv6, to) for to in friend_ids]
    hops = [
        remote(slots.at[pl.ds(0, slots.shape[0] - 1)], slots.at[pl.ds(0, slots.shape[0] - 1)], send, recv, near[0])
        for slots, send, recv in ((parts_in, send3, recv3), (over_diag, send4, recv4), (over_z, send5, recv5), (done, send6, recv6))]
    for copy in sum1:
        copy.start()
    parts_in[rank] = part[rank]

    for copy in halo2:
        copy.wait_recv()
    set_edges(par, left2, right2, grad_pre)
    shift_rows(par, range(GROUPS + 2), grad_pre, top2, bot2, moved)
    hops[0].wait_recv()
    over_diag[diag] = jnp.sum(parts_in[...], axis=0)
    for copy in sum2:
        copy.start()
    half = (COLS // STEP + 2) // 2
    products(par, (half, 3, lambda at: at * STEP - DMAX), grad_pre, moved, backward, prod)
    hops[1].wait_recv()
    over_z[z] = jnp.sum(over_diag[...], axis=0)
    for copy in sum3:
        copy.start()
    products(par, (half, 3, lambda at: (at + half) * STEP - DMAX), grad_pre, moved, backward, prod)
    lay_out(par, prod, spread)
    hops[2].wait_recv()
    done[rank] = jnp.sum(over_z[...], axis=0)
    for copy in sum4:
        copy.start()
    finish(par, x_ref, g_ref, spread, out_ref)
    hops[3].wait_recv()
    unpack(scale, done, conv_ref, mix_ref)
    for copy in halo1 + halo2 + hops:
        copy.wait_send()


def move_out(field, conv, mix, field_out, conv_out, mix_out, sems):
    size = CH // MOVES
    pieces = [(field.at[pl.ds(n * size, size)], field_out.at[pl.ds(n * size, size)]) for n in range(MOVES)]
    copies = [pltpu.make_async_copy(src, dst, sems.at[n])
              for n, (src, dst) in enumerate([(conv, conv_out), (mix, mix_out)] + pieces)]
    for copy in copies:
        copy.start()
    for copy in copies:
        copy.wait()


def specs(space, count):
    return [pl.BlockSpec(memory_space=space)] * count


def body(inputs, cotangent, conv_weight, mix_weight, counts, band_reach, dilation):
    shape = jax.ShapeDtypeStruct
    tiles, diags = lax.axis_size("tiles"), lax.axis_size("diag")
    depth = 8 if tiles == 64 else 2
    shares = (tiles // (2 * depth)) * 2
    dma = lambda n: pltpu.SemaphoreType.DMA((n,))
    whole = pltpu.VMEM((CH, ROWS, COLS), BF)
    field = pltpu.VMEM((COLS, CH, ROWS), BF)
    pack = pltpu.VMEM((GROUPS, CH, ROWS), BF)
    wide = pltpu.VMEM((COLS + 2 * EDGE, CH, ROWS), BF)
    side = pltpu.VMEM((EDGE, CH, ROWS), BF)
    ends = pltpu.VMEM((GROUPS + 2, CH, ROWS), BF)
    slots = lambda n: pltpu.VMEM((n, SUM_ROWS // shares, ROWS), F32)
    halo = [pack, pack, side, side, ends, ends]
    cells = TPD * tiles * (ROWS // 4) * COLS * diags
    results = pl.pallas_call(
        functools.partial(everything, depth, 1.0 / math.sqrt(cells)),
        out_shape=[pltpu.VMEM((CH, ROWS, COLS), BF), pltpu.VMEM((TAPS, CH, CH), F32), pltpu.VMEM((CH, CH), F32)],
        in_specs=specs(pltpu.HBM, 7),
        out_specs=specs(pltpu.VMEM, 3),
        scratch_shapes=[
            pltpu.SMEM(counts.shape, jnp.int32), pltpu.SMEM(band_reach.shape, jnp.int32), pltpu.SMEM(dilation.shape, jnp.int32),
            pltpu.VMEM(conv_weight.shape, BF), pltpu.VMEM(mix_weight.shape, BF),
            whole, whole, wide, field, wide,
            pltpu.VMEM((COLS + 2 * DMAX, 3 * CH, ROWS), F32),
            pltpu.VMEM((2, COLS + 2 * EDGE, CH, ROWS), BF),
            pltpu.VMEM(((COLS + 1) * TURN, ROWS), F32),
            pltpu.VMEM(((CH + 1) * BACK, ROWS), F32),
            pltpu.VMEM((3 * CH, 3 * CH), F32),
            pltpu.VMEM((CH, CH), F32),
            pltpu.VMEM((3 * CH, 3 * CH), BF),
            pltpu.VMEM((3 * CH, 3 * CH), BF),
            pltpu.VMEM((CH, CH), BF),
            *halo, *halo,
            slots(shares), slots(shares), slots(diags), slots(depth), slots(shares),
            dma(2 * LOADS + 5), dma(8), dma(8), dma(8), dma(8),
            *[pltpu.SemaphoreType.DMA] * 8,
        ],
        cost_estimate=pl.CostEstimate(flops=6 * CH * CH * TAPS * ROWS * COLS, bytes_accessed=3 * 2 * CH * ROWS * COLS,
                                      transcendentals=0),
        compiler_params=pltpu.CompilerParams(collective_id=0, has_side_effects=True, vmem_limit_bytes=VMEM_LIMIT),
    )(counts, band_reach, dilation, inputs, cotangent, conv_weight, mix_weight)
    return pl.pallas_call(
        move_out,
        out_shape=[shape(r.shape, r.dtype) for r in results],
        in_specs=specs(pltpu.VMEM, 3),
        out_specs=specs(pltpu.HBM, 3),
        scratch_shapes=[dma(MOVES + 2)],
        compiler_params=pltpu.CompilerParams(vmem_limit_bytes=8 * 1024 * 1024),
    )(*results)


def solution(mesh):
    in_specs = (
        P(None, "tiles", "diag"),
        P(None, "tiles", "diag"),
        P(),
        P(),
        P("tiles"),
        P("tiles"),
        P(),
    )
    out_specs = (P(None, "tiles", "diag"), P(), P())
    return jax.shard_map(body, mesh=mesh, in_specs=in_specs, out_specs=out_specs, check_vma=False)
```

```python
import functools
import math

import jax
import jax.numpy as jnp
from jax import lax
from jax.experimental import pallas as pl
from jax.experimental.pallas import tpu as pltpu
from jax.sharding import PartitionSpec as P

MESH = pl.DeviceIdType.MESH
TPD = 2
DMAX = 8
CH = 48
ROWS = 128
COLS = 128
EDGE = 2 * DMAX
GROUPS = COLS // EDGE
STEP = 8
TAPS = 9
SUM_ROWS = 192
VMEM_LIMIT = 56 * 1024 * 1024
BF = jnp.bfloat16
F32 = jnp.float32
LIVE, REACH, DIL, TILE, DIAG, LAST_TILE, LAST_DIAG = 0, 1, 5, 7, 8, 9, 10
TURN = 56
BACK = 136
LOADS = 3
MOVES = 4


def iota(shape, dim):
    return lax.broadcasted_iota(jnp.int32, shape, dim)


def reach_of(par, ids):
    reach = jnp.where(ids < 64, jnp.where(ids < 32, par[REACH], par[REACH + 1]),
                      jnp.where(ids < 96, par[REACH + 2], par[REACH + 3]))
    return jnp.where(ids < par[LIVE], reach, 0)


def pack_edges(par, field, first, last):
    lane = iota((1, 2 * ROWS), 1)
    near = lane % DMAX
    want = jnp.where(lane < ROWS, near, par[LIVE] - DMAX + near)
    place = jnp.where(lane < ROWS, (lane // DMAX + EDGE // 2) % EDGE, (lane - ROWS) // DMAX)
    hit = jnp.where(iota((ROWS, 2 * ROWS), 0) == want, 1.0, 0.0)
    weight = jnp.concatenate([jnp.where(place == kk, hit, 0.0).astype(BF) for kk in range(EDGE)], axis=0)
    lhs = jnp.concatenate(
        [jnp.concatenate([field[(g + 1) * EDGE + kk] for g in range(GROUPS)], axis=0) for kk in range(EDGE)], axis=1)
    out = jnp.dot(lhs, weight, preferred_element_type=F32).astype(BF)
    for g in range(GROUPS):
        first[g] = out[g * CH:(g + 1) * CH, :ROWS]
        last[g] = out[g * CH:(g + 1) * CH, ROWS:]


def set_edges(par, left, right, field):
    for e in range(EDGE):
        low, high = left[e], right[e]
        field[e] = jnp.where(par[DIAG] > 0, low, jnp.zeros_like(low))
        field[EDGE + COLS + e] = jnp.where(par[DIAG] < par[LAST_DIAG], high, jnp.zeros_like(high))


def shift_rows(par, groups, field, top, bot, moved):
    half = ROWS // 2
    lane = iota((1, 2 * ROWS), 1)
    move = jnp.where(lane < ROWS, -par[DIL], par[DIL])
    want = (lane % ROWS) + move
    rows = iota((ROWS, 2 * ROWS), 0)
    inner = jnp.where(rows == want, 1.0, 0.0).astype(BF)
    has_top = par[TILE] > 0
    has_bot = par[TILE] < par[LAST_TILE]
    top_want = jnp.where((want < 0) & has_top, want + DMAX, -1)
    low = want - par[LIVE]
    bot_want = jnp.where((low >= 0) & (low < DMAX) & has_bot, low, -1)
    wants = [jnp.where(rows < half, top_want, bot_want), jnp.where(rows < half, bot_want, top_want)]
    outers = [jnp.where(rows % DMAX == w, 1.0, 0.0) for w in wants]
    place = (rows % half) // DMAX
    has_left = par[DIAG] > 0
    has_right = par[DIAG] < par[LAST_DIAG]
    tops = jnp.concatenate([top[g] for g in groups], axis=0)
    bots = jnp.concatenate([bot[g] for g in groups], axis=0)
    upper = iota(tops.shape, 1) < half
    halos = [jnp.where(upper, tops, bots), jnp.where(upper, bots, tops)]

    for part in range(2):
        def column(at, carry):
            kk = at + part * (EDGE // 2)
            weight = jnp.concatenate([inner, jnp.where(place == at, outers[part], 0.0).astype(BF)], axis=0)
            tiles = [field[g * EDGE + kk] for g in groups]
            lhs = jnp.concatenate([jnp.concatenate(tiles, axis=0), halos[part]], axis=1)
            out = jnp.dot(lhs, weight, preferred_element_type=F32)
            for n, g in enumerate(groups):
                piece = out[n * CH:(n + 1) * CH]
                if g == 0:
                    piece = jnp.where(has_left, piece, 0.0)
                if g == GROUPS + 1:
                    piece = jnp.where(has_right, piece, 0.0)
                piece = piece.astype(BF)
                moved[0, g * EDGE + kk] = piece[:, :ROWS]
                moved[1, g * EDGE + kk] = piece[:, ROWS:]
            return carry

        lax.fori_loop(0, EDGE // 2, column, 0, unroll=EDGE // 2)


def stacked(par, field, moved, k):
    step = par[DIL]
    return jnp.concatenate([moved[0, EDGE + k + step], field[EDGE + k], moved[1, EDGE + k - step]], axis=0)


def pair(refs):
    return jnp.concatenate(refs, axis=1)


def eye():
    return jnp.where(iota((ROWS, ROWS), 0) == iota((ROWS, ROWS), 1), 1.0, 0.0).astype(BF)


def turn(one, value):
    return lax.dot_general(one, value, (((1,), (1,)), ((), ())), preferred_element_type=F32)


def turn_field(loads, value, held, put):
    one = eye()
    size = CH // len(loads)

    def channels(step, carry):
        c = step * 4
        out = turn(one, jnp.concatenate([value(c + n) for n in range(4)], axis=0))
        for n in range(4):
            held[pl.ds(c + n, COLS, stride=TURN), :] = out[:, n * ROWS:(n + 1) * ROWS]
        return carry

    for n, load in enumerate(loads):
        load.wait()
        lax.fori_loop(n * size // 4, (n + 1) * size // 4, channels, 0, unroll=size // 4)

    def column(k, carry):
        put(k, held[pl.ds(pl.multiple_of(k * TURN, 8), CH), :].astype(BF))
        return carry

    lax.fori_loop(0, COLS, column, 0, unroll=16)


def kept_cells(par):
    shape = (ROWS, COLS)
    return iota(shape, 1) + par[DIAG] * COLS < reach_of(par, iota(shape, 0))


def products(par, blocks, field, moved, weight, prod):
    count, unroll, number = blocks

    def block(at, carry):
        for j in range(0, STEP, 2):
            k = number(at) + j
            rhs = pair([stacked(par, field, moved, k), stacked(par, field, moved, k + 1)])
            out = jnp.dot(weight[...], rhs, preferred_element_type=F32)
            for n in range(2):
                prod[DMAX + k + n] = out[:, n * ROWS:(n + 1) * ROWS]
        return carry

    lax.fori_loop(0, count, block, 0, unroll=unroll)


def gathered(par, prod, k):
    step = par[DIL + 1]
    return prod[DMAX + k - step, :CH] + prod[DMAX + k, CH:2 * CH] + prod[DMAX + k + step, 2 * CH:]


def activate(par, blocks, prod, masked, mix_t, grad_pre, acc_mix):
    count, number = blocks

    def block(at, carry):
        ks = [number(at) * STEP + j for j in range(STEP)]
        upstream = pair([masked[k] for k in ks])
        back = jnp.dot(mix_t[...], upstream, preferred_element_type=F32)
        pre = pair([gathered(par, prod, k) for k in ks])
        grad = jnp.where(pre > 0, back, 0.0).astype(BF)
        for j, k in enumerate(ks):
            grad_pre[EDGE + k] = grad[:, j * ROWS:(j + 1) * ROWS]
        acc_mix[...] += lax.dot_general(upstream, jnp.maximum(pre, 0.0).astype(BF), (((1,), (1,)), ((), ())),
                                        preferred_element_type=F32)
        return carry

    lax.fori_loop(0, count, block, 0, unroll=4)


def kernel_grads(par, field, moved, grad_pre, acc):
    acc[...] = jnp.zeros_like(acc)
    step = par[DIL + 1]

    def block(blk, carry):
        ks = [blk * STEP - DMAX + j for j in range(STEP)]
        rhs = pair([stacked(par, field, moved, k) for k in ks])
        lhs = jnp.concatenate([pair([grad_pre[EDGE + k - move] for k in ks]) for move in (-step, 0, step)], axis=0)
        acc[...] += lax.dot_general(lhs, rhs, (((1,), (1,)), ((), ())), preferred_element_type=F32)
        return carry

    lax.fori_loop(0, (COLS + 2 * DMAX) // STEP, block, 0, unroll=6)


def share_out(acc, acc_mix, part):
    main, side = acc[:, :ROWS], acc[:, ROWS:3 * CH]
    tail = [side[n * CH:(n + 1) * CH] for n in range(3)] + [acc_mix[...], jnp.zeros((CH, 2 * EDGE), F32)]
    rows = jnp.concatenate([main, jnp.concatenate(tail, axis=1)], axis=0)
    size = part.shape[1]
    for n in range(part.shape[0]):
        part[n] = rows[n * size:(n + 1) * size]


def place_weights(conv, mix, forward, backward, mix_t):
    shape = (CH, 3 * CH)
    gap = iota(shape, 1) - iota(shape, 0)
    puts = [jnp.where(gap == a * CH, 1.0, 0.0).astype(BF) for a in range(3)]
    turned = (((0,), (0,)), ((), ()))
    for b in range(3):
        taps = jnp.zeros(shape, F32)
        back = jnp.zeros(shape, F32)
        for a in range(3):
            taps += jnp.dot(conv[3 * a + b], puts[a], preferred_element_type=F32)
            back += lax.dot_general(conv[3 * (2 - a) + 2 - b], puts[a], turned, preferred_element_type=F32)
        forward[b * CH:(b + 1) * CH, :] = taps.astype(BF)
        backward[b * CH:(b + 1) * CH, :] = back.astype(BF)
    mix_t[...] = lax.dot_general(mix[...], puts[0], turned, preferred_element_type=F32)[:, :CH].astype(BF)


def lay_out(par, prod, spread):
    def block(blk, carry):
        for j in range(STEP):
            k = blk * STEP + j
            spread[pl.ds(k, CH, stride=BACK), :] = gathered(par, prod, k)
        return carry

    lax.fori_loop(0, COLS // STEP, block, 0, unroll=2)


def finish(par, x_ref, g_ref, spread, out_ref):
    keep = jnp.where(kept_cells(par), 1.0, 0.0).astype(BF)
    live = jnp.where(iota((ROWS, COLS), 0) < par[LIVE], 1.0, 0.0).astype(BF)
    one = eye()
    zero = jnp.zeros((ROWS, COLS), BF)

    def channels(step, carry):
        c = step * 4
        parts = [spread[pl.ds(pl.multiple_of((c + n) * BACK, 8), COLS), :].astype(BF) for n in range(4)]
        out = turn(one, jnp.concatenate(parts, axis=0)).astype(BF)
        for n in range(4):
            part = jnp.where(x_ref[c + n] > zero, out[:, n * ROWS:(n + 1) * ROWS], zero)
            out_ref[c + n] = (g_ref[c + n] + part * keep) * live
        return carry

    lax.fori_loop(0, CH // 4, channels, 0, unroll=4)


def remote(src, dst, send, recv, device):
    return pltpu.make_async_remote_copy(src_ref=src, dst_ref=dst, send_sem=send, recv_sem=recv,
                                        device_id=device, device_id_type=MESH)


def neighbours():
    tile, diag = lax.axis_index("tiles"), lax.axis_index("diag")
    tiles, diags = lax.axis_size("tiles"), lax.axis_size("diag")
    up, down = lax.rem(tile + tiles - 1, tiles), lax.rem(tile + 1, tiles)
    lo, hi = lax.rem(diag + diags - 1, diags), lax.rem(diag + 1, diags)
    return [(tile, lo), (tile, hi), (up, diag), (down, diag), (up, lo), (up, hi), (down, lo), (down, hi)]


def far_first(first, second):
    moves = [(m, n) for m in range(first) for n in range(second) if m or n]
    return sorted(moves, key=lambda move: -min(move[0], first - move[0]) - min(move[1], second - move[1]))


def halo_copies(near, field, first, last, left, right, top, bot, send, recv):
    inner = pl.ds(1, GROUPS)
    plan = [
        (field.at[pl.ds(EDGE, EDGE)], right),
        (field.at[pl.ds(COLS, EDGE)], left),
        (first, bot.at[inner]),
        (last, top.at[inner]),
        (first.at[0], bot.at[GROUPS + 1]),
        (first.at[GROUPS - 1], bot.at[0]),
        (last.at[0], top.at[GROUPS + 1]),
        (last.at[GROUPS - 1], top.at[0]),
    ]
    return [remote(src, dst, send.at[n], recv.at[n], near[n]) for n, (src, dst) in enumerate(plan)]


def unpack(scale, done, conv_ref, mix_ref):
    rows = jnp.concatenate([done[n] for n in range(done.shape[0])], axis=0) * scale
    tail = rows[3 * CH:]
    for b in range(3):
        full = jnp.concatenate([rows[b * CH:(b + 1) * CH], tail[:, b * EDGE:(b + 1) * EDGE]], axis=1)
        for a in range(3):
            conv_ref[3 * a + b] = full[:, a * CH:(a + 1) * CH]
    mix_ref[...] = tail[:, 3 * EDGE:3 * EDGE + CH]


def everything(inner, scale, counts_in, reach_in, dilation_in, x_hbm, g_hbm, conv_in, mix_in, out_ref, conv_ref, mix_ref,
               counts, reach, dilation, conv, mix,
               x_ref, g_ref, field, masked, grad_pre, prod, moved, held, spread, acc, acc_mix, forward, backward, mix_t,
               first1, last1, left1, right1, top1, bot1, first2, last2, left2, right2, top2, bot2,
               part, parts_in, far, done, load, send1, recv1, send2, recv2, send3, recv3, send4, recv4, send5, recv5):
    tile, diag = lax.axis_index("tiles"), lax.axis_index("diag")
    tiles, diags = lax.axis_size("tiles"), lax.axis_size("diag")
    pairs = [(counts_in, counts), (reach_in, reach), (dilation_in, dilation), (conv_in, conv), (mix_in, mix)]
    small = [pltpu.make_async_copy(src, dst, load.at[2 * LOADS + n]) for n, (src, dst) in enumerate(pairs)]
    parts = [pl.ds(n * (CH // LOADS), CH // LOADS) for n in range(LOADS)]
    x_loads = [pltpu.make_async_copy(x_hbm.at[at], x_ref.at[at], load.at[n]) for n, at in enumerate(parts)]
    g_loads = [pltpu.make_async_copy(g_hbm.at[at], g_ref.at[at], load.at[LOADS + n]) for n, at in enumerate(parts)]
    for copy in small + x_loads:
        copy.start()

    shares = (tiles // inner) * diags
    outer, other = lax.div(tile, inner), lax.rem(tile, inner)
    rank = outer * diags + diag
    friends = [(lax.rem(outer + dx, tiles // inner), lax.rem(diag + dy, diags)) for dx, dy in far_first(tiles // inner, diags)]
    friend_ids = [(x * inner + other, y) for x, y in friends]
    friends = [x * diags + y for x, y in friends]
    deep, core = lax.div(other, 2), lax.rem(other, 2)
    cousin_ids = [(outer * inner + lax.rem(deep + dz, inner // 2) * 2 + lax.rem(core + dc, 2), diag)
                  for dz, dc in far_first(inner // 2, 2)]
    near = neighbours()
    barrier = pltpu.get_barrier_semaphore()
    for device in near + friend_ids + cousin_ids:
        pl.semaphore_signal(barrier, inc=1, device_id=device, device_id_type=MESH)

    for copy in g_loads:
        copy.start()
    for copy in small:
        copy.wait()
    par = [counts[0] * (ROWS // 4)] + [reach[n] for n in range(4)] + [dilation[0], dilation[1]]
    par += [tile, diag, tiles - 1, diags - 1]
    place_weights(conv, mix, forward, backward, mix_t)
    keep = jnp.where(kept_cells(par), 1.0, 0.0).astype(BF)

    def put_field(k, value):
        field[EDGE + k] = value

    def put_masked(k, value):
        masked[k] = value

    turn_field(x_loads, lambda c: jnp.maximum(x_ref[c], jnp.zeros((), BF)) * keep, held, put_field)
    pl.semaphore_wait(barrier, len(near) + len(friend_ids) + len(cousin_ids))
    halo1 = halo_copies(near, field, first1, last1, left1, right1, top1, bot1, send1, recv1)
    pack_edges(par, field, first1, last1)
    for copy in halo1[2:] + halo1[:2]:
        copy.start()
    turn_field(g_loads, lambda c: g_ref[c] * keep, held, put_masked)
    inside = range(1, GROUPS + 1)
    for copy in halo1[2:4]:
        copy.wait_recv()
    shift_rows(par, inside, field, top1, bot1, moved)
    halo2 = halo_copies(near, grad_pre, first2, last2, left2, right2, top2, bot2, send2, recv2)
    ends = EDGE // STEP
    middle = COLS // STEP - 2 * ends
    acc_mix[...] = jnp.zeros_like(acc_mix)
    products(par, (middle + 2, 7, lambda at: at * STEP + DMAX), field, moved, forward, prod)
    activate(par, (middle, lambda at: at + ends), prod, masked, mix_t, grad_pre, acc_mix)
    for copy in halo1[:2] + halo1[4:]:
        copy.wait_recv()
    set_edges(par, left1, right1, field)
    shift_rows(par, [0, GROUPS + 1], field, top1, bot1, moved)
    products(par, (4, 4, lambda at: at * STEP - DMAX + (at // 2) * (middle + 2) * STEP), field, moved, forward, prod)
    activate(par, (2 * ends, lambda at: at + (at // ends) * middle), prod, masked, mix_t, grad_pre, acc_mix)
    halo2[0].start()
    halo2[1].start()
    pack_edges(par, grad_pre, first2, last2)
    for copy in halo2[2:]:
        copy.start()
    for e in range(EDGE):
        grad_pre[e] = jnp.zeros((CH, ROWS), BF)
        grad_pre[EDGE + COLS + e] = jnp.zeros((CH, ROWS), BF)
    kernel_grads(par, field, moved, grad_pre, acc)
    share_out(acc, acc_mix, part)
    sum1 = [remote(part.at[to], parts_in.at[rank], send3, recv3, friend_ids[n]) for n, to in enumerate(friends)]
    sum2 = [remote(far.at[other], far.at[other], send4, recv4, to) for to in cousin_ids]
    sum3 = [remote(done.at[rank], done.at[rank], send5, recv5, to) for to in friend_ids]
    all1, all2, all3 = [
        remote(slots.at[pl.ds(0, slots.shape[0] - 1)], slots.at[pl.ds(0, slots.shape[0] - 1)], send, recv, near[0])
        for slots, send, recv in ((parts_in, send3, recv3), (far, send4, recv4), (done, send5, recv5))]
    for copy in sum1:
        copy.start()
    parts_in[rank] = part[rank]

    for copy in halo2:
        copy.wait_recv()
    set_edges(par, left2, right2, grad_pre)
    shift_rows(par, range(GROUPS + 2), grad_pre, top2, bot2, moved)
    all1.wait_recv()
    far[other] = jnp.sum(parts_in[...], axis=0)
    for copy in sum2:
        copy.start()
    early = (COLS // STEP + 2) * 2 // 3
    products(par, (early, 6, lambda at: at * STEP - DMAX), grad_pre, moved, backward, prod)
    all2.wait_recv()
    done[rank] = jnp.sum(far[...], axis=0)
    for copy in sum3:
        copy.start()
    products(par, (early // 2, 6, lambda at: (at + early) * STEP - DMAX), grad_pre, moved, backward, prod)
    lay_out(par, prod, spread)
    finish(par, x_ref, g_ref, spread, out_ref)
    all3.wait_recv()
    unpack(scale, done, conv_ref, mix_ref)
    for copy in halo1 + halo2 + [all1, all2, all3]:
        copy.wait_send()


def move_out(field, conv, mix, field_out, conv_out, mix_out, sems):
    size = CH // MOVES
    pieces = [(field.at[pl.ds(n * size, size)], field_out.at[pl.ds(n * size, size)]) for n in range(MOVES)]
    copies = [pltpu.make_async_copy(src, dst, sems.at[n])
              for n, (src, dst) in enumerate([(conv, conv_out), (mix, mix_out)] + pieces)]
    for copy in copies:
        copy.start()
    for copy in copies:
        copy.wait()


def specs(space, count):
    return [pl.BlockSpec(memory_space=space)] * count


def body(inputs, cotangent, conv_weight, mix_weight, counts, band_reach, dilation):
    shape = jax.ShapeDtypeStruct
    tiles, diags = lax.axis_size("tiles"), lax.axis_size("diag")
    inner = 16 if tiles == 64 else 2
    shares = (tiles // inner) * diags
    dma = lambda n: pltpu.SemaphoreType.DMA((n,))
    whole = pltpu.VMEM((CH, ROWS, COLS), BF)
    field = pltpu.VMEM((COLS, CH, ROWS), BF)
    pack = pltpu.VMEM((GROUPS, CH, ROWS), BF)
    wide = pltpu.VMEM((COLS + 2 * EDGE, CH, ROWS), BF)
    side = pltpu.VMEM((EDGE, CH, ROWS), BF)
    ends = pltpu.VMEM((GROUPS + 2, CH, ROWS), BF)
    slots = lambda n: pltpu.VMEM((n, SUM_ROWS // shares, ROWS), F32)
    halo = [pack, pack, side, side, ends, ends]
    cells = TPD * tiles * (ROWS // 4) * COLS * diags
    results = pl.pallas_call(
        functools.partial(everything, inner, 1.0 / math.sqrt(cells)),
        out_shape=[pltpu.VMEM((CH, ROWS, COLS), BF), pltpu.VMEM((TAPS, CH, CH), F32), pltpu.VMEM((CH, CH), F32)],
        in_specs=specs(pltpu.HBM, 7),
        out_specs=specs(pltpu.VMEM, 3),
        scratch_shapes=[
            pltpu.SMEM(counts.shape, jnp.int32), pltpu.SMEM(band_reach.shape, jnp.int32), pltpu.SMEM(dilation.shape, jnp.int32),
            pltpu.VMEM(conv_weight.shape, BF), pltpu.VMEM(mix_weight.shape, BF),
            whole, whole, wide, field, wide,
            pltpu.VMEM((COLS + 2 * DMAX, 3 * CH, ROWS), F32),
            pltpu.VMEM((2, COLS + 2 * EDGE, CH, ROWS), BF),
            pltpu.VMEM(((COLS + 1) * TURN, ROWS), F32),
            pltpu.VMEM(((CH + 1) * BACK, ROWS), F32),
            pltpu.VMEM((3 * CH, 3 * CH), F32),
            pltpu.VMEM((CH, CH), F32),
            pltpu.VMEM((3 * CH, 3 * CH), BF),
            pltpu.VMEM((3 * CH, 3 * CH), BF),
            pltpu.VMEM((CH, CH), BF),
            *halo, *halo,
            slots(shares), slots(shares), slots(inner), slots(shares),
            dma(2 * LOADS + 5), dma(8), dma(8), dma(8), dma(8),
            *[pltpu.SemaphoreType.DMA] * 6,
        ],
        cost_estimate=pl.CostEstimate(flops=6 * CH * CH * TAPS * ROWS * COLS, bytes_accessed=3 * 2 * CH * ROWS * COLS,
                                      transcendentals=0),
        compiler_params=pltpu.CompilerParams(collective_id=0, has_side_effects=True, vmem_limit_bytes=VMEM_LIMIT),
    )(counts, band_reach, dilation, inputs, cotangent, conv_weight, mix_weight)
    return pl.pallas_call(
        move_out,
        out_shape=[shape(r.shape, r.dtype) for r in results],
        in_specs=specs(pltpu.VMEM, 3),
        out_specs=specs(pltpu.HBM, 3),
        scratch_shapes=[dma(MOVES + 2)],
        compiler_params=pltpu.CompilerParams(vmem_limit_bytes=8 * 1024 * 1024),
    )(*results)


def solution(mesh):
    in_specs = (
        P(None, "tiles", "diag"),
        P(None, "tiles", "diag"),
        P(),
        P(),
        P("tiles"),
        P("tiles"),
        P(),
    )
    out_specs = (P(None, "tiles", "diag"), P(), P())
    return jax.shard_map(body, mesh=mesh, in_specs=in_specs, out_specs=out_specs, check_vma=False)
```

```python
import functools
import math

import jax
import jax.numpy as jnp
from jax import lax
from jax.experimental import pallas as pl
from jax.experimental.pallas import tpu as pltpu
from jax.sharding import PartitionSpec as P

MESH = pl.DeviceIdType.MESH
TPD = 2
DMAX = 8
CH = 48
ROWS = 128
COLS = 128
EDGE = 2 * DMAX
GROUPS = COLS // EDGE
STEP = 8
TAPS = 9
SUM_ROWS = 192
VMEM_LIMIT = 56 * 1024 * 1024
BF = jnp.bfloat16
F32 = jnp.float32
LIVE, REACH, DIL, TILE, DIAG, LAST_TILE, LAST_DIAG = 0, 1, 5, 7, 8, 9, 10
TURN = 56
BACK = 136
LOADS = 3
MOVES = 4


def iota(shape, dim):
    return lax.broadcasted_iota(jnp.int32, shape, dim)


def reach_of(par, ids):
    reach = jnp.where(ids < 64, jnp.where(ids < 32, par[REACH], par[REACH + 1]),
                      jnp.where(ids < 96, par[REACH + 2], par[REACH + 3]))
    return jnp.where(ids < par[LIVE], reach, 0)


def pack_edges(par, field, first, last):
    lane = iota((1, 2 * ROWS), 1)
    near = lane % DMAX
    want = jnp.where(lane < ROWS, near, par[LIVE] - DMAX + near)
    place = jnp.where(lane < ROWS, (lane // DMAX + EDGE // 2) % EDGE, (lane - ROWS) // DMAX)
    hit = jnp.where(iota((ROWS, 2 * ROWS), 0) == want, 1.0, 0.0)
    weight = jnp.concatenate([jnp.where(place == kk, hit, 0.0).astype(BF) for kk in range(EDGE)], axis=0)
    lhs = jnp.concatenate(
        [jnp.concatenate([field[(g + 1) * EDGE + kk] for g in range(GROUPS)], axis=0) for kk in range(EDGE)], axis=1)
    out = jnp.dot(lhs, weight, preferred_element_type=F32).astype(BF)
    for g in range(GROUPS):
        first[g] = out[g * CH:(g + 1) * CH, :ROWS]
        last[g] = out[g * CH:(g + 1) * CH, ROWS:]


def set_edges(par, left, right, field):
    for e in range(EDGE):
        low, high = left[e], right[e]
        field[e] = jnp.where(par[DIAG] > 0, low, jnp.zeros_like(low))
        field[EDGE + COLS + e] = jnp.where(par[DIAG] < par[LAST_DIAG], high, jnp.zeros_like(high))


def shift_rows(par, groups, field, top, bot, moved):
    half = ROWS // 2
    lane = iota((1, 2 * ROWS), 1)
    move = jnp.where(lane < ROWS, -par[DIL], par[DIL])
    want = (lane % ROWS) + move
    rows = iota((ROWS, 2 * ROWS), 0)
    inner = jnp.where(rows == want, 1.0, 0.0).astype(BF)
    has_top = par[TILE] > 0
    has_bot = par[TILE] < par[LAST_TILE]
    top_want = jnp.where((want < 0) & has_top, want + DMAX, -1)
    low = want - par[LIVE]
    bot_want = jnp.where((low >= 0) & (low < DMAX) & has_bot, low, -1)
    wants = [jnp.where(rows < half, top_want, bot_want), jnp.where(rows < half, bot_want, top_want)]
    outers = [jnp.where(rows % DMAX == w, 1.0, 0.0) for w in wants]
    place = (rows % half) // DMAX
    has_left = par[DIAG] > 0
    has_right = par[DIAG] < par[LAST_DIAG]
    tops = jnp.concatenate([top[g] for g in groups], axis=0)
    bots = jnp.concatenate([bot[g] for g in groups], axis=0)
    upper = iota(tops.shape, 1) < half
    halos = [jnp.where(upper, tops, bots), jnp.where(upper, bots, tops)]

    for part in range(2):
        def column(at, carry):
            kk = at + part * (EDGE // 2)
            weight = jnp.concatenate([inner, jnp.where(place == at, outers[part], 0.0).astype(BF)], axis=0)
            tiles = [field[g * EDGE + kk] for g in groups]
            lhs = jnp.concatenate([jnp.concatenate(tiles, axis=0), halos[part]], axis=1)
            out = jnp.dot(lhs, weight, preferred_element_type=F32)
            for n, g in enumerate(groups):
                piece = out[n * CH:(n + 1) * CH]
                if g == 0:
                    piece = jnp.where(has_left, piece, 0.0)
                if g == GROUPS + 1:
                    piece = jnp.where(has_right, piece, 0.0)
                piece = piece.astype(BF)
                moved[0, g * EDGE + kk] = piece[:, :ROWS]
                moved[1, g * EDGE + kk] = piece[:, ROWS:]
            return carry

        lax.fori_loop(0, EDGE // 2, column, 0, unroll=EDGE // 2)


def stacked(par, field, moved, k):
    step = par[DIL]
    return jnp.concatenate([moved[0, EDGE + k + step], field[EDGE + k], moved[1, EDGE + k - step]], axis=0)


def pair(refs):
    return jnp.concatenate(refs, axis=1)


def eye():
    return jnp.where(iota((ROWS, ROWS), 0) == iota((ROWS, ROWS), 1), 1.0, 0.0).astype(BF)


def turn(one, value):
    return lax.dot_general(one, value, (((1,), (1,)), ((), ())), preferred_element_type=F32)


def turn_field(loads, value, held, put):
    one = eye()
    size = CH // len(loads)

    def channels(step, carry):
        c = step * 4
        out = turn(one, jnp.concatenate([value(c + n) for n in range(4)], axis=0))
        for n in range(4):
            held[pl.ds(c + n, COLS, stride=TURN), :] = out[:, n * ROWS:(n + 1) * ROWS]
        return carry

    for n, load in enumerate(loads):
        load.wait()
        lax.fori_loop(n * size // 4, (n + 1) * size // 4, channels, 0, unroll=size // 4)

    def column(k, carry):
        put(k, held[pl.ds(pl.multiple_of(k * TURN, 8), CH), :].astype(BF))
        return carry

    lax.fori_loop(0, COLS, column, 0, unroll=16)


def kept_cells(par):
    shape = (ROWS, COLS)
    return iota(shape, 1) + par[DIAG] * COLS < reach_of(par, iota(shape, 0))


def products(par, blocks, field, moved, weight, prod):
    count, unroll, number = blocks

    def block(at, carry):
        for j in range(0, STEP, 2):
            k = number(at) + j
            rhs = pair([stacked(par, field, moved, k), stacked(par, field, moved, k + 1)])
            out = jnp.dot(weight[...], rhs, preferred_element_type=F32)
            for n in range(2):
                prod[DMAX + k + n] = out[:, n * ROWS:(n + 1) * ROWS]
        return carry

    lax.fori_loop(0, count, block, 0, unroll=unroll)


def gathered(par, prod, k):
    step = par[DIL + 1]
    return prod[DMAX + k - step, :CH] + prod[DMAX + k, CH:2 * CH] + prod[DMAX + k + step, 2 * CH:]


def activate(par, blocks, prod, masked, mix_t, grad_pre, acc_mix):
    count, number = blocks

    def block(at, carry):
        ks = [number(at) * STEP + j for j in range(STEP)]
        upstream = pair([masked[k] for k in ks])
        back = jnp.dot(mix_t[...], upstream, preferred_element_type=F32)
        pre = pair([gathered(par, prod, k) for k in ks])
        grad = jnp.where(pre > 0, back, 0.0).astype(BF)
        for j, k in enumerate(ks):
            grad_pre[EDGE + k] = grad[:, j * ROWS:(j + 1) * ROWS]
        acc_mix[...] += lax.dot_general(upstream, jnp.maximum(pre, 0.0).astype(BF), (((1,), (1,)), ((), ())),
                                        preferred_element_type=F32)
        return carry

    lax.fori_loop(0, count, block, 0, unroll=min(count, 6))


def kernel_grads(par, field, moved, grad_pre, acc):
    acc[...] = jnp.zeros_like(acc)
    step = par[DIL + 1]

    def block(blk, carry):
        ks = [blk * STEP - DMAX + j for j in range(STEP)]
        rhs = pair([stacked(par, field, moved, k) for k in ks])
        lhs = jnp.concatenate([pair([grad_pre[EDGE + k - move] for k in ks]) for move in (-step, 0, step)], axis=0)
        acc[...] += lax.dot_general(lhs, rhs, (((1,), (1,)), ((), ())), preferred_element_type=F32)
        return carry

    lax.fori_loop(0, (COLS + 2 * DMAX) // STEP, block, 0, unroll=9)


def share_out(acc, acc_mix, part):
    main, side = acc[:, :ROWS], acc[:, ROWS:3 * CH]
    tail = [side[n * CH:(n + 1) * CH] for n in range(3)] + [acc_mix[...], jnp.zeros((CH, 2 * EDGE), F32)]
    rows = jnp.concatenate([main, jnp.concatenate(tail, axis=1)], axis=0)
    size = part.shape[1]
    for n in range(part.shape[0]):
        part[n] = rows[n * size:(n + 1) * size]


def place_weights(conv, mix, forward, backward, mix_t):
    shape = (CH, 3 * CH)
    gap = iota(shape, 1) - iota(shape, 0)
    puts = [jnp.where(gap == a * CH, 1.0, 0.0).astype(BF) for a in range(3)]
    turned = (((0,), (0,)), ((), ()))
    for b in range(3):
        taps = jnp.zeros(shape, F32)
        back = jnp.zeros(shape, F32)
        for a in range(3):
            taps += jnp.dot(conv[3 * a + b], puts[a], preferred_element_type=F32)
            back += lax.dot_general(conv[3 * (2 - a) + 2 - b], puts[a], turned, preferred_element_type=F32)
        forward[b * CH:(b + 1) * CH, :] = taps.astype(BF)
        backward[b * CH:(b + 1) * CH, :] = back.astype(BF)
    mix_t[...] = lax.dot_general(mix[...], puts[0], turned, preferred_element_type=F32)[:, :CH].astype(BF)


def lay_out(par, prod, spread):
    def block(blk, carry):
        for j in range(STEP):
            k = blk * STEP + j
            spread[pl.ds(k, CH, stride=BACK), :] = gathered(par, prod, k)
        return carry

    lax.fori_loop(0, COLS // STEP, block, 0, unroll=4)


def finish(par, x_ref, g_ref, spread, out_ref):
    keep = jnp.where(kept_cells(par), 1.0, 0.0).astype(BF)
    live = jnp.where(iota((ROWS, COLS), 0) < par[LIVE], 1.0, 0.0).astype(BF)
    one = eye()
    zero = jnp.zeros((ROWS, COLS), BF)

    def channels(step, carry):
        c = step * 4
        parts = [spread[pl.ds(pl.multiple_of((c + n) * BACK, 8), COLS), :].astype(BF) for n in range(4)]
        out = turn(one, jnp.concatenate(parts, axis=0)).astype(BF)
        for n in range(4):
            part = jnp.where(x_ref[c + n] > zero, out[:, n * ROWS:(n + 1) * ROWS], zero)
            out_ref[c + n] = (g_ref[c + n] + part * keep) * live
        return carry

    lax.fori_loop(0, CH // 4, channels, 0, unroll=6)


def remote(src, dst, send, recv, device):
    return pltpu.make_async_remote_copy(src_ref=src, dst_ref=dst, send_sem=send, recv_sem=recv,
                                        device_id=device, device_id_type=MESH)


def neighbours():
    tile, diag = lax.axis_index("tiles"), lax.axis_index("diag")
    tiles, diags = lax.axis_size("tiles"), lax.axis_size("diag")
    up, down = lax.rem(tile + tiles - 1, tiles), lax.rem(tile + 1, tiles)
    lo, hi = lax.rem(diag + diags - 1, diags), lax.rem(diag + 1, diags)
    return [(tile, lo), (tile, hi), (up, diag), (down, diag), (up, lo), (up, hi), (down, lo), (down, hi)]


def far_first(first, second):
    moves = [(m, n) for m in range(first) for n in range(second) if m or n]
    return sorted(moves, key=lambda move: -min(move[0], first - move[0]) - min(move[1], second - move[1]))


def halo_copies(near, field, first, last, left, right, top, bot, send, recv):
    inner = pl.ds(1, GROUPS)
    plan = [
        (field.at[pl.ds(EDGE, EDGE)], right),
        (field.at[pl.ds(COLS, EDGE)], left),
        (first, bot.at[inner]),
        (last, top.at[inner]),
        (first.at[0], bot.at[GROUPS + 1]),
        (first.at[GROUPS - 1], bot.at[0]),
        (last.at[0], top.at[GROUPS + 1]),
        (last.at[GROUPS - 1], top.at[0]),
    ]
    return [remote(src, dst, send.at[n], recv.at[n], near[n]) for n, (src, dst) in enumerate(plan)]


def unpack(scale, done, conv_ref, mix_ref):
    rows = jnp.concatenate([done[n] for n in range(done.shape[0])], axis=0) * scale
    tail = rows[3 * CH:]
    for b in range(3):
        full = jnp.concatenate([rows[b * CH:(b + 1) * CH], tail[:, b * EDGE:(b + 1) * EDGE]], axis=1)
        for a in range(3):
            conv_ref[3 * a + b] = full[:, a * CH:(a + 1) * CH]
    mix_ref[...] = tail[:, 3 * EDGE:3 * EDGE + CH]


def everything(inner, scale, counts_in, reach_in, dilation_in, x_hbm, g_hbm, conv_in, mix_in, out_ref, conv_ref, mix_ref,
               counts, reach, dilation, conv, mix,
               x_ref, g_ref, field, masked, grad_pre, prod, moved, held, spread, acc, acc_mix, forward, backward, mix_t,
               first1, last1, left1, right1, top1, bot1, first2, last2, left2, right2, top2, bot2,
               part, parts_in, far, done, load, send1, recv1, send2, recv2, send3, recv3, send4, recv4, send5, recv5):
    tile, diag = lax.axis_index("tiles"), lax.axis_index("diag")
    tiles, diags = lax.axis_size("tiles"), lax.axis_size("diag")
    pairs = [(counts_in, counts), (reach_in, reach), (dilation_in, dilation), (conv_in, conv), (mix_in, mix)]
    small = [pltpu.make_async_copy(src, dst, load.at[2 * LOADS + n]) for n, (src, dst) in enumerate(pairs)]
    parts = [pl.ds(n * (CH // LOADS), CH // LOADS) for n in range(LOADS)]
    x_loads = [pltpu.make_async_copy(x_hbm.at[at], x_ref.at[at], load.at[n]) for n, at in enumerate(parts)]
    g_loads = [pltpu.make_async_copy(g_hbm.at[at], g_ref.at[at], load.at[LOADS + n]) for n, at in enumerate(parts)]
    for copy in small + x_loads:
        copy.start()

    shares = (tiles // inner) * diags
    outer, other = lax.div(tile, inner), lax.rem(tile, inner)
    rank = outer * diags + diag
    friends = [(lax.rem(outer + dx, tiles // inner), lax.rem(diag + dy, diags)) for dx, dy in far_first(tiles // inner, diags)]
    friend_ids = [(x * inner + other, y) for x, y in friends]
    friends = [x * diags + y for x, y in friends]
    deep, core = lax.div(other, 2), lax.rem(other, 2)
    cousin_ids = [(outer * inner + lax.rem(deep + dz, inner // 2) * 2 + lax.rem(core + dc, 2), diag)
                  for dz, dc in far_first(inner // 2, 2)]
    near = neighbours()
    barrier = pltpu.get_barrier_semaphore()
    for device in near + friend_ids + cousin_ids:
        pl.semaphore_signal(barrier, inc=1, device_id=device, device_id_type=MESH)

    for copy in g_loads:
        copy.start()
    for copy in small:
        copy.wait()
    par = [counts[0] * (ROWS // 4)] + [reach[n] for n in range(4)] + [dilation[0], dilation[1]]
    par += [tile, diag, tiles - 1, diags - 1]
    place_weights(conv, mix, forward, backward, mix_t)
    keep = jnp.where(kept_cells(par), 1.0, 0.0).astype(BF)

    def put_field(k, value):
        field[EDGE + k] = value

    def put_masked(k, value):
        masked[k] = value

    turn_field(x_loads, lambda c: jnp.maximum(x_ref[c], jnp.zeros((), BF)) * keep, held, put_field)
    pl.semaphore_wait(barrier, len(near) + len(friend_ids) + len(cousin_ids))
    halo1 = halo_copies(near, field, first1, last1, left1, right1, top1, bot1, send1, recv1)
    pack_edges(par, field, first1, last1)
    for copy in halo1[2:] + halo1[:2]:
        copy.start()
    turn_field(g_loads, lambda c: g_ref[c] * keep, held, put_masked)
    inside = range(1, GROUPS + 1)
    for copy in halo1[2:4]:
        copy.wait_recv()
    shift_rows(par, inside, field, top1, bot1, moved)
    halo2 = halo_copies(near, grad_pre, first2, last2, left2, right2, top2, bot2, send2, recv2)
    ends = EDGE // STEP
    middle = COLS // STEP - 2 * ends
    acc_mix[...] = jnp.zeros_like(acc_mix)
    products(par, (middle + 2, middle + 2, lambda at: at * STEP + DMAX), field, moved, forward, prod)
    activate(par, (middle, lambda at: at + ends), prod, masked, mix_t, grad_pre, acc_mix)
    for copy in halo1[:2] + halo1[4:]:
        copy.wait_recv()
    set_edges(par, left1, right1, field)
    shift_rows(par, [0, GROUPS + 1], field, top1, bot1, moved)
    products(par, (4, 4, lambda at: at * STEP - DMAX + (at // 2) * (middle + 2) * STEP), field, moved, forward, prod)
    activate(par, (2 * ends, lambda at: at + (at // ends) * middle), prod, masked, mix_t, grad_pre, acc_mix)
    halo2[0].start()
    halo2[1].start()
    pack_edges(par, grad_pre, first2, last2)
    for copy in halo2[2:]:
        copy.start()
    for e in range(EDGE):
        grad_pre[e] = jnp.zeros((CH, ROWS), BF)
        grad_pre[EDGE + COLS + e] = jnp.zeros((CH, ROWS), BF)
    kernel_grads(par, field, moved, grad_pre, acc)
    share_out(acc, acc_mix, part)
    sum1 = [remote(part.at[to], parts_in.at[rank], send3, recv3, friend_ids[n]) for n, to in enumerate(friends)]
    sum2 = [remote(far.at[other], far.at[other], send4, recv4, to) for to in cousin_ids]
    sum3 = [remote(done.at[rank], done.at[rank], send5, recv5, to) for to in friend_ids]
    all1, all2, all3 = [
        remote(slots.at[pl.ds(0, slots.shape[0] - 1)], slots.at[pl.ds(0, slots.shape[0] - 1)], send, recv, near[0])
        for slots, send, recv in ((parts_in, send3, recv3), (far, send4, recv4), (done, send5, recv5))]
    for copy in sum1:
        copy.start()
    parts_in[rank] = part[rank]

    for copy in halo2:
        copy.wait_recv()
    set_edges(par, left2, right2, grad_pre)
    shift_rows(par, range(GROUPS + 2), grad_pre, top2, bot2, moved)
    all1.wait_recv()
    far[other] = jnp.sum(parts_in[...], axis=0)
    for copy in sum2:
        copy.start()
    early = (COLS // STEP + 2) * 2 // 3
    products(par, (early, early, lambda at: at * STEP - DMAX), grad_pre, moved, backward, prod)
    all2.wait_recv()
    done[rank] = jnp.sum(far[...], axis=0)
    for copy in sum3:
        copy.start()
    products(par, (early // 2, 6, lambda at: (at + early) * STEP - DMAX), grad_pre, moved, backward, prod)
    lay_out(par, prod, spread)
    finish(par, x_ref, g_ref, spread, out_ref)
    all3.wait_recv()
    unpack(scale, done, conv_ref, mix_ref)
    for copy in halo1 + halo2 + [all1, all2, all3]:
        copy.wait_send()


def move_out(field, conv, mix, field_out, conv_out, mix_out, sems):
    size = CH // MOVES
    pieces = [(field.at[pl.ds(n * size, size)], field_out.at[pl.ds(n * size, size)]) for n in range(MOVES)]
    copies = [pltpu.make_async_copy(src, dst, sems.at[n])
              for n, (src, dst) in enumerate([(conv, conv_out), (mix, mix_out)] + pieces)]
    for copy in copies:
        copy.start()
    for copy in copies:
        copy.wait()


def specs(space, count):
    return [pl.BlockSpec(memory_space=space)] * count


def body(inputs, cotangent, conv_weight, mix_weight, counts, band_reach, dilation):
    shape = jax.ShapeDtypeStruct
    tiles, diags = lax.axis_size("tiles"), lax.axis_size("diag")
    inner = 16 if tiles == 64 else 2
    shares = (tiles // inner) * diags
    dma = lambda n: pltpu.SemaphoreType.DMA((n,))
    whole = pltpu.VMEM((CH, ROWS, COLS), BF)
    field = pltpu.VMEM((COLS, CH, ROWS), BF)
    pack = pltpu.VMEM((GROUPS, CH, ROWS), BF)
    wide = pltpu.VMEM((COLS + 2 * EDGE, CH, ROWS), BF)
    side = pltpu.VMEM((EDGE, CH, ROWS), BF)
    ends = pltpu.VMEM((GROUPS + 2, CH, ROWS), BF)
    slots = lambda n: pltpu.VMEM((n, SUM_ROWS // shares, ROWS), F32)
    halo = [pack, pack, side, side, ends, ends]
    cells = TPD * tiles * (ROWS // 4) * COLS * diags
    results = pl.pallas_call(
        functools.partial(everything, inner, 1.0 / math.sqrt(cells)),
        out_shape=[pltpu.VMEM((CH, ROWS, COLS), BF), pltpu.VMEM((TAPS, CH, CH), F32), pltpu.VMEM((CH, CH), F32)],
        in_specs=specs(pltpu.HBM, 7),
        out_specs=specs(pltpu.VMEM, 3),
        scratch_shapes=[
            pltpu.SMEM(counts.shape, jnp.int32), pltpu.SMEM(band_reach.shape, jnp.int32), pltpu.SMEM(dilation.shape, jnp.int32),
            pltpu.VMEM(conv_weight.shape, BF), pltpu.VMEM(mix_weight.shape, BF),
            whole, whole, wide, field, wide,
            pltpu.VMEM((COLS + 2 * DMAX, 3 * CH, ROWS), F32),
            pltpu.VMEM((2, COLS + 2 * EDGE, CH, ROWS), BF),
            pltpu.VMEM(((COLS + 1) * TURN, ROWS), F32),
            pltpu.VMEM(((CH + 1) * BACK, ROWS), F32),
            pltpu.VMEM((3 * CH, 3 * CH), F32),
            pltpu.VMEM((CH, CH), F32),
            pltpu.VMEM((3 * CH, 3 * CH), BF),
            pltpu.VMEM((3 * CH, 3 * CH), BF),
            pltpu.VMEM((CH, CH), BF),
            *halo, *halo,
            slots(shares), slots(shares), slots(inner), slots(shares),
            dma(2 * LOADS + 5), dma(8), dma(8), dma(8), dma(8),
            *[pltpu.SemaphoreType.DMA] * 6,
        ],
        cost_estimate=pl.CostEstimate(flops=6 * CH * CH * TAPS * ROWS * COLS, bytes_accessed=3 * 2 * CH * ROWS * COLS,
                                      transcendentals=0),
        compiler_params=pltpu.CompilerParams(collective_id=0, has_side_effects=True, vmem_limit_bytes=VMEM_LIMIT),
    )(counts, band_reach, dilation, inputs, cotangent, conv_weight, mix_weight)
    return pl.pallas_call(
        move_out,
        out_shape=[shape(r.shape, r.dtype) for r in results],
        in_specs=specs(pltpu.VMEM, 3),
        out_specs=specs(pltpu.HBM, 3),
        scratch_shapes=[dma(MOVES + 2)],
        compiler_params=pltpu.CompilerParams(vmem_limit_bytes=8 * 1024 * 1024),
    )(*results)


def solution(mesh):
    in_specs = (
        P(None, "tiles", "diag"),
        P(None, "tiles", "diag"),
        P(),
        P(),
        P("tiles"),
        P("tiles"),
        P(),
    )
    out_specs = (P(None, "tiles", "diag"), P(), P())
    return jax.shard_map(body, mesh=mesh, in_specs=in_specs, out_specs=out_specs, check_vma=False)
```

```python
import functools
import math

import jax
import jax.numpy as jnp
from jax import lax
from jax.experimental import pallas as pl
from jax.experimental.pallas import tpu as pltpu
from jax.sharding import PartitionSpec as P

MESH = pl.DeviceIdType.MESH
TPD = 2
DMAX = 8
CH = 48
ROWS = 128
COLS = 128
EDGE = 2 * DMAX
GROUPS = COLS // EDGE
STEP = 8
TAPS = 9
SUM_ROWS = 192
VMEM_LIMIT = 56 * 1024 * 1024
BF = jnp.bfloat16
F32 = jnp.float32
LIVE, REACH, DIL, TILE, DIAG, LAST_TILE, LAST_DIAG = 0, 1, 5, 7, 8, 9, 10
TURN = 56
BACK = 136
LOADS = 3
MOVES = 4


def iota(shape, dim):
    return lax.broadcasted_iota(jnp.int32, shape, dim)


def reach_of(par, ids):
    reach = jnp.where(ids < 64, jnp.where(ids < 32, par[REACH], par[REACH + 1]),
                      jnp.where(ids < 96, par[REACH + 2], par[REACH + 3]))
    return jnp.where(ids < par[LIVE], reach, 0)


def pack_edges(par, field, first, last):
    lane = iota((1, 2 * ROWS), 1)
    near = lane % DMAX
    want = jnp.where(lane < ROWS, near, par[LIVE] - DMAX + near)
    place = jnp.where(lane < ROWS, (lane // DMAX + EDGE // 2) % EDGE, (lane - ROWS) // DMAX)
    hit = jnp.where(iota((ROWS, 2 * ROWS), 0) == want, 1.0, 0.0)
    weight = jnp.concatenate([jnp.where(place == kk, hit, 0.0).astype(BF) for kk in range(EDGE)], axis=0)
    lhs = jnp.concatenate(
        [jnp.concatenate([field[(g + 1) * EDGE + kk] for g in range(GROUPS)], axis=0) for kk in range(EDGE)], axis=1)
    out = jnp.dot(lhs, weight, preferred_element_type=F32).astype(BF)
    for g in range(GROUPS):
        first[g] = out[g * CH:(g + 1) * CH, :ROWS]
        last[g] = out[g * CH:(g + 1) * CH, ROWS:]


def set_edges(par, left, right, field):
    for e in range(EDGE):
        low, high = left[e], right[e]
        field[e] = jnp.where(par[DIAG] > 0, low, jnp.zeros_like(low))
        field[EDGE + COLS + e] = jnp.where(par[DIAG] < par[LAST_DIAG], high, jnp.zeros_like(high))


def shift_rows(par, groups, field, top, bot, moved):
    half = ROWS // 2
    lane = iota((1, 2 * ROWS), 1)
    move = jnp.where(lane < ROWS, -par[DIL], par[DIL])
    want = (lane % ROWS) + move
    rows = iota((ROWS, 2 * ROWS), 0)
    inner = jnp.where(rows == want, 1.0, 0.0).astype(BF)
    has_top = par[TILE] > 0
    has_bot = par[TILE] < par[LAST_TILE]
    top_want = jnp.where((want < 0) & has_top, want + DMAX, -1)
    low = want - par[LIVE]
    bot_want = jnp.where((low >= 0) & (low < DMAX) & has_bot, low, -1)
    wants = [jnp.where(rows < half, top_want, bot_want), jnp.where(rows < half, bot_want, top_want)]
    outers = [jnp.where(rows % DMAX == w, 1.0, 0.0) for w in wants]
    place = (rows % half) // DMAX
    has_left = par[DIAG] > 0
    has_right = par[DIAG] < par[LAST_DIAG]
    tops = jnp.concatenate([top[g] for g in groups], axis=0)
    bots = jnp.concatenate([bot[g] for g in groups], axis=0)
    upper = iota(tops.shape, 1) < half
    halos = [jnp.where(upper, tops, bots), jnp.where(upper, bots, tops)]

    for part in range(2):
        def column(at, carry):
            kk = at + part * (EDGE // 2)
            weight = jnp.concatenate([inner, jnp.where(place == at, outers[part], 0.0).astype(BF)], axis=0)
            tiles = [field[g * EDGE + kk] for g in groups]
            lhs = jnp.concatenate([jnp.concatenate(tiles, axis=0), halos[part]], axis=1)
            out = jnp.dot(lhs, weight, preferred_element_type=F32)
            for n, g in enumerate(groups):
                piece = out[n * CH:(n + 1) * CH]
                if g == 0:
                    piece = jnp.where(has_left, piece, 0.0)
                if g == GROUPS + 1:
                    piece = jnp.where(has_right, piece, 0.0)
                piece = piece.astype(BF)
                moved[0, g * EDGE + kk] = piece[:, :ROWS]
                moved[1, g * EDGE + kk] = piece[:, ROWS:]
            return carry

        lax.fori_loop(0, EDGE // 2, column, 0, unroll=EDGE // 2)


def stacked(par, field, moved, k):
    step = par[DIL]
    return jnp.concatenate([moved[0, EDGE + k + step], field[EDGE + k], moved[1, EDGE + k - step]], axis=0)


def pair(refs):
    return jnp.concatenate(refs, axis=1)


def eye():
    return jnp.where(iota((ROWS, ROWS), 0) == iota((ROWS, ROWS), 1), 1.0, 0.0).astype(BF)


def turn(one, value):
    return lax.dot_general(one, value, (((1,), (1,)), ((), ())), preferred_element_type=F32)


def turn_field(loads, value, held, put):
    one = eye()
    size = CH // len(loads)

    def channels(step, carry):
        c = step * 4
        out = turn(one, jnp.concatenate([value(c + n) for n in range(4)], axis=0))
        for n in range(4):
            held[pl.ds(c + n, COLS, stride=TURN), :] = out[:, n * ROWS:(n + 1) * ROWS]
        return carry

    for n, load in enumerate(loads):
        load.wait()
        lax.fori_loop(n * size // 4, (n + 1) * size // 4, channels, 0, unroll=size // 4)

    def column(k, carry):
        put(k, held[pl.ds(pl.multiple_of(k * TURN, 8), CH), :].astype(BF))
        return carry

    lax.fori_loop(0, COLS, column, 0, unroll=16)


def kept_cells(par):
    shape = (ROWS, COLS)
    return iota(shape, 1) + par[DIAG] * COLS < reach_of(par, iota(shape, 0))


def products(par, blocks, field, moved, weight, prod):
    count, unroll, number = blocks

    def block(at, carry):
        for j in range(0, STEP, 2):
            k = number(at) + j
            rhs = pair([stacked(par, field, moved, k), stacked(par, field, moved, k + 1)])
            out = jnp.dot(weight[...], rhs, preferred_element_type=F32)
            for n in range(2):
                prod[DMAX + k + n] = out[:, n * ROWS:(n + 1) * ROWS]
        return carry

    lax.fori_loop(0, count, block, 0, unroll=unroll)


def gathered(par, prod, k):
    step = par[DIL + 1]
    return prod[DMAX + k - step, :CH] + prod[DMAX + k, CH:2 * CH] + prod[DMAX + k + step, 2 * CH:]


def activate(par, blocks, prod, masked, mix_t, grad_pre, acc_mix):
    count, number = blocks

    def block(at, carry):
        ks = [number(at) * STEP + j for j in range(STEP)]
        upstream = pair([masked[k] for k in ks])
        back = jnp.dot(mix_t[...], upstream, preferred_element_type=F32)
        pre = pair([gathered(par, prod, k) for k in ks])
        grad = jnp.where(pre > 0, back, 0.0).astype(BF)
        for j, k in enumerate(ks):
            grad_pre[EDGE + k] = grad[:, j * ROWS:(j + 1) * ROWS]
        acc_mix[...] += lax.dot_general(upstream, jnp.maximum(pre, 0.0).astype(BF), (((1,), (1,)), ((), ())),
                                        preferred_element_type=F32)
        return carry

    lax.fori_loop(0, count, block, 0, unroll=count)


def kernel_grads(par, field, moved, grad_pre, acc):
    acc[...] = jnp.zeros_like(acc)
    step = par[DIL + 1]

    def block(blk, carry):
        ks = [blk * STEP - DMAX + j for j in range(STEP)]
        rhs = pair([stacked(par, field, moved, k) for k in ks])
        lhs = jnp.concatenate([pair([grad_pre[EDGE + k - move] for k in ks]) for move in (-step, 0, step)], axis=0)
        acc[...] += lax.dot_general(lhs, rhs, (((1,), (1,)), ((), ())), preferred_element_type=F32)
        return carry

    lax.fori_loop(0, (COLS + 2 * DMAX) // STEP, block, 0, unroll=18)


def share_out(acc, acc_mix, part):
    main, side = acc[:, :ROWS], acc[:, ROWS:3 * CH]
    tail = [side[n * CH:(n + 1) * CH] for n in range(3)] + [acc_mix[...], jnp.zeros((CH, 2 * EDGE), F32)]
    rows = jnp.concatenate([main, jnp.concatenate(tail, axis=1)], axis=0)
    size = part.shape[1]
    for n in range(part.shape[0]):
        part[n] = rows[n * size:(n + 1) * size]


def place_weights(conv, mix, forward, backward, mix_t):
    shape = (CH, 3 * CH)
    gap = iota(shape, 1) - iota(shape, 0)
    puts = [jnp.where(gap == a * CH, 1.0, 0.0).astype(BF) for a in range(3)]
    turned = (((0,), (0,)), ((), ()))
    for b in range(3):
        taps = jnp.zeros(shape, F32)
        back = jnp.zeros(shape, F32)
        for a in range(3):
            taps += jnp.dot(conv[3 * a + b], puts[a], preferred_element_type=F32)
            back += lax.dot_general(conv[3 * (2 - a) + 2 - b], puts[a], turned, preferred_element_type=F32)
        forward[b * CH:(b + 1) * CH, :] = taps.astype(BF)
        backward[b * CH:(b + 1) * CH, :] = back.astype(BF)
    mix_t[...] = lax.dot_general(mix[...], puts[0], turned, preferred_element_type=F32)[:, :CH].astype(BF)


def lay_out(par, prod, spread):
    def block(blk, carry):
        for j in range(STEP):
            k = blk * STEP + j
            spread[pl.ds(k, CH, stride=BACK), :] = gathered(par, prod, k)
        return carry

    lax.fori_loop(0, COLS // STEP, block, 0, unroll=4)


def finish(par, x_ref, g_ref, spread, out_ref):
    keep = jnp.where(kept_cells(par), 1.0, 0.0).astype(BF)
    live = jnp.where(iota((ROWS, COLS), 0) < par[LIVE], 1.0, 0.0).astype(BF)
    one = eye()
    zero = jnp.zeros((ROWS, COLS), BF)

    def channels(step, carry):
        c = step * 4
        parts = [spread[pl.ds(pl.multiple_of((c + n) * BACK, 8), COLS), :].astype(BF) for n in range(4)]
        out = turn(one, jnp.concatenate(parts, axis=0)).astype(BF)
        for n in range(4):
            part = jnp.where(x_ref[c + n] > zero, out[:, n * ROWS:(n + 1) * ROWS], zero)
            out_ref[c + n] = (g_ref[c + n] + part * keep) * live
        return carry

    lax.fori_loop(0, CH // 4, channels, 0, unroll=12)


def remote(src, dst, send, recv, device):
    return pltpu.make_async_remote_copy(src_ref=src, dst_ref=dst, send_sem=send, recv_sem=recv,
                                        device_id=device, device_id_type=MESH)


def neighbours():
    tile, diag = lax.axis_index("tiles"), lax.axis_index("diag")
    tiles, diags = lax.axis_size("tiles"), lax.axis_size("diag")
    up, down = lax.rem(tile + tiles - 1, tiles), lax.rem(tile + 1, tiles)
    lo, hi = lax.rem(diag + diags - 1, diags), lax.rem(diag + 1, diags)
    return [(tile, lo), (tile, hi), (up, diag), (down, diag), (up, lo), (up, hi), (down, lo), (down, hi)]


def far_first(first, second):
    moves = [(m, n) for m in range(first) for n in range(second) if m or n]
    return sorted(moves, key=lambda move: -min(move[0], first - move[0]) - min(move[1], second - move[1]))


def halo_copies(near, field, first, last, left, right, top, bot, send, recv):
    inner = pl.ds(1, GROUPS)
    plan = [
        (field.at[pl.ds(EDGE, EDGE)], right),
        (field.at[pl.ds(COLS, EDGE)], left),
        (first, bot.at[inner]),
        (last, top.at[inner]),
        (first.at[0], bot.at[GROUPS + 1]),
        (first.at[GROUPS - 1], bot.at[0]),
        (last.at[0], top.at[GROUPS + 1]),
        (last.at[GROUPS - 1], top.at[0]),
    ]
    return [remote(src, dst, send.at[n], recv.at[n], near[n]) for n, (src, dst) in enumerate(plan)]


def unpack(scale, done, conv_ref, mix_ref):
    rows = jnp.concatenate([done[n] for n in range(done.shape[0])], axis=0) * scale
    tail = rows[3 * CH:]
    for b in range(3):
        full = jnp.concatenate([rows[b * CH:(b + 1) * CH], tail[:, b * EDGE:(b + 1) * EDGE]], axis=1)
        for a in range(3):
            conv_ref[3 * a + b] = full[:, a * CH:(a + 1) * CH]
    mix_ref[...] = tail[:, 3 * EDGE:3 * EDGE + CH]


def everything(inner, scale, counts_in, reach_in, dilation_in, x_hbm, g_hbm, conv_in, mix_in, out_ref, conv_ref, mix_ref,
               counts, reach, dilation, conv, mix,
               x_ref, g_ref, field, masked, grad_pre, prod, moved, held, spread, acc, acc_mix, forward, backward, mix_t,
               first1, last1, left1, right1, top1, bot1, first2, last2, left2, right2, top2, bot2,
               part, parts_in, far, done, load, send1, recv1, send2, recv2, send3, recv3, send4, recv4, send5, recv5):
    tile, diag = lax.axis_index("tiles"), lax.axis_index("diag")
    tiles, diags = lax.axis_size("tiles"), lax.axis_size("diag")
    pairs = [(counts_in, counts), (reach_in, reach), (dilation_in, dilation), (conv_in, conv), (mix_in, mix)]
    small = [pltpu.make_async_copy(src, dst, load.at[2 * LOADS + n]) for n, (src, dst) in enumerate(pairs)]
    parts = [pl.ds(n * (CH // LOADS), CH // LOADS) for n in range(LOADS)]
    x_loads = [pltpu.make_async_copy(x_hbm.at[at], x_ref.at[at], load.at[n]) for n, at in enumerate(parts)]
    g_loads = [pltpu.make_async_copy(g_hbm.at[at], g_ref.at[at], load.at[LOADS + n]) for n, at in enumerate(parts)]
    for copy in small + x_loads:
        copy.start()

    shares = (tiles // inner) * diags
    outer, other = lax.div(tile, inner), lax.rem(tile, inner)
    rank = outer * diags + diag
    friends = [(lax.rem(outer + dx, tiles // inner), lax.rem(diag + dy, diags)) for dx, dy in far_first(tiles // inner, diags)]
    friend_ids = [(x * inner + other, y) for x, y in friends]
    friends = [x * diags + y for x, y in friends]
    deep, core = lax.div(other, 2), lax.rem(other, 2)
    cousin_ids = [(outer * inner + lax.rem(deep + dz, inner // 2) * 2 + lax.rem(core + dc, 2), diag)
                  for dz, dc in far_first(inner // 2, 2)]
    near = neighbours()
    barrier = pltpu.get_barrier_semaphore()
    for device in near + friend_ids + cousin_ids:
        pl.semaphore_signal(barrier, inc=1, device_id=device, device_id_type=MESH)

    for copy in g_loads:
        copy.start()
    for copy in small:
        copy.wait()
    par = [counts[0] * (ROWS // 4)] + [reach[n] for n in range(4)] + [dilation[0], dilation[1]]
    par += [tile, diag, tiles - 1, diags - 1]
    place_weights(conv, mix, forward, backward, mix_t)
    keep = jnp.where(kept_cells(par), 1.0, 0.0).astype(BF)

    def put_field(k, value):
        field[EDGE + k] = value

    def put_masked(k, value):
        masked[k] = value

    turn_field(x_loads, lambda c: jnp.maximum(x_ref[c], jnp.zeros((), BF)) * keep, held, put_field)
    pl.semaphore_wait(barrier, len(near) + len(friend_ids) + len(cousin_ids))
    halo1 = halo_copies(near, field, first1, last1, left1, right1, top1, bot1, send1, recv1)
    pack_edges(par, field, first1, last1)
    for copy in halo1[2:] + halo1[:2]:
        copy.start()
    turn_field(g_loads, lambda c: g_ref[c] * keep, held, put_masked)
    inside = range(1, GROUPS + 1)
    for copy in halo1[2:4]:
        copy.wait_recv()
    shift_rows(par, inside, field, top1, bot1, moved)
    halo2 = halo_copies(near, grad_pre, first2, last2, left2, right2, top2, bot2, send2, recv2)
    ends = EDGE // STEP
    middle = COLS // STEP - 2 * ends
    acc_mix[...] = jnp.zeros_like(acc_mix)
    products(par, (middle + 2, middle + 2, lambda at: at * STEP + DMAX), field, moved, forward, prod)
    activate(par, (middle, lambda at: at + ends), prod, masked, mix_t, grad_pre, acc_mix)
    for copy in halo1[:2] + halo1[4:]:
        copy.wait_recv()
    set_edges(par, left1, right1, field)
    shift_rows(par, [0, GROUPS + 1], field, top1, bot1, moved)
    products(par, (4, 4, lambda at: at * STEP - DMAX + (at // 2) * (middle + 2) * STEP), field, moved, forward, prod)
    activate(par, (2 * ends, lambda at: at + (at // ends) * middle), prod, masked, mix_t, grad_pre, acc_mix)
    halo2[0].start()
    halo2[1].start()
    pack_edges(par, grad_pre, first2, last2)
    for copy in halo2[2:]:
        copy.start()
    for e in range(EDGE):
        grad_pre[e] = jnp.zeros((CH, ROWS), BF)
        grad_pre[EDGE + COLS + e] = jnp.zeros((CH, ROWS), BF)
    kernel_grads(par, field, moved, grad_pre, acc)
    share_out(acc, acc_mix, part)
    sum1 = [remote(part.at[to], parts_in.at[rank], send3, recv3, friend_ids[n]) for n, to in enumerate(friends)]
    sum2 = [remote(far.at[other], far.at[other], send4, recv4, to) for to in cousin_ids]
    sum3 = [remote(done.at[rank], done.at[rank], send5, recv5, to) for to in friend_ids]
    all1, all2, all3 = [
        remote(slots.at[pl.ds(0, slots.shape[0] - 1)], slots.at[pl.ds(0, slots.shape[0] - 1)], send, recv, near[0])
        for slots, send, recv in ((parts_in, send3, recv3), (far, send4, recv4), (done, send5, recv5))]
    for copy in sum1:
        copy.start()
    parts_in[rank] = part[rank]

    for copy in halo2:
        copy.wait_recv()
    set_edges(par, left2, right2, grad_pre)
    shift_rows(par, range(GROUPS + 2), grad_pre, top2, bot2, moved)
    all1.wait_recv()
    far[other] = jnp.sum(parts_in[...], axis=0)
    for copy in sum2:
        copy.start()
    wide_blocks = COLS // STEP + 2
    early = wide_blocks * 5 // 6
    late = wide_blocks - early
    products(par, (early, early, lambda at: at * STEP - DMAX), grad_pre, moved, backward, prod)
    all2.wait_recv()
    done[rank] = jnp.sum(far[...], axis=0)
    for copy in sum3:
        copy.start()
    products(par, (late, late, lambda at: (at + early) * STEP - DMAX), grad_pre, moved, backward, prod)
    lay_out(par, prod, spread)
    finish(par, x_ref, g_ref, spread, out_ref)
    all3.wait_recv()
    unpack(scale, done, conv_ref, mix_ref)
    for copy in halo1 + halo2 + [all1, all2, all3]:
        copy.wait_send()


def move_out(field, conv, mix, field_out, conv_out, mix_out, sems):
    size = CH // MOVES
    pieces = [(field.at[pl.ds(n * size, size)], field_out.at[pl.ds(n * size, size)]) for n in range(MOVES)]
    copies = [pltpu.make_async_copy(src, dst, sems.at[n])
              for n, (src, dst) in enumerate([(conv, conv_out), (mix, mix_out)] + pieces)]
    for copy in copies:
        copy.start()
    for copy in copies:
        copy.wait()


def specs(space, count):
    return [pl.BlockSpec(memory_space=space)] * count


def body(inputs, cotangent, conv_weight, mix_weight, counts, band_reach, dilation):
    shape = jax.ShapeDtypeStruct
    tiles, diags = lax.axis_size("tiles"), lax.axis_size("diag")
    inner = 16 if tiles == 64 else 2
    shares = (tiles // inner) * diags
    dma = lambda n: pltpu.SemaphoreType.DMA((n,))
    whole = pltpu.VMEM((CH, ROWS, COLS), BF)
    field = pltpu.VMEM((COLS, CH, ROWS), BF)
    pack = pltpu.VMEM((GROUPS, CH, ROWS), BF)
    wide = pltpu.VMEM((COLS + 2 * EDGE, CH, ROWS), BF)
    side = pltpu.VMEM((EDGE, CH, ROWS), BF)
    ends = pltpu.VMEM((GROUPS + 2, CH, ROWS), BF)
    slots = lambda n: pltpu.VMEM((n, SUM_ROWS // shares, ROWS), F32)
    halo = [pack, pack, side, side, ends, ends]
    cells = TPD * tiles * (ROWS // 4) * COLS * diags
    results = pl.pallas_call(
        functools.partial(everything, inner, 1.0 / math.sqrt(cells)),
        out_shape=[pltpu.VMEM((CH, ROWS, COLS), BF), pltpu.VMEM((TAPS, CH, CH), F32), pltpu.VMEM((CH, CH), F32)],
        in_specs=specs(pltpu.HBM, 7),
        out_specs=specs(pltpu.VMEM, 3),
        scratch_shapes=[
            pltpu.SMEM(counts.shape, jnp.int32), pltpu.SMEM(band_reach.shape, jnp.int32), pltpu.SMEM(dilation.shape, jnp.int32),
            pltpu.VMEM(conv_weight.shape, BF), pltpu.VMEM(mix_weight.shape, BF),
            whole, whole, wide, field, wide,
            pltpu.VMEM((COLS + 2 * DMAX, 3 * CH, ROWS), F32),
            pltpu.VMEM((2, COLS + 2 * EDGE, CH, ROWS), BF),
            pltpu.VMEM(((COLS + 1) * TURN, ROWS), F32),
            pltpu.VMEM(((CH + 1) * BACK, ROWS), F32),
            pltpu.VMEM((3 * CH, 3 * CH), F32),
            pltpu.VMEM((CH, CH), F32),
            pltpu.VMEM((3 * CH, 3 * CH), BF),
            pltpu.VMEM((3 * CH, 3 * CH), BF),
            pltpu.VMEM((CH, CH), BF),
            *halo, *halo,
            slots(shares), slots(shares), slots(inner), slots(shares),
            dma(2 * LOADS + 5), dma(8), dma(8), dma(8), dma(8),
            *[pltpu.SemaphoreType.DMA] * 6,
        ],
        cost_estimate=pl.CostEstimate(flops=6 * CH * CH * TAPS * ROWS * COLS, bytes_accessed=3 * 2 * CH * ROWS * COLS,
                                      transcendentals=0),
        compiler_params=pltpu.CompilerParams(collective_id=0, has_side_effects=True, vmem_limit_bytes=VMEM_LIMIT),
    )(counts, band_reach, dilation, inputs, cotangent, conv_weight, mix_weight)
    return pl.pallas_call(
        move_out,
        out_shape=[shape(r.shape, r.dtype) for r in results],
        in_specs=specs(pltpu.VMEM, 3),
        out_specs=specs(pltpu.HBM, 3),
        scratch_shapes=[dma(MOVES + 2)],
        compiler_params=pltpu.CompilerParams(vmem_limit_bytes=8 * 1024 * 1024),
    )(*results)


def solution(mesh):
    in_specs = (
        P(None, "tiles", "diag"),
        P(None, "tiles", "diag"),
        P(),
        P(),
        P("tiles"),
        P("tiles"),
        P(),
    )
    out_specs = (P(None, "tiles", "diag"), P(), P())
    return jax.shard_map(body, mesh=mesh, in_specs=in_specs, out_specs=out_specs, check_vma=False)
```
